128 devices in a mesh: shard: 8 (over x, z_lo), replica: 16 (over y, z_hi, core).
Axes of the slice: x: 4, y: 4, z: 4 (z_hi: 2, z_lo: 2; z = z_hi * 2 + z_lo), core: 2. Of those that a mesh axis runs over, the one named last changes fastest.
Arguments:
- tokens: bfloat16 [16, 1024, 1024], P('replica', 'shard'), may hold values from -6 to 6
- seq_lengths: int32 [16, 2], P('replica'), may hold values from 1 to 585, 1024 in all within a row
- token_places: int32 [16, 1024], P('replica'), may hold values from 0 to 1023, each once within a row
- attention_gain: bfloat16 [1024], P('shard'), may hold values from 0.5 to 1.5
- query_weight: bfloat16 [1024, 1024], P('shard'), may hold values from -0.1875 to 0.1875
- key_weight: bfloat16 [1024, 512], P('shard'), may hold values from -0.1875 to 0.1875
- value_weight: bfloat16 [1024, 512], P('shard'), may hold values from -0.1875 to 0.1875
- query_gain: bfloat16 [64], P('shard'), may hold values from 0.796875 to 1.796875
- key_gain: bfloat16 [64], P('shard'), may hold values from 0.796875 to 1.796875
- out_weight: bfloat16 [1024, 1024], P('shard'), may hold values from -1.5 to 1.5
- feedforward_gain: bfloat16 [1024], P('shard'), may hold values from 0.5 to 1.5
- gate_weight: bfloat16 [1024, 4608], P('shard'), may hold values from -0.1875 to 0.1875
- up_weight: bfloat16 [1024, 4608], P('shard'), may hold values from -0.1875 to 0.1875
- down_weight: bfloat16 [4608, 1024], P('shard'), may hold values from -0.1875 to 0.1875
- cotangent: bfloat16 [16, 1024, 1024], P('replica', 'shard'), may hold values from -6 to 6
Outputs:
- layer_out: bfloat16 [16, 1024, 1024], P('replica', 'shard')
- input_grad: float32 [16, 1024, 1024], P('replica', 'shard')
- attention_gain_grad: float32 [1024], P('shard')
- query_weight_grad: float32 [1024, 1024], P('shard')
- key_weight_grad: float32 [1024, 512], P('shard')
- value_weight_grad: float32 [1024, 512], P('shard')
- query_gain_grad: float32 [64], P('shard')
- key_gain_grad: float32 [64], P('shard')
- out_weight_grad: float32 [1024, 1024], P('shard')
- feedforward_gain_grad: float32 [1024], P('shard')
- gate_weight_grad: float32 [1024, 4608], P('shard')
- up_weight_grad: float32 [1024, 4608], P('shard')
- down_weight_grad: float32 [4608, 1024], P('shard')
The draws below stay inside these ranges and needn't reach their ends.
Inputs may be any that keep to these rules, and one draw needn't show every extreme that they name: `seq_lengths`: each group's 2 lengths add up to 1024, and neither exceeds 585. `token_places`: each group's row holds every place of its pack once.
All inputs are finite; a program needn't handle non-finite values.
Results may differ from the reference program's by a relative error of at most 0.035.
Values may be sent and summed in bfloat16 or wider, within the bound.
No kernel may reach another device: no remote copies, remote signals or barrier semaphores. Data moves between devices by JAX's collectives and lax.ppermute only.
A program may use at most 192 MiB of HBM per device.

```python
import math
import jax
import jax.numpy as jnp
import numpy as np
from jax import lax

D = 1024
HEADS = 16
KV_HEADS = 8
HD = 64
FF = 4608
SEQS = 2
GROUP_TOK = 1024
LONGEST = 585
GROUPS = 16


def block_scale(rng, shape, split, smallest, high):
    gain = 1.0
    for dim, parts in split:
        heights = jax.random.uniform(jax.random.fold_in(jax.random.fold_in(rng, 6), dim), (parts,), jnp.float32, smallest / len(split), high / len(split))
        gain = gain * jnp.repeat(jnp.exp(heights), shape[dim] // parts).reshape((-1,) + (1,) * (len(shape) - 1 - dim))
    return gain


def split_up(amount, total, most, lean):
    loads = [(1 << 20) // math.isqrt(rank ** lean) + 1 for rank in range(2, amount + 1)]
    surplus, given = total - most - (amount - 1), [1] * (amount - 1)
    while surplus > 0:
        candidates = [i for i in range(amount - 1) if given[i] < most]
        whole, budget = sum([loads[i] for i in candidates]), surplus
        for i in candidates:
            more = min(most - given[i], max(1, budget * loads[i] // whole), surplus)
            given[i] = given[i] + more
            surplus = surplus - more
    return np.array([most] + given)


def ragged_sizes(rng, amount, total, reach, slope):
    if amount == 2:
        one = jax.random.randint(rng, (), max(1, total - reach), min(reach, total - 1) + 1)
        return jnp.stack([one, total - one])
    tallies = jnp.asarray(split_up(amount, total, reach, slope), jnp.int32)
    pairs = (amount - 1) // 2
    giver, sink = tallies[1:1 + 2 * pairs:2], tallies[2:2 + 2 * pairs:2]
    slack = jnp.minimum(giver - 1, reach - sink)
    moved = jax.random.randint(jax.random.fold_in(rng, 1), (pairs,), 0, 1 << 20) % (slack + 1)
    tallies = tallies.at[1:1 + 2 * pairs:2].set(giver - moved).at[2:2 + 2 * pairs:2].set(sink + moved)
    return tallies[jax.random.permutation(jax.random.fold_in(rng, 2), amount)]


def noise(own_key, extent, spread, reach, cuts=(), kind=jnp.bfloat16):
    factor_of = block_scale(own_key, extent, cuts, -0.22, 0.18) if cuts else 1.0
    drawn = jax.random.normal(own_key, extent, jnp.float32) * spread * factor_of
    return jnp.minimum(jnp.maximum(drawn, -reach), reach).astype(kind)


def setup_inputs(seed: int = 0) -> dict:
    key_list = jax.random.split(jax.random.key(seed), 16)
    tokens = noise(key_list[0], (GROUPS, GROUP_TOK, D), 1.0, 6.0, ((0, 16), (1, 8)))
    seq_lengths = jax.vmap(lambda own: ragged_sizes(own, SEQS, GROUP_TOK, LONGEST, 1))(jax.random.split(key_list[1], GROUPS)).reshape((GROUPS, SEQS)).astype(jnp.int32)
    token_places = jax.vmap(lambda own: jax.random.permutation(own, GROUP_TOK))(jax.random.split(key_list[2], GROUPS)).reshape((GROUPS, GROUP_TOK)).astype(jnp.int32)
    attention_gain = jnp.clip(1.0 + 0.1 * jax.random.normal(key_list[3], (D,), jnp.float32), 0.5, 1.5).astype(jnp.bfloat16)
    query_weight = noise(key_list[4], (D, HEADS * HD), D ** -0.5, 0.1875, ((0, 8),))
    key_weight = noise(key_list[5], (D, KV_HEADS * HD), D ** -0.5, 0.1875, ((0, 8),))
    value_weight = noise(key_list[6], (D, KV_HEADS * HD), D ** -0.5, 0.1875, ((0, 8),))
    query_gain = jnp.clip(0.796875 + 1.0 * jax.random.uniform(key_list[7], (HD,), jnp.float32) ** block_scale(key_list[7], (HD,), ((0, 8),), -0.2, 0.2), 0.796875, 1.796875).astype(jnp.bfloat16)
    key_gain = jnp.clip(0.796875 + 1.0 * jax.random.uniform(key_list[8], (HD,), jnp.float32) ** block_scale(key_list[8], (HD,), ((0, 8),), -0.2, 0.2), 0.796875, 1.796875).astype(jnp.bfloat16)
    out_weight = noise(key_list[9], (HEADS * HD, D), (HEADS * HD // 64) ** -0.5, 1.5, ((0, 8),))
    feedforward_gain = jnp.clip(1.0 + 0.1 * jax.random.normal(key_list[10], (D,), jnp.float32), 0.5, 1.5).astype(jnp.bfloat16)
    gate_weight = noise(key_list[11], (D, FF), D ** -0.5, 0.1875, ((0, 8),))
    up_weight = noise(key_list[12], (D, FF), D ** -0.5, 0.1875, ((0, 8),))
    down_weight = noise(key_list[13], (FF, D), (FF // 4) ** -0.5, 0.1875, ((0, 8),))
    cotangent = noise(key_list[14], (GROUPS, GROUP_TOK, D), 1.0, 6.0, ((0, 16), (1, 8)))
    return {"tokens": tokens, "seq_lengths": seq_lengths, "token_places": token_places, "attention_gain": attention_gain, "query_weight": query_weight, "key_weight": key_weight, "value_weight": value_weight, "query_gain": query_gain, "key_gain": key_gain, "out_weight": out_weight, "feedforward_gain": feedforward_gain, "gate_weight": gate_weight, "up_weight": up_weight, "down_weight": down_weight, "cotangent": cotangent}


norm_eps = 1e-05
rope_base = 1000000.0
highest = lax.Precision.HIGHEST

@jax.custom_vjp
def low(v):
    return lax.optimization_barrier(v.astype(jnp.bfloat16)).astype(jnp.float32)

@jax.custom_vjp
def low_back(v):
    return v

def low_keep(v):
    return (low(v), None)

def low_pass(kept, grad):
    return (grad,)

def back_keep(v):
    return (v, None)

def back_low(kept, grad):
    return (low(grad),)
low.defvjp(low_keep, low_pass)
low_back.defvjp(back_keep, back_low)

def rms_scale(values):
    return lax.rsqrt(lax.optimization_barrier(jnp.mean(values * values, axis=-1, keepdims=True)) + norm_eps)

def seq_layout(places, lengths):
    seq_ends = jnp.cumsum(lengths).astype(jnp.int32)
    passed = places[:, None] >= seq_ends[None, :]
    segment = lax.optimization_barrier(jnp.sum(passed.astype(jnp.int32), axis=1)).astype(jnp.int32)
    before = lax.optimization_barrier(jnp.sum(jnp.where(passed, lengths[None, :], 0), axis=1)).astype(jnp.int32)
    return (segment, (places - before).astype(jnp.int32))

def rope_tables(positions):
    half_size = HD // 2
    frequency = rope_base ** (-2.0 * jnp.arange(half_size, dtype=jnp.float32) / HD)
    angles = positions.astype(jnp.float32)[:, None] * frequency[None, :]
    return (jnp.cos(angles), jnp.sin(angles))

def rotate(values, cosine_table, sine_table):
    half_size = values.shape[-1] // 2
    front_half = values[..., :half_size]
    back_half = values[..., half_size:]
    cosine_rows = cosine_table[:, None, :]
    sine_rows = sine_table[:, None, :]
    return jnp.concatenate([front_half * cosine_rows - back_half * sine_rows, back_half * cosine_rows + front_half * sine_rows], axis=-1)

def attention(queries, key_rows, value_rows, segment, places):
    count_rows = queries.shape[0]
    block_rows = math.gcd(count_rows, 512)
    head_repeat = HEADS // KV_HEADS
    keys_full = jnp.repeat(key_rows, head_repeat, axis=1)
    values_full = jnp.repeat(value_rows, head_repeat, axis=1)

    def one_block(block_inputs):
        query_block, segment_block, place_block = block_inputs
        scores = low_back(jnp.einsum('qhd,khd->hqk', query_block, keys_full, precision=highest) * HD ** (-0.5))
        allowed = (segment_block[:, None] == segment[None, :]) & (places[None, :] <= place_block[:, None])
        scores = jnp.where(allowed[None], scores, -1e+30)
        weights = jax.nn.softmax(scores, axis=-1)
        return jnp.einsum('hqk,khd->qhd', low(weights), values_full, precision=highest)
    blocks = lax.map(jax.checkpoint(one_block), (queries.reshape(count_rows // block_rows, block_rows, HEADS, HD), segment.reshape(count_rows // block_rows, block_rows), places.reshape(count_rows // block_rows, block_rows)))
    return blocks.reshape(count_rows, HEADS, HD)

def forward(params, hidden_in, segment, positions, places):
    attention_gain, query_weight, key_weight, value_weight, query_gain, key_gain, out_weight, feedforward_gain, gate_weight, up_weight, down_weight = params
    count_rows = hidden_in.shape[0]
    first_normed = low(hidden_in * rms_scale(hidden_in) * attention_gain)
    query_pre = low_back(jnp.dot(first_normed, query_weight, precision=highest)).reshape(count_rows, HEADS, HD)
    key_pre = low_back(jnp.dot(first_normed, key_weight, precision=highest)).reshape(count_rows, KV_HEADS, HD)
    value_pre = low_back(jnp.dot(first_normed, value_weight, precision=highest)).reshape(count_rows, KV_HEADS, HD)
    cosine_table, sine_table = rope_tables(positions)
    queries = low(rotate(query_pre * rms_scale(query_pre) * query_gain, cosine_table, sine_table))
    key_rows = low(rotate(key_pre * rms_scale(key_pre) * key_gain, cosine_table, sine_table))
    value_rows = low(value_pre)
    mixed_out = attention(queries, key_rows, value_rows, segment, places)
    mixed_out = low(low_back(mixed_out)).reshape(count_rows, HEADS * HD)
    middle = hidden_in + low_back(jnp.dot(mixed_out, out_weight, precision=highest))
    second_normed = low(middle * rms_scale(middle) * feedforward_gain)
    gate_value = low_back(jnp.dot(second_normed, gate_weight, precision=highest))
    up_value = low_back(jnp.dot(second_normed, up_weight, precision=highest))
    hidden_ffn = low(low_back(jax.nn.silu(gate_value) * up_value))
    return middle + low_back(jnp.dot(hidden_ffn, down_weight, precision=highest))

def reference(tokens, seq_lengths, token_places, attention_gain, query_weight, key_weight, value_weight, query_gain, key_gain, out_weight, feedforward_gain, gate_weight, up_weight, down_weight, cotangent):
    params = (attention_gain.astype(jnp.float32), query_weight.astype(jnp.float32), key_weight.astype(jnp.float32), value_weight.astype(jnp.float32), query_gain.astype(jnp.float32), key_gain.astype(jnp.float32), out_weight.astype(jnp.float32), feedforward_gain.astype(jnp.float32), gate_weight.astype(jnp.float32), up_weight.astype(jnp.float32), down_weight.astype(jnp.float32))

    def one_group(totals, group_items):
        group_tokens, group_lengths, group_places, group_cotangent = group_items
        segment, positions = seq_layout(group_places, group_lengths)

        def apply_layer(weights, inputs):
            return forward(weights, inputs, segment, positions, group_places)
        result, pullback = jax.vjp(apply_layer, params, group_tokens.astype(jnp.float32))
        weight_grads, group_input_grad = pullback(group_cotangent.astype(jnp.float32))
        totals = jax.tree.map(jnp.add, totals, weight_grads)
        return (totals, (result.astype(jnp.bfloat16), group_input_grad))
    zeros_start = jax.tree.map(jnp.zeros_like, params)
    grads, (layer_out, input_grad) = lax.scan(one_group, zeros_start, (tokens, seq_lengths, token_places, cotangent))
    return (layer_out, input_grad, grads[0], grads[1], grads[2], grads[3], grads[4], grads[5], grads[6], grads[7], grads[8], grads[9], grads[10])
```

```python
import jax
import jax.numpy as jnp
from jax import lax
from jax.sharding import PartitionSpec as P

HEADS = 16
KV_HEADS = 8
HD = 64
AXES = ("shard", "replica")

norm_eps = 1e-05
rope_base = 1000000.0
bf16 = jnp.bfloat16
f32 = jnp.float32


def place(x, y, z, core):
    return ((x % 4) * 2 + (z % 4) % 2) * 16 + ((y % 4) * 2 + (z % 4) // 2) * 2 + core % 2


def pairs(move, keep=lambda x, y, z, c: True):
    found = []
    for x in range(4):
        for y in range(4):
            for z in range(4):
                for c in range(2):
                    if keep(x, y, z, c):
                        found.append((place(x, y, z, c), place(*move(x, y, z, c))))
    return found


def home(x, y, z, c):
    return c == z % 2


x_up = pairs(lambda x, y, z, c: (x + 1, y, z, c))
x_down = pairs(lambda x, y, z, c: (x - 1, y, z, c))
x_far = pairs(lambda x, y, z, c: (x + 2, y, z, c))
y_up = pairs(lambda x, y, z, c: (x, y + 1, z, c))
y_down = pairs(lambda x, y, z, c: (x, y - 1, z, c))
y_far = pairs(lambda x, y, z, c: (x, y + 2, z, c))
z_up = pairs(lambda x, y, z, c: (x, y, z + 1, c))
z_down = pairs(lambda x, y, z, c: (x, y, z - 1, c))
z_far = pairs(lambda x, y, z, c: (x, y, z + 2, c))
z_up_home = pairs(lambda x, y, z, c: (x, y, z + 1, c), home)
z_down_home = pairs(lambda x, y, z, c: (x, y, z - 1, c), home)
other_core = pairs(lambda x, y, z, c: (x, y, z, 1 - c))
from_home = pairs(lambda x, y, z, c: (x, y, z, 1 - c), home)
regroup = pairs(lambda x, y, z, c: (x, y, (z // 2) * 2 + c, z % 2))


def send(values, moves):
    return lax.ppermute(values, AXES, moves)


def cat(pieces, axis=0):
    return jnp.concatenate(pieces, axis=axis)


def pick(values, index, axis):
    return lax.dynamic_index_in_dim(values, index, axis, keepdims=False)


def unroll(values, index, axis):
    doubled = cat([values, values], axis)
    return lax.dynamic_slice_in_dim(doubled, (4 - index) % 4, 4, axis)


def gather_group(block):
    near = [send(block, x_down), send(block, x_far), send(block, x_up)]
    mine = cat([block] + near)
    return cat([mine, send(mine, other_core)])


def scatter_group(partial):
    rows = partial.shape[0] // 8
    blocks = partial.reshape(8, rows, partial.shape[1])
    got = send(blocks[4:].astype(bf16), other_core)
    summed = blocks[:4] + got.astype(f32)
    low = summed.astype(bf16)
    return (
        summed[0]
        + send(low[1], x_up).astype(f32)
        + send(low[2], x_far).astype(f32)
        + send(low[3], x_down).astype(f32)
    )


def spread_columns(columns, x, z_low):
    near = [pick(columns, (x + step) % 4, 1) for step in range(4)]
    got = jnp.stack([near[0], send(near[3], x_down), send(near[2], x_far), send(near[1], x_up)])
    across = cat([send(got[:2], z_up), send(got[2:], z_down)])
    even = jnp.where(z_low == 0, got, across)
    odd = jnp.where(z_low == 0, across, got)
    ordered = unroll(jnp.stack([even, odd], axis=1), x, 0)
    return ordered.reshape(1024, columns.shape[2])


def reduce_ring(pieces, up, down, far):
    return (
        pieces[0]
        + send(pieces[1].astype(bf16), up).astype(f32)
        + send(pieces[2].astype(bf16), far).astype(f32)
        + send(pieces[3].astype(bf16), down).astype(f32)
    )


def reduce_ring_wide(pieces, up, down):
    half = pieces[0].shape[0] // 2
    low = pieces[2].astype(bf16)
    to_up = send(low[:half], up).astype(f32)
    to_down = send(low[half:], down).astype(f32)
    first = cat([pieces[1][:half] + to_up, pieces[1][half:]])
    third = cat([pieces[3][:half], pieces[3][half:] + to_down])
    return (
        pieces[0]
        + send(first.astype(bf16), up).astype(f32)
        + send(third.astype(bf16), down).astype(f32)
    )


def gather_ring(block, up, down, far):
    return jnp.stack([block, send(block, down), send(block, far), send(block, up)])


def gather_ring_wide(block, up, down):
    half = block.shape[0] // 2
    after, before = send(block, down), send(block, up)
    across = cat([send(after[:half], down), send(before[half:], up)])
    return jnp.stack([block, after, across, before])


def reduce_weights(by_row, by_block, where):
    x, y, z, core, z_low = where
    width, block_width = by_row.shape[1], by_block.shape[1]
    grid = cat([by_row, by_block], 1).reshape(8, 4, 4, 8, width + block_width)
    wide = width > 512
    pieces = [pick(grid, (y + step) % 4, 1) for step in range(4)]
    if wide:
        rows = reduce_ring_wide(pieces, y_up, y_down)
    else:
        rows = reduce_ring(pieces, y_up, y_down, y_far)
    rows = reduce_ring([pick(rows, (z + step) % 4, 1) for step in range(4)], z_up, z_down, z_far)
    rows = rows.astype(bf16)
    own = rows[..., :width].reshape(4, 2, 8, width)
    near = [pick(own, (x + step) % 4, 0) for step in range(4)]
    got = jnp.stack([near[0], send(near[3], x_down), send(near[2], x_far), send(near[1], x_up)])
    flat = rows[..., width:].reshape(32, 2 * block_width)
    same = cat([pick(got, z_low, 1).reshape(32, width), flat], 1)
    odd = cat([pick(got, 1 - z_low, 1).reshape(32, width), flat], 1)
    stacked = jnp.stack([same, send(odd, z_down), send(same, z_far), send(odd, z_up)])
    stacked = stacked.reshape(128, width + 2 * block_width)
    if wide:
        stacked = gather_ring_wide(stacked, y_up, y_down)
    else:
        stacked = gather_ring(stacked, y_up, y_down, y_far)
    stacked = stacked.reshape(4, 4, 32, width + 2 * block_width)
    stacked = unroll(unroll(stacked, y, 0), z, 1)
    row_part, block_part = stacked[..., :width], stacked[..., width:]
    row_other = send(row_part, other_core)
    block_other = send(block_part, from_home)
    block_part = jnp.where(core == z_low, block_part, block_other)
    first = jnp.where(core == 0, row_part, row_other)
    second = jnp.where(core == 0, row_other, row_part)
    both = jnp.stack([first, second], axis=2).reshape(4, 4, 2, 4, 8, width)
    both = unroll(both, x, 3)
    by_row_out = both.transpose(0, 1, 4, 3, 2, 5).reshape(128, 8, width)
    by_block_out = block_part.reshape(4, 4, 8, 8, block_width)
    by_block_out = by_block_out.transpose(2, 0, 1, 3, 4).reshape(1024, block_width)
    return by_row_out, by_block_out


def rms_scale(values):
    return lax.rsqrt(jnp.mean(values * values, axis=-1, keepdims=True) + norm_eps)


def rope_tables(positions):
    half_size = HD // 2
    frequency = rope_base ** (-2.0 * jnp.arange(half_size, dtype=f32) / HD)
    angles = positions.astype(f32)[:, None] * frequency[None, :]
    return (jnp.cos(angles), jnp.sin(angles))


def rotate(values, cosine_table, sine_table):
    half_size = values.shape[-1] // 2
    front, back = values[..., :half_size], values[..., half_size:]
    cosine, sine = cosine_table[:, None, :], sine_table[:, None, :]
    return cat([front * cosine - back * sine, back * cosine + front * sine], -1)


def unrotate(values, cosine_table, sine_table):
    half_size = values.shape[-1] // 2
    front, back = values[..., :half_size], values[..., half_size:]
    cosine, sine = cosine_table[:, None, :], sine_table[:, None, :]
    return cat([front * cosine + back * sine, back * cosine - front * sine], -1)


def norm_back(inputs, scale_rows, gain_vector, upstream):
    normed = inputs * scale_rows
    scaled = upstream * gain_vector
    entry_grad = scale_rows * (scaled - normed * jnp.mean(scaled * normed, axis=-1, keepdims=True))
    return (entry_grad, upstream * normed)


def matmul(left_side, right_side):
    return jnp.dot(left_side, right_side, preferred_element_type=f32)


def matmul_tn(left_side, right_side):
    return lax.dot_general(
        left_side, right_side, (((0,), (0,)), ((), ())), preferred_element_type=f32
    )


def matmul_nt(left_side, right_side):
    return lax.dot_general(
        left_side, right_side, (((1,), (1,)), ((), ())), preferred_element_type=f32
    )


def attend(queries, keys, values, allowed):
    scores = jnp.einsum("qhd,kd->hqk", queries, keys, preferred_element_type=f32) * HD**-0.5
    scores = jnp.where(allowed[None], scores, -1e30)
    top = jnp.max(scores, axis=-1, keepdims=True)
    exponent = jnp.exp(scores - top)
    totals = jnp.sum(exponent, axis=-1, keepdims=True)
    probs = exponent / totals
    mixed = jnp.einsum("hqk,kd->qhd", probs.astype(bf16), values, preferred_element_type=f32)
    return mixed, top + jnp.log(totals)


def attend_back(queries, keys, values, allowed, logs, mixed_grad):
    scores = jnp.einsum("qhd,kd->hqk", queries, keys, preferred_element_type=f32) * HD**-0.5
    scores = jnp.where(allowed[None], scores, -1e30)
    probs = jnp.exp(scores - logs)
    prob_grad = jnp.einsum("qhd,kd->hqk", mixed_grad, values, preferred_element_type=f32)
    inner = jnp.sum(probs * prob_grad, axis=-1, keepdims=True)
    score_grad = (probs * (prob_grad - inner)).astype(bf16)
    scale = HD**-0.5
    query_grad = jnp.einsum("hqk,kd->qhd", score_grad, keys, preferred_element_type=f32) * scale
    key_grad = jnp.einsum("hqk,qhd->kd", score_grad, queries, preferred_element_type=f32) * scale
    value_grad = jnp.einsum(
        "hqk,qhd->kd", probs.astype(bf16), mixed_grad, preferred_element_type=f32
    )
    return query_grad, key_grad, value_grad


def on_device(
    tokens,
    seq_lengths,
    token_places,
    attention_gain,
    query_weight,
    key_weight,
    value_weight,
    query_gain,
    key_gain,
    out_weight,
    feedforward_gain,
    gate_weight,
    up_weight,
    down_weight,
    cotangent,
):
    shard, replica = lax.axis_index("shard"), lax.axis_index("replica")
    x, z_low = shard // 2, shard % 2
    y, z, core = replica // 4, (replica // 2) % 2 * 2 + z_low, replica % 2
    where = (x, y, z, core, z_low)

    own_places = lax.dynamic_slice_in_dim(token_places[0], shard * 128, 128)
    first_length = seq_lengths[0, :1]
    notes = cat(
        [
            attention_gain,
            feedforward_gain,
            query_gain,
            key_gain,
            (first_length // 32).astype(bf16),
            (first_length % 32).astype(bf16),
            jnp.zeros((110,), bf16),
            (own_places // 32).astype(bf16),
            (own_places % 32).astype(bf16),
            jnp.zeros((384,), bf16),
        ]
    )
    notes = jnp.broadcast_to(notes[None], (16, 1024))
    packed = send(cat([tokens[0], notes]), regroup)
    gathered = gather_group(packed).reshape(8, 144, 1024)
    inputs_all = gathered[:, :128].reshape(1024, 1024)
    notes_all = gathered[:, 128]
    inputs = packed[:128].astype(f32)

    both = jnp.concatenate(
        [
            query_weight.reshape(128, 4, 2, 128),
            key_weight.reshape(128, 4, 2, 64),
            value_weight.reshape(128, 4, 2, 64),
        ],
        axis=3,
    )
    attention_slice = spread_columns(pick(both, core, 2), x, z_low)
    rows_held = cat([out_weight, down_weight])
    rows_got = cat([send(rows_held[:352], z_up_home), send(rows_held[352:], z_down_home)])
    rows_slot = jnp.where(core == z_low, rows_held, rows_got)
    out_slot, down_slot = rows_slot[:128], rows_slot[128:]
    both = jnp.concatenate(
        [gate_weight.reshape(128, 4, 2, 576), up_weight.reshape(128, 4, 2, 576)], axis=3
    )
    feed_slice = spread_columns(pick(both, core, 2), x, z_low)
    upstream_own = send(cotangent[0], regroup)
    upstream = gather_group(upstream_own)

    gains = notes_all[:, :384].reshape(2, 4, 384)
    gains = unroll(jnp.where(core == 0, gains, gains[::-1]), x, 1).transpose(1, 0, 2)
    gain_first = gains[..., :128].reshape(1024).astype(f32)
    gain_second = gains[..., 128:256].reshape(1024).astype(f32)
    gain_query = gains[..., 256:264].reshape(64).astype(f32)
    gain_key = gains[..., 264:272].reshape(64).astype(f32)
    length = (notes_all[0, 272].astype(f32) * 32 + notes_all[0, 273].astype(f32)).astype(jnp.int32)
    places = notes_all[:, 384:512].astype(f32) * 32 + notes_all[:, 512:640].astype(f32)
    places = places.reshape(1024).astype(jnp.int32)
    segment = (places >= length).astype(jnp.int32)
    cosine, sine = rope_tables(places - segment * length)
    allowed = (segment[:, None] == segment[None, :]) & (places[None, :] <= places[:, None])

    inputs_all = inputs_all.astype(f32)
    first_scale = rms_scale(inputs_all)
    first_normed = (inputs_all * first_scale * gain_first).astype(bf16)
    pre = matmul(first_normed, attention_slice)
    query_pre = pre[:, :128].reshape(1024, 2, HD)
    key_pre = pre[:, 128:192].reshape(1024, 1, HD)
    values = pre[:, 192:].astype(bf16)
    query_scale, key_scale = rms_scale(query_pre), rms_scale(key_pre)
    queries = rotate(query_pre * query_scale * gain_query, cosine, sine).astype(bf16)
    keys = rotate(key_pre * key_scale * gain_key, cosine, sine).astype(bf16)[:, 0]
    mixed, logs = attend(queries, keys, values, allowed)
    mixed = mixed.astype(bf16).reshape(1024, 128)
    middle = inputs + scatter_group(matmul(mixed, out_slot))

    second_scale = rms_scale(middle)
    second_normed = gather_group((middle * second_scale * gain_second).astype(bf16))
    pre = matmul(second_normed, feed_slice)
    gate, up = pre[:, :576], pre[:, 576:]
    sigmoid = jax.nn.sigmoid(gate)
    silu = gate * sigmoid
    hidden = (silu * up).astype(bf16)
    hidden_grad = matmul_nt(upstream, down_slot).astype(bf16).astype(f32)
    gate_grad = (hidden_grad * up * sigmoid * (1.0 + gate * (1.0 - sigmoid))).astype(bf16)
    up_grad = (hidden_grad * silu).astype(bf16)
    pre_grad = cat([gate_grad, up_grad], 1)
    second_grad = scatter_group(matmul_nt(pre_grad, feed_slice))
    result = middle + scatter_group(matmul(hidden, down_slot))
    feed_weight_grad = matmul_tn(second_normed, pre_grad)
    down_weight_grad = matmul_tn(upstream, hidden)
    feed_sum, down_sum = reduce_weights(feed_weight_grad, down_weight_grad, where)

    middle_norm_grad, second_gain_terms = norm_back(middle, second_scale, gain_second, second_grad)
    middle_grad = upstream_own.astype(f32) + middle_norm_grad
    second_gain_grad = jnp.sum(second_gain_terms, axis=0)
    branch_grad = gather_group(middle_grad.astype(bf16))
    mixed_grad = matmul_nt(branch_grad, out_slot).astype(bf16)
    out_weight_grad = matmul_tn(branch_grad, mixed)
    query_grad, key_grad, value_grad = attend_back(
        queries, keys, values, allowed, logs, mixed_grad.reshape(1024, 2, HD)
    )
    key_turned = unrotate(key_grad[:, None], cosine, sine)
    key_pre_grad, key_terms = norm_back(key_pre, key_scale, gain_key, key_turned)
    query_turned = unrotate(query_grad, cosine, sine)
    query_pre_grad, query_terms = norm_back(query_pre, query_scale, gain_query, query_turned)
    pre_grad = cat(
        [query_pre_grad.reshape(1024, 128), key_pre_grad.reshape(1024, HD), value_grad], 1
    ).astype(bf16)
    first_partial = matmul_nt(pre_grad, attention_slice)
    first_grad = scatter_group(first_partial)
    attention_weight_grad = matmul_tn(first_normed, pre_grad)
    first_gain_grad = jnp.sum(first_partial * (inputs_all * first_scale), axis=0)
    small = jnp.stack([jnp.sum(query_terms, axis=(0, 1)), jnp.sum(key_terms, axis=(0, 1))], 1)
    small = jnp.pad(small.reshape(8, 8, 2), ((0, 0), (0, 120), (0, 0))).reshape(1024, 2)
    extra = cat([first_gain_grad[:, None], second_gain_grad[:, None], small], 1)
    extra = jnp.pad(extra, ((0, 0), (0, 124)))
    attention_sum, out_sum = reduce_weights(
        cat([attention_weight_grad, extra], 1), out_weight_grad, where
    )
    own_scale = rms_scale(inputs)
    input_norm_grad, _ = norm_back(inputs, own_scale, gain_first, first_grad)
    input_grad = middle_grad + input_norm_grad

    attention_sum = attention_sum.astype(f32)
    gain_sums = jnp.sum(attention_sum[:, :, 256:260], axis=1)
    feed_sum = feed_sum.astype(f32)
    return (
        send(result.astype(bf16), regroup)[None],
        send(input_grad.astype(bf16), regroup).astype(f32)[None],
        gain_sums[:, 0],
        attention_sum[:, :, :128].reshape(128, 1024),
        attention_sum[:, :, 128:192].reshape(128, 512),
        attention_sum[:, :, 192:256].reshape(128, 512),
        gain_sums[:8, 2],
        gain_sums[:8, 3],
        out_sum.T.astype(f32),
        gain_sums[:, 1],
        feed_sum[:, :, :576].reshape(128, 4608),
        feed_sum[:, :, 576:].reshape(128, 4608),
        down_sum.T.astype(f32),
    )


def solution(mesh):
    placed = (
        P("replica", "shard", None),
        P("replica", None),
        P("replica", None),
        P("shard"),
        P("shard", None),
        P("shard", None),
        P("shard", None),
        P("shard"),
        P("shard"),
        P("shard", None),
        P("shard"),
        P("shard", None),
        P("shard", None),
        P("shard", None),
        P("replica", "shard", None),
    )
    return jax.shard_map(
        on_device,
        mesh=mesh,
        in_specs=placed,
        out_specs=(
            P("replica", "shard", None),
            P("replica", "shard", None),
            P("shard"),
            P("shard", None),
            P("shard", None),
            P("shard", None),
            P("shard"),
            P("shard"),
            P("shard", None),
            P("shard"),
            P("shard", None),
            P("shard", None),
            P("shard", None),
        ),
        check_vma=False,
    )
```

```python
import jax
import jax.numpy as jnp
from jax import lax
from jax.experimental import pallas as pl
from jax.experimental.pallas import tpu as pltpu
from jax.sharding import PartitionSpec as P

HEADS = 16
KV_HEADS = 8
HD = 64
AXES = ("shard", "replica")

norm_eps = 1e-05
rope_base = 1000000.0
bf16 = jnp.bfloat16
f32 = jnp.float32


def place(x, y, z, core):
    return ((x % 4) * 2 + (z % 4) % 2) * 16 + ((y % 4) * 2 + (z % 4) // 2) * 2 + core % 2


def pairs(move, keep=lambda x, y, z, c: True):
    found = []
    for x in range(4):
        for y in range(4):
            for z in range(4):
                for c in range(2):
                    if keep(x, y, z, c):
                        found.append((place(x, y, z, c), place(*move(x, y, z, c))))
    return found


def home(x, y, z, c):
    return c == z % 2


x_up = pairs(lambda x, y, z, c: (x + 1, y, z, c))
x_down = pairs(lambda x, y, z, c: (x - 1, y, z, c))
x_far = pairs(lambda x, y, z, c: (x + 2, y, z, c))
y_up = pairs(lambda x, y, z, c: (x, y + 1, z, c))
y_down = pairs(lambda x, y, z, c: (x, y - 1, z, c))
y_far = pairs(lambda x, y, z, c: (x, y + 2, z, c))
z_up = pairs(lambda x, y, z, c: (x, y, z + 1, c))
z_down = pairs(lambda x, y, z, c: (x, y, z - 1, c))
z_far = pairs(lambda x, y, z, c: (x, y, z + 2, c))
z_up_home = pairs(lambda x, y, z, c: (x, y, z + 1, c), home)
z_down_home = pairs(lambda x, y, z, c: (x, y, z - 1, c), home)
other_core = pairs(lambda x, y, z, c: (x, y, z, 1 - c))
from_home = pairs(lambda x, y, z, c: (x, y, z, 1 - c), home)
regroup = pairs(lambda x, y, z, c: (x, y, (z // 2) * 2 + c, z % 2))


def send(values, moves):
    return lax.ppermute(values, AXES, moves)


def cat(pieces, axis=0):
    return jnp.concatenate(pieces, axis=axis)


def pick(values, index, axis):
    return lax.dynamic_index_in_dim(values, index, axis, keepdims=False)


def unroll(values, index, axis):
    doubled = cat([values, values], axis)
    return lax.dynamic_slice_in_dim(doubled, (4 - index) % 4, 4, axis)


x_rings = [
    [place(x, y, z, core) for x in range(4)] for core in range(2) for y in range(4) for z in range(4)
]
planes = [
    [place(x, y, z, core) for y in range(4) for z in range(4)] for x in range(4) for core in range(2)
]
x_groups = [
    [place(x, y, z, core) for x in range(4) for core in range(2)]
    for y in range(4)
    for z in range(4)
]


def join(*values):
    return lax.optimization_barrier(values)


def exchange(values, groups):
    return lax.all_to_all(values, AXES, 0, 0, axis_index_groups=groups)


def gather_half(block):
    return exchange(jnp.broadcast_to(block[None], (4, *block.shape)), x_rings)


def scatter_sums(own, got):
    summed = (own + got.astype(f32)).astype(bf16).reshape(4, 128, own.shape[1])
    return exchange(summed, x_rings)


def add_up(parts):
    return jnp.sum(parts.astype(f32), axis=0)


def units(values, rows, columns):
    height, width = values.shape
    return values.reshape(rows, height // rows // 8, 8, columns, width // columns // 128, 128)


def rows_for_planes(by_row):
    grid = by_row.astype(bf16).reshape(8, 4, 4, 8, by_row.shape[1] // 128, 128)
    return grid.transpose(1, 2, 0, 4, 3, 5)


def block_for_planes(by_block):
    return units(by_block.astype(bf16), 4, 4).transpose(0, 3, 1, 4, 2, 5)


def exchange_rows(by_row):
    return exchange(by_row.reshape(4, 2, *by_row.shape[1:]), x_rings)


def return_planes(got, by_block):
    both = [cat([got[:, parity].reshape(-1, 128), by_block.reshape(-1, 128)]) for parity in range(2)]
    return exchange(jnp.stack(both * 8), planes)


def exchange_x(by_row, x):
    own = by_row.reshape(4, 2, *by_row.shape[1:])
    near = [pick(own, (x + step) % 4, 0) for step in range(4)]
    return jnp.stack([near[0]] + send_x(*near[1:])[::-1])


def send_ring(pieces, up, down, far):
    low = [piece.astype(bf16) for piece in pieces[1:]]
    return [send(low[0], up), send(low[1], far), send(low[2], down)]


def gather_z(got, by_block, z_low):
    same = cat([pick(got, z_low, 1).reshape(-1, 128), by_block.reshape(-1, 128)])
    odd = cat([pick(got, 1 - z_low, 1).reshape(-1, 128), by_block.reshape(-1, 128)])
    return jnp.stack([same, send(odd, z_down), send(same, z_far), send(odd, z_up)])


def gather_y(block):
    return jnp.stack([block, send(block, y_down), send(block, y_far), send(block, y_up)])


def send_x(first, second, third):
    return [send(first, x_up), send(second, x_far), send(third, x_down)]


def gather_x(block):
    return [block, send(block, x_down), send(block, x_far), send(block, x_up)]


def quarter(values, step):
    return values[step * 128 : (step + 1) * 128]


def scatter_parts(own, got):
    sums = [quarter(own, step) + quarter(got, step).astype(f32) for step in range(4)]
    return sums[0], [part.astype(bf16) for part in sums[1:]]


def turn_back(rows, x):
    blocks = rows.reshape(4, 128, rows.shape[1])
    return lax.dynamic_slice_in_dim(cat([blocks, blocks]), x, 4, 0).reshape(rows.shape)


def whole(count):
    return [pl.BlockSpec(memory_space=pltpu.VMEM)] * count


def spot(values):
    return jnp.stack(values).astype(jnp.int32)


def call(kernel, scalars, arrays, outs, scratch=(), limit=40, flops=0):
    size = sum(a.size * a.dtype.itemsize for a in arrays)
    return pl.pallas_call(
        kernel,
        out_shape=[jax.ShapeDtypeStruct(shape, kind) for shape, kind in outs],
        in_specs=[pl.BlockSpec(memory_space=pltpu.SMEM)] + whole(len(arrays)),
        out_specs=whole(len(outs)),
        scratch_shapes=list(scratch),
        compiler_params=pltpu.CompilerParams(vmem_limit_bytes=limit * 2**20),
        cost_estimate=pl.CostEstimate(flops=flops, bytes_accessed=size, transcendentals=0),
    )(scalars, *arrays)


def rms_scale(values):
    return lax.rsqrt(jnp.mean(values * values, axis=-1, keepdims=True) + norm_eps)


def norm_back(inputs, scale_rows, gain_vector, upstream):
    normed = inputs * scale_rows
    scaled = upstream * gain_vector
    entry_grad = scale_rows * (scaled - normed * jnp.mean(scaled * normed, axis=-1, keepdims=True))
    return (entry_grad, upstream * normed)


def matmul(left_side, right_side):
    return jnp.dot(left_side, right_side, preferred_element_type=f32)


def matmul_tn(left_side, right_side):
    return lax.dot_general(
        left_side, right_side, (((0,), (0,)), ((), ())), preferred_element_type=f32
    )


def matmul_nt(left_side, right_side):
    return lax.dot_general(
        left_side, right_side, (((1,), (1,)), ((), ())), preferred_element_type=f32
    )


def columns_kernel(spot_ref, q_ref, k_ref, v_ref, gate_ref, up_ref, packed_ref, out_ref, feed_ref):
    core = spot_ref[0]
    for at in range(4):
        out_ref[at, :, :1024] = packed_ref[...]
        out_ref[at, 128:, 1024:] = jnp.zeros((16, 256), bf16)
        out_ref[at, :128, 1024:1152] = jnp.where(
            core == 0,
            q_ref[:, at * 256 : at * 256 + 128],
            q_ref[:, at * 256 + 128 : at * 256 + 256],
        )
        for ref, low in ((k_ref, 1152), (v_ref, 1216)):
            pair = ref[:, at * 128 : at * 128 + 128]
            out_ref[at, :128, low : low + 64] = jnp.where(core == 0, pair[:, :64], pair[:, 64:])
        for row, ref in enumerate((gate_ref, up_ref)):
            some = ref[:, at * 1152 : at * 1152 + 1152]
            feed_ref[at, :, row * 576 : row * 576 + 576] = jnp.where(
                core == 0, some[:, :576], some[:, 576:]
            )


def pick_columns(query_weight, key_weight, value_weight, gate_weight, up_weight, packed, core):
    outs = [((4, 144, 1280), bf16), ((4, 128, 1152), bf16)]
    arrays = (query_weight, key_weight, value_weight, gate_weight, up_weight, packed)
    return call(columns_kernel, spot([core]), arrays, outs, limit=16)


def pack_kernel(tokens_ref, first_ref, second_ref, small_ref, out_ref):
    out_ref[:128, :] = tokens_ref[...]
    out_ref[128:, :] = jnp.zeros((16, 1024), bf16)
    for step, ref in enumerate((first_ref, second_ref, small_ref)):
        row = jnp.broadcast_to(ref[...].astype(f32), (16, 128)).astype(bf16)
        out_ref[128:, step * 128 : step * 128 + 128] = row


def pack(*arrays):
    return pl.pallas_call(
        pack_kernel, out_shape=jax.ShapeDtypeStruct((144, 1024), bf16)
    )(*arrays)


def lanes(width):
    return lax.broadcasted_iota(jnp.int32, (1, width), 1)


def swap_halves(values):
    first = lanes(256) % 64 < 32
    return jnp.where(first, pltpu.roll(values, 224, 1), pltpu.roll(values, 32, 1))


def head_means(values):
    lane = lanes(256)
    found = jnp.zeros_like(values)
    for head in range(3):
        inside = (lane >= head * 64) & (lane < head * 64 + 64)
        mean = jnp.sum(jnp.where(inside, values, 0.0), axis=1, keepdims=True) * (1.0 / 64)
        found = jnp.where(inside, mean, found)
    return found


def twice(values):
    return jnp.concatenate([values, values], axis=1)


def attend_kernel(
    spot_ref,
    half_ref,
    far_ref,
    across_ref,
    gain_ref,
    cosine_ref,
    sine_ref,
    place_ref,
    place_row_ref,
    start_row_ref,
    weight_ref,
    normed_ref,
    qkv_ref,
    head_ref,
    scale_ref,
    mixed_ref,
    logs_ref,
    gains_ref,
    turned_ref,
):
    z_low, core = spot_ref[0], spot_ref[1]
    for at in range(4):
        for piece, parity in ((half_ref[at, :128, 1024:], z_low), (across_ref[at], 1 - z_low)):
            weight_ref[pl.ds(pl.multiple_of((at * 2 + parity) * 128, 128), 128), :] = piece
        for ref, slot in ((half_ref, at * 2 + core), (far_ref, at * 2 + 1 - core)):
            to = pl.ds(pl.multiple_of(slot * 128, 128), 128)
            gains_ref[:8, to] = ref[at, 128:, :128].astype(f32)[:8]
            gains_ref[8:, to] = ref[at, 128:, 128:256].astype(f32)[:8]
    gain = gain_ref[...]
    lane = lanes(256)
    for block in range(8):
        ref = half_ref if block < 4 else far_ref
        rows = slice(block * 128, block * 128 + 128)
        inputs = ref[block % 4, :128, :1024].astype(f32)
        scale = lax.rsqrt(jnp.mean(inputs * inputs, axis=1, keepdims=True) + norm_eps)
        normed = (inputs * scale * gains_ref[0:1, :]).astype(bf16)
        normed_ref[rows, :] = normed
        pre = matmul(normed, weight_ref[...])
        scales = lax.rsqrt(head_means(pre * pre) + norm_eps)
        heads = pre * scales
        head_ref[rows, :] = heads
        scale_ref[rows, :] = scales
        gained = heads * gain
        turned = gained * twice(cosine_ref[rows, :]) + swap_halves(gained) * twice(sine_ref[rows, :])
        qkv_ref[rows, :] = jnp.where(lane < 192, turned, pre).astype(bf16)
        turned_ref[:, rows] = jnp.where(lane < 192, turned, pre)[:, 128:].T.astype(bf16)

    keys = qkv_ref[:, 128:192]
    values = turned_ref[64:, :]
    place = place_ref[...]
    for part in range(4):
        rows = slice(part * 256, part * 256 + 256)
        allowed = (place <= place_row_ref[:, rows]) & (place >= start_row_ref[:, rows])
        for head in range(2):
            columns = slice(head * 64, head * 64 + 64)
            scores = matmul_nt(keys, qkv_ref[rows, columns]) * HD**-0.5
            scores = jnp.where(allowed, scores, -1e30)
            top = jnp.max(scores, axis=0, keepdims=True)
            exponent = jnp.exp(scores - top)
            total = jnp.sum(exponent, axis=0, keepdims=True)
            probs = (exponent * (1.0 / total)).astype(bf16)
            mixed_ref[rows, columns] = matmul(values, probs).T.astype(bf16)
            logs_ref[head : head + 1, rows] = top + jnp.log(total)


def attend(half, far, across, gain, tables, where):
    outs = [
        ((1024, 256), bf16),
        ((1024, 1024), bf16),
        ((1024, 256), bf16),
        ((1024, 256), f32),
        ((1024, 256), f32),
        ((1024, 128), bf16),
        ((8, 1024), f32),
        ((16, 1024), f32),
    ]
    arrays = (half, far, across, gain, *tables)
    scratch = [pltpu.VMEM((128, 1024), bf16)]
    scalars = spot([where[4], where[3]])
    return call(attend_kernel, scalars, arrays, outs, scratch, 44, 2 * 1024**3)


def attend_back_kernel(
    spot_ref,
    near_ref,
    far_ref,
    out_weight_ref,
    weight_ref,
    normed_ref,
    qkv_ref,
    head_ref,
    scale_ref,
    mixed_ref,
    logs_ref,
    gain_ref,
    cosine_ref,
    sine_ref,
    place_ref,
    place_row_ref,
    start_row_ref,
    other_ref,
    own_ref,
    pre_grad_ref,
    out_grad_ref,
    sums_ref,
    first_ref,
    branch_ref,
    mixed_grad_ref,
    grad_ref,
    turned_ref,
):
    x = spot_ref[0]
    for step in range(4):
        to = pl.multiple_of(((x + step) % 4) * 128, 128)
        piece = slice(step * 128, step * 128 + 128)
        branch_ref[pl.ds(to, 128), :] = near_ref[piece, :]
        branch_ref[pl.ds(to + 512, 128), :] = far_ref[piece, :]
    mixed_grad_ref[...] = matmul_nt(branch_ref[...], out_weight_ref[...]).astype(bf16)
    keys, values = qkv_ref[:, 128:192], qkv_ref[:, 192:]
    turned_ref[...] = qkv_ref[:, 128:].astype(f32).T.astype(bf16)
    keys_turned = turned_ref[:64, :]
    place = place_ref[...]
    grad_ref[:, 128:] = jnp.zeros((1024, 128), f32)
    for part in range(4):
        rows = slice(part * 256, part * 256 + 256)
        allowed = (place <= place_row_ref[:, rows]) & (place >= start_row_ref[:, rows])
        for head in range(2):
            columns = slice(head * 64, head * 64 + 64)
            queries, upstream = qkv_ref[rows, columns], mixed_grad_ref[rows, columns]
            scores = matmul_nt(keys, queries) * HD**-0.5
            probs = jnp.where(allowed, jnp.exp(scores - logs_ref[head : head + 1, rows]), 0.0)
            prob_grad = matmul_nt(values, upstream)
            inner = jnp.sum(probs * prob_grad, axis=0, keepdims=True)
            score_grad = (probs * (prob_grad - inner)).astype(bf16)
            grad_ref[:, 128:192] += matmul(score_grad, queries) * HD**-0.5
            grad_ref[:, 192:] += matmul(probs.astype(bf16), upstream)
            grad_ref[rows, columns] = matmul(keys_turned, score_grad).T * HD**-0.5
    out_grad_ref[...] = matmul(mixed_ref[...].astype(f32).T.astype(bf16), branch_ref[...])
    gain = gain_ref[...]
    lane = lanes(256)
    sums_ref[...] = jnp.zeros((8, 256), f32)
    first_ref[...] = jnp.zeros((8, 1024), f32)
    for block in (4, 5, 6, 7, 0, 1, 2, 3):
        rows = slice(block * 128, block * 128 + 128)
        grads = grad_ref[rows, :]
        back = grads * twice(cosine_ref[rows, :]) - swap_halves(grads) * twice(sine_ref[rows, :])
        heads = head_ref[rows, :]
        sums_ref[0:1, :] += jnp.sum(back * heads, axis=0, keepdims=True)
        gained = back * gain
        entry = scale_ref[rows, :] * (gained - heads * head_means(gained * heads))
        pre_grad = jnp.where(lane < 192, entry, grads).astype(bf16)
        pre_grad_ref[rows, :] = pre_grad
        partial = matmul_nt(pre_grad, weight_ref[...])
        first_ref[0:1, :] += jnp.sum(partial * normed_ref[rows, :].astype(f32), axis=0, keepdims=True)
        if block < 4:
            own_ref[rows, :] = partial
        else:
            other_ref[(block - 4) * 128 : (block - 3) * 128, :] = partial.astype(bf16)


def attend_back(near, far, out_slot, kept, gain, tables, where):
    outs = [
        ((512, 1024), bf16),
        ((512, 1024), f32),
        ((1024, 256), bf16),
        ((128, 1024), f32),
        ((8, 256), f32),
        ((8, 1024), f32),
    ]
    arrays = (near, far, out_slot, *kept, gain, *tables)
    scratch = [
        pltpu.VMEM((1024, 1024), bf16),
        pltpu.VMEM((1024, 128), bf16),
        pltpu.VMEM((1024, 256), f32),
        pltpu.VMEM((128, 1024), bf16),
    ]
    return call(attend_back_kernel, spot([where[0]]), arrays, outs, scratch, 48, 4 * 1024**3)


def feed_kernel(
    spot_ref,
    half_ref,
    far_ref,
    upstream_ref,
    came_ref,
    lower_ref,
    upper_ref,
    down_ref,
    other_ref,
    own_ref,
    hidden_ref,
    pre_grad_ref,
    normed_ref,
    weight_ref,
):
    z_low, core = spot_ref[0], spot_ref[1]
    for at in range(4):
        across = lower_ref if at < 2 else upper_ref
        for piece, parity in ((came_ref[at], z_low), (across[at % 2], 1 - z_low)):
            weight_ref[pl.ds(pl.multiple_of((at * 2 + parity) * 128, 128), 128), :] = piece
    normed_ref[:512] = half_ref[...]
    normed_ref[512:] = far_ref[...]

    def rows_of(part, slot_core):
        slots = [
            pl.ds(pl.multiple_of((part * 4 + step * 2 + slot_core) * 128, 128), 128)
            for step in range(2)
        ]
        return slots, jnp.concatenate([upstream_ref[slot, :] for slot in slots], axis=0)

    def work(start, part, slot_core):
        rows = pl.ds(pl.multiple_of(start, 256), 256)
        slots, upstream = rows_of(part, slot_core)
        pre = matmul(normed_ref[rows, :], weight_ref[...])
        gate, up = pre[:, :576], pre[:, 576:]
        hidden_grad = matmul_nt(upstream, down_ref[...]).astype(bf16).astype(f32)
        sigmoid = 1.0 / (1.0 + jnp.exp(-gate))
        silu = gate * sigmoid
        hidden = (silu * up).astype(bf16)
        for step, slot in enumerate(slots):
            hidden_ref[slot, :] = hidden[step * 128 : step * 128 + 128]
        gate_grad = hidden_grad * up * sigmoid * (1.0 + gate * (1.0 - sigmoid))
        pre_grad = jnp.concatenate([gate_grad, hidden_grad * silu], axis=1).astype(bf16)
        pre_grad_ref[rows, :] = pre_grad
        return matmul_nt(pre_grad, weight_ref[...])

    def other_half(part, carry):
        rows = pl.ds(pl.multiple_of(part * 256, 256), 256)
        other_ref[rows, :] = work(part * 256 + 512, part, 1 - core).astype(bf16)
        return carry

    def own_half(part, carry):
        rows = pl.ds(pl.multiple_of(part * 256, 256), 256)
        own_ref[rows, :] = work(part * 256, part, core)
        return carry

    lax.fori_loop(0, 2, other_half, 0)
    lax.fori_loop(0, 2, own_half, 0)


def feed(half, far, upstream, weights, down_slot, where):
    arrays = (half, far, upstream, *weights, down_slot)
    outs = [
        ((512, 1024), bf16),
        ((512, 1024), f32),
        ((1024, 576), bf16),
        ((1024, 1152), bf16),
        ((1024, 1024), bf16),
    ]
    scratch = [pltpu.VMEM((1024, 1152), bf16)]
    scalars = spot([where[4], where[3]])
    return call(feed_kernel, scalars, arrays, outs, scratch, 44, 6 * 1024**3)


def feed_grads_kernel(spot_ref, mine_ref, other_ref, gate_ref, up_ref, down_ref):
    core, z_low = spot_ref[0], spot_ref[1]
    home = core == z_low
    for at in range(16):
        mine = mine_ref[at].astype(f32)
        other = other_ref[at].astype(f32)
        first = jnp.where(core == 0, mine[:288], other[:288])
        second = jnp.where(core == 0, other[:288], mine[:288])
        block = jnp.where(home, mine[288:], other[288:])
        rows = slice(at * 8, at * 8 + 8)
        for x in range(4):
            wide = [
                jnp.concatenate(
                    [one[(x * 9 + i) * 8 : (x * 9 + i) * 8 + 8] for i in range(9)], axis=1
                )
                for one in (first, second)
            ]
            columns = slice(x * 1152, x * 1152 + 1152)
            gate_ref[rows, columns] = jnp.concatenate([one[:, :576] for one in wide], axis=1)
            up_ref[rows, columns] = jnp.concatenate([one[:, 576:] for one in wide], axis=1)
        for i in range(18):
            for j in range(2):
                piece = block[(i * 2 + j) * 8 : (i * 2 + j) * 8 + 8]
                low, left = at // 4 * 144 + i * 8, at % 4 * 256 + j * 128
                down_ref[low : low + 8, left : left + 128] = piece


def feed_grads(mine, other, where):
    outs = [((128, 4608), f32), ((128, 4608), f32), ((576, 1024), f32)]
    return call(feed_grads_kernel, spot(where[3:]), (mine, other), outs, (), 40)


def attention_grads_kernel(spot_ref, mine_ref, other_ref, q_ref, k_ref, v_ref, out_ref, extra_ref):
    core, z_low, x, y, z = (spot_ref[i] for i in range(5))
    home = core == z_low
    for y_step in range(4):
        for z_step in range(4):
            mine = mine_ref[y_step, z_step].astype(f32)
            other = other_ref[y_step, z_step].astype(f32)
            first = jnp.where(core == 0, mine[:96], other[:96])
            second = jnp.where(core == 0, other[:96], mine[:96])
            block = jnp.where(home, mine[96:], other[96:])
            y_at, z_at = (y + y_step) % 4, (z + z_step) % 4
            rows = pl.ds(pl.multiple_of((y_at * 4 + z_at) * 8, 8), 8)
            extra = jnp.zeros((8, 128), f32)
            for step in range(4):
                slot, low = (x + step) % 4, step * 24
                to = pl.multiple_of(slot * 256, 128)
                q_ref[rows, pl.ds(to, 128)] = first[low : low + 8]
                q_ref[rows, pl.ds(to + 128, 128)] = second[low : low + 8]
                one, two = first[low + 8 : low + 16], second[low + 8 : low + 16]
                columns = pl.ds(pl.multiple_of(slot * 128, 128), 128)
                k_ref[rows, columns] = jnp.concatenate([one[:, :64], two[:, :64]], axis=1)
                v_ref[rows, columns] = jnp.concatenate([one[:, 64:], two[:, 64:]], axis=1)
                extra = extra + first[low + 16 : low + 24] + second[low + 16 : low + 24]
            extra_ref[rows, :] = extra
            for i in range(4):
                for j in range(2):
                    to = pl.ds(pl.multiple_of(y_at * 32 + i * 8, 8), 8)
                    columns = pl.ds(pl.multiple_of(z_at * 256 + j * 128, 128), 128)
                    out_ref[to, columns] = block[(i * 2 + j) * 8 : (i * 2 + j) * 8 + 8]


def attention_grads(mine, other, where):
    outs = [
        ((128, 1024), f32),
        ((128, 512), f32),
        ((128, 512), f32),
        ((128, 1024), f32),
        ((128, 128), f32),
    ]
    x, y, z, core, z_low = where
    return call(
        attention_grads_kernel, spot([core, z_low, x, y, z]), (mine, other), outs, (), 24
    )


def on_device(
    tokens,
    seq_lengths,
    token_places,
    attention_gain,
    query_weight,
    key_weight,
    value_weight,
    query_gain,
    key_gain,
    out_weight,
    feedforward_gain,
    gate_weight,
    up_weight,
    down_weight,
    cotangent,
):
    shard, replica = lax.axis_index("shard"), lax.axis_index("replica")
    x, z_low = shard // 2, shard % 2
    y, z, core = replica // 4, (replica // 2) % 2 * 2 + z_low, replica % 2
    where = (x, y, z, core, z_low)

    facts = cat([token_places, jnp.broadcast_to(seq_lengths[:, :1], (1, 128))], 1)
    facts = jnp.where(core == z_low, facts, send(facts, other_core))
    places = facts[0, :1024].reshape(4, 2, 128)
    places = jnp.stack([pick(places, core, 1), pick(places, 1 - core, 1)]).reshape(1, 1024)
    starts = jnp.where(places >= facts[:, 1024:1025], facts[:, 1024:1025], 0)
    lane = jnp.arange(128)
    frequency = rope_base ** (-2.0 * (lane % 32).astype(f32) / HD)
    angles = (places - starts).astype(f32).reshape(1024, 1) * frequency[None, :]
    cosine, sine = jnp.cos(angles), jnp.sin(angles) * jnp.where(lane % 64 < 32, -1.0, 1.0)
    places_f = places.astype(f32)
    tables = (cosine, sine, places_f.reshape(1024, 1), places_f, starts.astype(f32))

    small = cat([query_gain, key_gain, jnp.zeros((112,), bf16)])
    packed = pack(tokens[0], attention_gain[None], feedforward_gain[None], small[None])
    packed = send(packed, regroup)
    packed_out, for_feed = pick_columns(
        query_weight, key_weight, value_weight, gate_weight, up_weight, packed, core
    )
    half = exchange(packed_out, x_rings)
    rows_held = cat([out_weight, down_weight])
    half, for_feed, rows_held, tables = join(half, for_feed, rows_held, tables)

    across = send(half[:, :128, 1024:], z_up)
    far = send(half, other_core)
    rows_got = [send(rows_held[:352], z_up_home), send(rows_held[352:], z_down_home)]
    feed_came = exchange(for_feed, x_rings)
    upstream_own = send(cotangent[0], regroup)
    far, across, upstream_own = join(far, across, upstream_own)
    upstream = lax.all_gather(upstream_own, AXES, axis=0, axis_index_groups=x_groups, tiled=True)
    rows_slot = jnp.where(core == z_low, rows_held, cat(rows_got))
    out_slot, down_slot = rows_slot[:128], rows_slot[128:]
    inputs = packed[:128].astype(f32)
    notes = jnp.stack([half[:, 128, 256:272], far[:, 128, 256:272]], axis=1)
    notes = jnp.where(core == 0, notes, notes[:, ::-1]).astype(f32)
    gain_query, gain_key = notes[..., :8].reshape(64), notes[..., 8:].reshape(64)
    gain = cat([gain_query, gain_query, gain_key, jnp.ones((64,), f32)])[None]

    attention_slice, first_normed, qkv, heads, scales, mixed, logs, gains = attend(
        half, far, across, gain, tables, where
    )
    gain_first, gain_second = gains[0], gains[8]
    other_half = matmul(mixed[512:], out_slot).astype(bf16)
    other_half, mixed, feed_came = join(other_half, mixed, feed_came)
    got = send(other_half, other_core)
    own_half = matmul(mixed[:512], out_slot)
    parts = scatter_sums(own_half, got)
    parts, feed_came = join(parts, feed_came)

    lower, upper = send(feed_came[:2], z_up), send(feed_came[2:], z_down)
    middle = inputs + add_up(parts)
    second_scale = rms_scale(middle)
    half = gather_half((middle * second_scale * gain_second).astype(bf16)).reshape(512, 1024)
    far = send(half, other_core)
    other_half, own_half, hidden, pre_grad, normed_all = feed(
        half, far, upstream, (feed_came, lower, upper), down_slot, where
    )
    got = send(other_half, other_core)
    result_rows = matmul(hidden, down_slot).astype(bf16)
    got, result_rows, pre_grad = join(got, result_rows, pre_grad)

    result_sum = lax.psum_scatter(
        result_rows, AXES, scatter_dimension=0, axis_index_groups=x_groups, tiled=True
    )
    parts = scatter_sums(own_half, got)
    feed_weight_grad = matmul_tn(normed_all, pre_grad)
    down_weight_grad = matmul_tn(hidden, upstream)
    feed_parts = cat(
        [
            rows_for_planes(feed_weight_grad).reshape(16, 72, 8, 128),
            block_for_planes(down_weight_grad).reshape(16, 36, 8, 128),
        ],
        1,
    )
    parts, feed_parts = join(parts, feed_parts)

    feed_parts = exchange(feed_parts, planes)
    second_grad = add_up(parts)
    middle_norm_grad, second_gain_terms = norm_back(middle, second_scale, gain_second, second_grad)
    middle_grad = upstream_own.astype(f32) + middle_norm_grad
    second_gain_grad = jnp.sum(second_gain_terms, axis=0)
    near = cat(gather_x(middle_grad.astype(bf16)))
    far = send(near, other_core)
    other_half, own_half, pre_grad, out_weight_grad, gain_terms, first_terms = attend_back(
        near,
        far,
        out_slot,
        (attention_slice, first_normed, qkv, heads, scales, mixed, logs),
        gain,
        tables,
        where,
    )
    got = send(other_half, other_core)
    attention_weight_grad = matmul_tn(first_normed, pre_grad)
    first_gain_grad = first_terms[0] / gain_first
    small = jnp.stack([gain_terms[0, :64] + gain_terms[0, 64:128], gain_terms[0, 128:192]], 1)
    small = jnp.pad(small.reshape(8, 8, 2), ((0, 0), (0, 120), (0, 0))).reshape(1024, 2)
    extra = cat([first_gain_grad[:, None], second_gain_grad[:, None], small], 1)
    extra = jnp.pad(extra, ((0, 0), (0, 124)))
    by_row = rows_for_planes(cat([attention_weight_grad, extra], 1)).reshape(4, 4, 24, 8, 128)
    by_block = block_for_planes(out_weight_grad).reshape(4, 4, 8, 8, 128)
    attention_parts = cat([by_row, by_block], 2)
    first, rest = scatter_parts(turn_back(own_half, x), turn_back(got, x))
    first, rest, attention_parts = join(first, rest, attention_parts)

    parts = send_x(*rest)
    pieces = [pick(attention_parts, (y + step) % 4, 0) for step in range(4)]
    ring = send_ring(pieces, y_up, y_down, y_far)
    first, parts, ring, feed_parts = join(first, parts, ring, feed_parts)
    rows = add_up(feed_parts).astype(bf16)
    feed_got = exchange_rows(rows[:72].reshape(8, 9, 8, 128))
    feed_mine = return_planes(feed_got, rows[72:])

    rows = pieces[0].astype(f32) + add_up(jnp.stack(ring))
    pieces = [pick(rows, (z + step) % 4, 0) for step in range(4)]
    ring = send_ring(pieces, z_up, z_down, z_far)
    rows = (pieces[0] + add_up(jnp.stack(ring))).astype(bf16)
    attention_got = exchange_x(rows[:24].reshape(8, 3, 8, 128), x)
    first_grad = first + add_up(jnp.stack(parts))
    input_norm_grad, _ = norm_back(inputs, rms_scale(inputs), gain_first, first_grad)
    input_grad = middle_grad + input_norm_grad
    result = send((middle + result_sum.astype(f32)).astype(bf16), regroup)
    input_grad = send(input_grad.astype(bf16), regroup)
    mine = gather_y(gather_z(attention_got, rows[24:], z_low))
    query_sum, key_sum, value_sum, out_sum, gain_sums = attention_grads(
        mine, send(mine, other_core), where
    )
    gate_sum, up_sum, down_sum = feed_grads(feed_mine, send(feed_mine, other_core), where)
    return (
        result[None],
        input_grad.astype(f32)[None],
        gain_sums[:, 0],
        query_sum,
        key_sum,
        value_sum,
        gain_sums[:8, 2],
        gain_sums[:8, 3],
        out_sum,
        gain_sums[:, 1],
        gate_sum,
        up_sum,
        down_sum,
    )


def solution(mesh):
    placed = (
        P("replica", "shard", None),
        P("replica", None),
        P("replica", None),
        P("shard"),
        P("shard", None),
        P("shard", None),
        P("shard", None),
        P("shard"),
        P("shard"),
        P("shard", None),
        P("shard"),
        P("shard", None),
        P("shard", None),
        P("shard", None),
        P("replica", "shard", None),
    )
    return jax.shard_map(
        on_device,
        mesh=mesh,
        in_specs=placed,
        out_specs=(
            P("replica", "shard", None),
            P("replica", "shard", None),
            P("shard"),
            P("shard", None),
            P("shard", None),
            P("shard", None),
            P("shard"),
            P("shard"),
            P("shard", None),
            P("shard"),
            P("shard", None),
            P("shard", None),
            P("shard", None),
        ),
        check_vma=False,
    )
```

```python
import jax
import jax.numpy as jnp
from jax import lax
from jax.experimental import pallas as pl
from jax.experimental.pallas import tpu as pltpu
from jax.sharding import PartitionSpec as P

HEADS = 16
KV_HEADS = 8
HD = 64
AXES = ("shard", "replica")

norm_eps = 1e-05
rope_base = 1000000.0
bf16 = jnp.bfloat16
f32 = jnp.float32


def place(x, y, z, core):
    return ((x % 4) * 2 + (z % 4) % 2) * 16 + ((y % 4) * 2 + (z % 4) // 2) * 2 + core % 2


def pairs(move, keep=lambda x, y, z, c: True):
    found = []
    for x in range(4):
        for y in range(4):
            for z in range(4):
                for c in range(2):
                    if keep(x, y, z, c):
                        found.append((place(x, y, z, c), place(*move(x, y, z, c))))
    return found


def home(x, y, z, c):
    return c == z % 2


x_up = pairs(lambda x, y, z, c: (x + 1, y, z, c))
x_down = pairs(lambda x, y, z, c: (x - 1, y, z, c))
x_far = pairs(lambda x, y, z, c: (x + 2, y, z, c))
y_up = pairs(lambda x, y, z, c: (x, y + 1, z, c))
y_down = pairs(lambda x, y, z, c: (x, y - 1, z, c))
y_far = pairs(lambda x, y, z, c: (x, y + 2, z, c))
z_up = pairs(lambda x, y, z, c: (x, y, z + 1, c))
z_down = pairs(lambda x, y, z, c: (x, y, z - 1, c))
z_far = pairs(lambda x, y, z, c: (x, y, z + 2, c))
z_up_home = pairs(lambda x, y, z, c: (x, y, z + 1, c), home)
z_down_home = pairs(lambda x, y, z, c: (x, y, z - 1, c), home)
other_core = pairs(lambda x, y, z, c: (x, y, z, 1 - c))
from_home = pairs(lambda x, y, z, c: (x, y, z, 1 - c), home)
regroup = pairs(lambda x, y, z, c: (x, y, (z // 2) * 2 + c, z % 2))


def send(values, moves):
    return lax.ppermute(values, AXES, moves)


def cat(pieces, axis=0):
    return jnp.concatenate(pieces, axis=axis)


def pick(values, index, axis):
    return lax.dynamic_index_in_dim(values, index, axis, keepdims=False)


def unroll(values, index, axis):
    doubled = cat([values, values], axis)
    return lax.dynamic_slice_in_dim(doubled, (4 - index) % 4, 4, axis)


x_rings = [
    [place(x, y, z, core) for x in range(4)] for core in range(2) for y in range(4) for z in range(4)
]
planes = [
    [place(x, y, z, core) for y in range(4) for z in range(4)] for x in range(4) for core in range(2)
]
x_groups = [
    [place(x, y, z, core) for x in range(4) for core in range(2)]
    for y in range(4)
    for z in range(4)
]


def join(*values):
    return lax.optimization_barrier(values)


def exchange(values, groups):
    return lax.all_to_all(values, AXES, 0, 0, axis_index_groups=groups)


def gather_half(block):
    return exchange(jnp.broadcast_to(block[None], (4, *block.shape)), x_rings)


def scatter_sums(own, got):
    summed = (own + got.astype(f32)).astype(bf16).reshape(4, 128, own.shape[1])
    return exchange(summed, x_rings)


def add_up(parts):
    return jnp.sum(parts.astype(f32), axis=0)


def units(values, rows, columns):
    height, width = values.shape
    return values.reshape(rows, height // rows // 8, 8, columns, width // columns // 128, 128)


def rows_for_planes(by_row):
    grid = by_row.astype(bf16).reshape(8, 4, 4, 8, by_row.shape[1] // 128, 128)
    return grid.transpose(1, 2, 0, 4, 3, 5)


def block_for_planes(by_block):
    return units(by_block.astype(bf16), 4, 4).transpose(0, 3, 1, 4, 2, 5)


def exchange_rows(by_row):
    return exchange(by_row.reshape(4, 2, *by_row.shape[1:]), x_rings)


def return_planes(got, by_block):
    both = [cat([got[:, parity].reshape(-1, 128), by_block.reshape(-1, 128)]) for parity in range(2)]
    both = jnp.stack(both)
    return exchange(
        jnp.broadcast_to(both[None], (8, *both.shape)).reshape(16, *both.shape[1:]), planes
    )


def exchange_x(by_row, x):
    own = by_row.reshape(4, 2, *by_row.shape[1:])
    near = [pick(own, (x + step) % 4, 0) for step in range(4)]
    return jnp.stack([near[0]] + send_x(*near[1:])[::-1])


def send_ring(pieces, up, down, far):
    low = [piece.astype(bf16) for piece in pieces[1:]]
    return [send(low[0], up), send(low[1], far), send(low[2], down)]


def gather_z(got, by_block, z_low):
    same = cat([pick(got, z_low, 1).reshape(-1, 128), by_block.reshape(-1, 128)])
    odd = cat([pick(got, 1 - z_low, 1).reshape(-1, 128), by_block.reshape(-1, 128)])
    return jnp.stack([same, send(odd, z_down), send(same, z_far), send(odd, z_up)])


def gather_y(block):
    return jnp.stack([block, send(block, y_down), send(block, y_far), send(block, y_up)])


def send_x(first, second, third):
    return [send(first, x_up), send(second, x_far), send(third, x_down)]


def gather_x(block):
    return [block, send(block, x_down), send(block, x_far), send(block, x_up)]


def quarter(values, step):
    return values[step * 128 : (step + 1) * 128]


def scatter_parts(own, got):
    sums = [quarter(own, step).astype(f32) + quarter(got, step).astype(f32) for step in range(4)]
    return sums[0], [part.astype(bf16) for part in sums[1:]]


def whole(count):
    return [pl.BlockSpec(memory_space=pltpu.VMEM)] * count


def spot(values):
    return jnp.stack(values).astype(jnp.int32)


def call(kernel, scalars, arrays, outs, scratch=(), limit=40, flops=0):
    size = sum(a.size * a.dtype.itemsize for a in arrays)
    return pl.pallas_call(
        kernel,
        out_shape=[jax.ShapeDtypeStruct(shape, kind) for shape, kind in outs],
        in_specs=[pl.BlockSpec(memory_space=pltpu.SMEM)] + whole(len(arrays)),
        out_specs=whole(len(outs)),
        scratch_shapes=list(scratch),
        compiler_params=pltpu.CompilerParams(vmem_limit_bytes=limit * 2**20),
        cost_estimate=pl.CostEstimate(flops=flops, bytes_accessed=size, transcendentals=0),
    )(scalars, *arrays)


def rms_scale(values):
    return lax.rsqrt(jnp.mean(values * values, axis=-1, keepdims=True) + norm_eps)


def norm_back(inputs, scale_rows, gain_vector, upstream):
    normed = inputs * scale_rows
    scaled = upstream * gain_vector
    entry_grad = scale_rows * (scaled - normed * jnp.mean(scaled * normed, axis=-1, keepdims=True))
    return (entry_grad, upstream * normed)


def matmul(left_side, right_side):
    return jnp.dot(left_side, right_side, preferred_element_type=f32)


def matmul_tn(left_side, right_side):
    return lax.dot_general(
        left_side, right_side, (((0,), (0,)), ((), ())), preferred_element_type=f32
    )


def matmul_nt(left_side, right_side):
    return lax.dot_general(
        left_side, right_side, (((1,), (1,)), ((), ())), preferred_element_type=f32
    )


def columns_kernel(spot_ref, q_ref, k_ref, v_ref, gate_ref, up_ref, packed_ref, out_ref, feed_ref):
    core = spot_ref[0]
    for at in range(4):
        out_ref[at, :, :1024] = packed_ref[...]
        out_ref[at, 128:, 1024:] = jnp.zeros((16, 256), bf16)
        out_ref[at, :128, 1024:1152] = jnp.where(
            core == 0,
            q_ref[:, at * 256 : at * 256 + 128],
            q_ref[:, at * 256 + 128 : at * 256 + 256],
        )
        for ref, low in ((k_ref, 1152), (v_ref, 1216)):
            pair = ref[:, at * 128 : at * 128 + 128]
            out_ref[at, :128, low : low + 64] = jnp.where(core == 0, pair[:, :64], pair[:, 64:])
        for row, ref in enumerate((gate_ref, up_ref)):
            some = ref[:, at * 1152 : at * 1152 + 1152]
            feed_ref[at, :, row * 576 : row * 576 + 576] = jnp.where(
                core == 0, some[:, :576], some[:, 576:]
            )


def pick_columns(query_weight, key_weight, value_weight, gate_weight, up_weight, packed, core):
    outs = [((4, 144, 1280), bf16), ((4, 128, 1152), bf16)]
    arrays = (query_weight, key_weight, value_weight, gate_weight, up_weight, packed)
    return call(columns_kernel, spot([core]), arrays, outs, limit=16)


def pack_kernel(tokens_ref, first_ref, second_ref, small_ref, out_ref):
    out_ref[:128, :] = tokens_ref[...]
    out_ref[128:, :] = jnp.zeros((16, 1024), bf16)
    for step, ref in enumerate((first_ref, second_ref, small_ref)):
        row = jnp.broadcast_to(ref[...].astype(f32), (16, 128)).astype(bf16)
        out_ref[128:, step * 128 : step * 128 + 128] = row


def pack(*arrays):
    return pl.pallas_call(
        pack_kernel, out_shape=jax.ShapeDtypeStruct((144, 1024), bf16)
    )(*arrays)


def place_tables(facts, core):
    places = facts[0, :1024].reshape(4, 2, 128)
    places = jnp.stack([pick(places, core, 1), pick(places, 1 - core, 1)]).reshape(1, 1024)
    starts = jnp.where(places >= facts[:, 1024:1025], facts[:, 1024:1025], 0)
    lane = jnp.arange(128)
    frequency = rope_base ** (-2.0 * (lane % 32).astype(f32) / HD)
    angles = (places - starts).astype(f32).reshape(1024, 1) * frequency[None, :]
    cosine, sine = jnp.cos(angles), jnp.sin(angles) * jnp.where(lane % 64 < 32, -1.0, 1.0)
    places = places.astype(f32)
    return cosine, sine, places.reshape(1024, 1), places, starts.astype(f32)


def lanes(width):
    return lax.broadcasted_iota(jnp.int32, (1, width), 1)


def swap_halves(values):
    first = lanes(256) % 64 < 32
    return jnp.where(first, pltpu.roll(values, 224, 1), pltpu.roll(values, 32, 1))


def head_means(values):
    lane = lanes(256)
    found = jnp.zeros_like(values)
    for head in range(3):
        inside = (lane >= head * 64) & (lane < head * 64 + 64)
        mean = jnp.sum(jnp.where(inside, values, 0.0), axis=1, keepdims=True) * (1.0 / 64)
        found = jnp.where(inside, mean, found)
    return found


def twice(values):
    return jnp.concatenate([values, values], axis=1)


def attend_kernel(
    spot_ref,
    half_ref,
    far_ref,
    across_ref,
    gain_ref,
    cosine_ref,
    sine_ref,
    place_ref,
    place_row_ref,
    start_row_ref,
    weight_ref,
    normed_ref,
    qkv_ref,
    head_ref,
    scale_ref,
    mixed_ref,
    logs_ref,
    gains_ref,
    turned_ref,
):
    z_low, core = spot_ref[0], spot_ref[1]
    for at in range(4):
        for piece, parity in ((half_ref[at, :128, 1024:], z_low), (across_ref[at], 1 - z_low)):
            weight_ref[pl.ds(pl.multiple_of((at * 2 + parity) * 128, 128), 128), :] = piece
        for ref, slot in ((half_ref, at * 2 + core), (far_ref, at * 2 + 1 - core)):
            to = pl.ds(pl.multiple_of(slot * 128, 128), 128)
            gains_ref[:8, to] = ref[at, 128:, :128].astype(f32)[:8]
            gains_ref[8:, to] = ref[at, 128:, 128:256].astype(f32)[:8]
    gain = gain_ref[...]
    lane = lanes(256)
    for block in range(8):
        ref = half_ref if block < 4 else far_ref
        rows = slice(block * 128, block * 128 + 128)
        inputs = ref[block % 4, :128, :1024].astype(f32)
        scale = lax.rsqrt(jnp.mean(inputs * inputs, axis=1, keepdims=True) + norm_eps)
        normed = (inputs * scale * gains_ref[0:1, :]).astype(bf16)
        normed_ref[rows, :] = normed
        pre = matmul(normed, weight_ref[...])
        scales = lax.rsqrt(head_means(pre * pre) + norm_eps)
        heads = pre * scales
        head_ref[rows, :] = heads
        scale_ref[rows, :] = scales
        gained = heads * gain
        turned = gained * twice(cosine_ref[rows, :]) + swap_halves(gained) * twice(sine_ref[rows, :])
        qkv_ref[rows, :] = jnp.where(lane < 192, turned, pre).astype(bf16)
        turned_ref[:, rows] = jnp.where(lane < 192, turned, pre)[:, 128:].T.astype(bf16)

    keys = qkv_ref[:, 128:192]
    values = turned_ref[64:, :]
    place = place_ref[...]
    for part in range(4):
        rows = slice(part * 256, part * 256 + 256)
        allowed = (place <= place_row_ref[:, rows]) & (place >= start_row_ref[:, rows])
        for head in range(2):
            columns = slice(head * 64, head * 64 + 64)
            scores = matmul_nt(keys, qkv_ref[rows, columns]) * HD**-0.5
            scores = jnp.where(allowed, scores, -1e30)
            top = jnp.max(scores, axis=0, keepdims=True)
            exponent = jnp.exp(scores - top)
            total = jnp.sum(exponent, axis=0, keepdims=True)
            probs = (exponent * (1.0 / total)).astype(bf16)
            mixed_ref[rows, columns] = matmul(values, probs).T.astype(bf16)
            logs_ref[head : head + 1, rows] = top + jnp.log(total)


def attend(half, far, across, gain, tables, where):
    outs = [
        ((1024, 256), bf16),
        ((1024, 1024), bf16),
        ((1024, 256), bf16),
        ((1024, 256), f32),
        ((1024, 256), f32),
        ((1024, 128), bf16),
        ((8, 1024), f32),
        ((16, 1024), f32),
    ]
    arrays = (half, far, across, gain, *tables)
    scratch = [pltpu.VMEM((128, 1024), bf16)]
    scalars = spot([where[4], where[3]])
    return call(attend_kernel, scalars, arrays, outs, scratch, 30, 2 * 1024**3)


def attend_back_kernel(
    spot_ref,
    near_ref,
    far_ref,
    out_weight_ref,
    weight_ref,
    normed_ref,
    qkv_ref,
    head_ref,
    scale_ref,
    mixed_ref,
    logs_ref,
    gain_ref,
    cosine_ref,
    sine_ref,
    place_ref,
    place_row_ref,
    start_row_ref,
    other_ref,
    own_ref,
    pre_grad_ref,
    out_grad_ref,
    sums_ref,
    first_ref,
    branch_ref,
    mixed_grad_ref,
    grad_ref,
    turned_ref,
):
    x = spot_ref[0]
    for step in range(4):
        to = pl.multiple_of(((x + step) % 4) * 128, 128)
        piece = slice(step * 128, step * 128 + 128)
        branch_ref[pl.ds(to, 128), :] = near_ref[piece, :]
        branch_ref[pl.ds(to + 512, 128), :] = far_ref[piece, :]
    mixed_grad_ref[...] = matmul_nt(branch_ref[...], out_weight_ref[...]).astype(bf16)
    keys, values = qkv_ref[:, 128:192], qkv_ref[:, 192:]
    turned_ref[...] = qkv_ref[:, 128:].astype(f32).T.astype(bf16)
    keys_turned = turned_ref[:64, :]
    place = place_ref[...]
    grad_ref[:, 128:] = jnp.zeros((1024, 128), f32)
    for part in range(4):
        rows = slice(part * 256, part * 256 + 256)
        allowed = (place <= place_row_ref[:, rows]) & (place >= start_row_ref[:, rows])
        for head in range(2):
            columns = slice(head * 64, head * 64 + 64)
            queries, upstream = qkv_ref[rows, columns], mixed_grad_ref[rows, columns]
            scores = matmul_nt(keys, queries) * HD**-0.5
            probs = jnp.where(allowed, jnp.exp(scores - logs_ref[head : head + 1, rows]), 0.0)
            prob_grad = matmul_nt(values, upstream)
            inner = jnp.sum(probs * prob_grad, axis=0, keepdims=True)
            score_grad = (probs * (prob_grad - inner)).astype(bf16)
            grad_ref[:, 128:192] += matmul(score_grad, queries) * HD**-0.5
            grad_ref[:, 192:] += matmul(probs.astype(bf16), upstream)
            grad_ref[rows, columns] = matmul(keys_turned, score_grad).T * HD**-0.5
    out_grad_ref[...] = matmul(mixed_ref[...].astype(f32).T.astype(bf16), branch_ref[...])
    gain = gain_ref[...]
    lane = lanes(256)
    sums_ref[...] = jnp.zeros((8, 256), f32)
    first_ref[...] = jnp.zeros((8, 1024), f32)
    for block in (4, 5, 6, 7, 0, 1, 2, 3):
        rows = slice(block * 128, block * 128 + 128)
        grads = grad_ref[rows, :]
        back = grads * twice(cosine_ref[rows, :]) - swap_halves(grads) * twice(sine_ref[rows, :])
        heads = head_ref[rows, :]
        sums_ref[0:1, :] += jnp.sum(back * heads, axis=0, keepdims=True)
        gained = back * gain
        entry = scale_ref[rows, :] * (gained - heads * head_means(gained * heads))
        pre_grad = jnp.where(lane < 192, entry, grads).astype(bf16)
        pre_grad_ref[rows, :] = pre_grad
        partial = matmul_nt(pre_grad, weight_ref[...])
        first_ref[0:1, :] += jnp.sum(partial * normed_ref[rows, :].astype(f32), axis=0, keepdims=True)
        to = pl.ds(pl.multiple_of(((block % 4 + 4 - x) % 4) * 128, 128), 128)
        if block < 4:
            own_ref[to, :] = partial.astype(bf16)
        else:
            other_ref[to, :] = partial.astype(bf16)


def attend_back(near, far, out_slot, kept, gain, tables, where):
    outs = [
        ((512, 1024), bf16),
        ((512, 1024), bf16),
        ((1024, 256), bf16),
        ((128, 1024), f32),
        ((8, 256), f32),
        ((8, 1024), f32),
    ]
    arrays = (near, far, out_slot, *kept, gain, *tables)
    scratch = [
        pltpu.VMEM((1024, 1024), bf16),
        pltpu.VMEM((1024, 128), bf16),
        pltpu.VMEM((1024, 256), f32),
        pltpu.VMEM((128, 1024), bf16),
    ]
    return call(attend_back_kernel, spot([where[0]]), arrays, outs, scratch, 36, 4 * 1024**3)


def feed_kernel(
    spot_ref,
    half_ref,
    far_ref,
    upstream_ref,
    came_ref,
    lower_ref,
    upper_ref,
    down_ref,
    other_ref,
    own_ref,
    hidden_ref,
    pre_grad_ref,
    normed_ref,
    weight_ref,
):
    z_low, core, x = spot_ref[0], spot_ref[1], spot_ref[2]
    for at in range(4):
        across = lower_ref if at < 2 else upper_ref
        for piece, parity in ((came_ref[at], z_low), (across[at % 2], 1 - z_low)):
            weight_ref[pl.ds(pl.multiple_of((at * 2 + parity) * 128, 128), 128), :] = piece
    normed_ref[:512] = half_ref[...]
    normed_ref[512:] = far_ref[...]

    def rows_of(part, slot_core):
        slots = [
            pl.ds(pl.multiple_of((part * 4 + step * 2 + slot_core) * 128, 128), 128)
            for step in range(2)
        ]
        return slots, jnp.concatenate([upstream_ref[slot, :] for slot in slots], axis=0)

    def work(start, part, slot_core):
        rows = pl.ds(pl.multiple_of(start, 256), 256)
        slots, upstream = rows_of(part, slot_core)
        pre = matmul(normed_ref[rows, :], weight_ref[...])
        gate, up = pre[:, :576], pre[:, 576:]
        hidden_grad = matmul_nt(upstream, down_ref[...]).astype(bf16).astype(f32)
        sigmoid = 1.0 / (1.0 + jnp.exp(-gate))
        silu = gate * sigmoid
        hidden = (silu * up).astype(bf16)
        for step, slot in enumerate(slots):
            hidden_ref[slot, :] = hidden[step * 128 : step * 128 + 128]
        gate_grad = hidden_grad * up * sigmoid * (1.0 + gate * (1.0 - sigmoid))
        pre_grad = jnp.concatenate([gate_grad, hidden_grad * silu], axis=1).astype(bf16)
        pre_grad_ref[rows, :] = pre_grad
        return matmul_nt(pre_grad, weight_ref[...])

    def keep(ref, part, partial):
        for step in range(2):
            to = pl.multiple_of(((part * 2 + step + 4 - x) % 4) * 128, 128)
            ref[pl.ds(to, 128), :] = partial[step * 128 : step * 128 + 128].astype(bf16)

    def other_half(part, carry):
        keep(other_ref, part, work(part * 256 + 512, part, 1 - core))
        return carry

    def own_half(part, carry):
        keep(own_ref, part, work(part * 256, part, core))
        return carry

    lax.fori_loop(0, 2, other_half, 0)
    lax.fori_loop(0, 2, own_half, 0)


def feed(half, far, upstream, weights, down_slot, where):
    arrays = (half, far, upstream, *weights, down_slot)
    outs = [
        ((512, 1024), bf16),
        ((512, 1024), bf16),
        ((1024, 576), bf16),
        ((1024, 1152), bf16),
        ((1024, 1024), bf16),
    ]
    scratch = [pltpu.VMEM((1024, 1152), bf16)]
    scalars = spot([where[4], where[3], where[0]])
    return call(feed_kernel, scalars, arrays, outs, scratch, 34, 6 * 1024**3)


def feed_grads_kernel(spot_ref, mine_ref, other_ref, gate_ref, up_ref, down_ref):
    core, z_low = spot_ref[0], spot_ref[1]
    home = core == z_low
    for at in range(16):
        mine = mine_ref[at].astype(f32)
        other = other_ref[at].astype(f32)
        first = jnp.where(core == 0, mine[:288], other[:288])
        second = jnp.where(core == 0, other[:288], mine[:288])
        block = jnp.where(home, mine[288:], other[288:])
        rows = slice(at * 8, at * 8 + 8)
        for x in range(4):
            wide = [
                jnp.concatenate(
                    [one[(x * 9 + i) * 8 : (x * 9 + i) * 8 + 8] for i in range(9)], axis=1
                )
                for one in (first, second)
            ]
            columns = slice(x * 1152, x * 1152 + 1152)
            gate_ref[rows, columns] = jnp.concatenate([one[:, :576] for one in wide], axis=1)
            up_ref[rows, columns] = jnp.concatenate([one[:, 576:] for one in wide], axis=1)
        for i in range(18):
            for j in range(2):
                piece = block[(i * 2 + j) * 8 : (i * 2 + j) * 8 + 8]
                low, left = at // 4 * 144 + i * 8, at % 4 * 256 + j * 128
                down_ref[low : low + 8, left : left + 128] = piece


def feed_grads(mine, other, where):
    outs = [((128, 4608), f32), ((128, 4608), f32), ((576, 1024), f32)]
    return call(feed_grads_kernel, spot(where[3:]), (mine, other), outs, (), 40)


def attention_grads_kernel(spot_ref, mine_ref, other_ref, q_ref, k_ref, v_ref, out_ref, extra_ref):
    core, z_low, x, y, z = (spot_ref[i] for i in range(5))
    home = core == z_low
    for y_step in range(4):
        for z_step in range(4):
            mine = mine_ref[y_step, z_step].astype(f32)
            other = other_ref[y_step, z_step].astype(f32)
            first = jnp.where(core == 0, mine[:96], other[:96])
            second = jnp.where(core == 0, other[:96], mine[:96])
            block = jnp.where(home, mine[96:], other[96:])
            y_at, z_at = (y + y_step) % 4, (z + z_step) % 4
            rows = pl.ds(pl.multiple_of((y_at * 4 + z_at) * 8, 8), 8)
            extra = jnp.zeros((8, 128), f32)
            for step in range(4):
                slot, low = (x + step) % 4, step * 24
                to = pl.multiple_of(slot * 256, 128)
                q_ref[rows, pl.ds(to, 128)] = first[low : low + 8]
                q_ref[rows, pl.ds(to + 128, 128)] = second[low : low + 8]
                one, two = first[low + 8 : low + 16], second[low + 8 : low + 16]
                columns = pl.ds(pl.multiple_of(slot * 128, 128), 128)
                k_ref[rows, columns] = jnp.concatenate([one[:, :64], two[:, :64]], axis=1)
                v_ref[rows, columns] = jnp.concatenate([one[:, 64:], two[:, 64:]], axis=1)
                extra = extra + first[low + 16 : low + 24] + second[low + 16 : low + 24]
            extra_ref[rows, :] = extra
            for i in range(4):
                for j in range(2):
                    to = pl.ds(pl.multiple_of(y_at * 32 + i * 8, 8), 8)
                    columns = pl.ds(pl.multiple_of(z_at * 256 + j * 128, 128), 128)
                    out_ref[to, columns] = block[(i * 2 + j) * 8 : (i * 2 + j) * 8 + 8]


def attention_grads(mine, other, where):
    outs = [
        ((128, 1024), f32),
        ((128, 512), f32),
        ((128, 512), f32),
        ((128, 1024), f32),
        ((128, 128), f32),
    ]
    x, y, z, core, z_low = where
    return call(
        attention_grads_kernel, spot([core, z_low, x, y, z]), (mine, other), outs, (), 24
    )


def on_device(
    tokens,
    seq_lengths,
    token_places,
    attention_gain,
    query_weight,
    key_weight,
    value_weight,
    query_gain,
    key_gain,
    out_weight,
    feedforward_gain,
    gate_weight,
    up_weight,
    down_weight,
    cotangent,
):
    shard, replica = lax.axis_index("shard"), lax.axis_index("replica")
    x, z_low = shard // 2, shard % 2
    y, z, core = replica // 4, (replica // 2) % 2 * 2 + z_low, replica % 2
    where = (x, y, z, core, z_low)

    facts = cat([token_places, jnp.broadcast_to(seq_lengths[:, :1], (1, 128))], 1)
    small = cat([query_gain, key_gain, jnp.zeros((112,), bf16)])
    packed = pack(tokens[0], attention_gain[None], feedforward_gain[None], small[None])
    packed = send(packed, regroup)
    facts = jnp.where(core == z_low, facts, send(facts, other_core))
    packed_out, for_feed = pick_columns(
        query_weight, key_weight, value_weight, gate_weight, up_weight, packed, core
    )
    packed_out, for_feed, facts, rows_mine, cotangent = join(
        packed_out, for_feed, facts, (out_weight, down_weight), cotangent
    )
    half = exchange(packed_out, x_rings)
    tables = place_tables(facts, core)
    upstream_own = send(cotangent[0], regroup)
    rows_got = [send(rows_mine[0], z_up_home), send(rows_mine[1], z_down_home)]
    out_slot, down_slot = (
        jnp.where(core == z_low, mine, got) for mine, got in zip(rows_mine, rows_got)
    )
    half, for_feed, upstream_own, out_slot, down_slot, tables = join(
        half, for_feed, upstream_own, out_slot, down_slot, tables
    )

    upstream = lax.all_gather(upstream_own, AXES, axis=0, axis_index_groups=x_groups, tiled=True)
    far = send(half, other_core)
    across = send(half[:, :128, 1024:], z_up)
    feed_came = exchange(for_feed, x_rings)
    far, across = join(far, across)
    inputs = packed[:128].astype(f32)
    notes = jnp.stack([half[:, 128, 256:272], far[:, 128, 256:272]], axis=1)
    notes = jnp.where(core == 0, notes, notes[:, ::-1]).astype(f32)
    gain_query, gain_key = notes[..., :8].reshape(64), notes[..., 8:].reshape(64)
    gain = cat([gain_query, gain_query, gain_key, jnp.ones((64,), f32)])[None]

    attention_slice, first_normed, qkv, heads, scales, mixed, logs, gains = attend(
        half, far, across, gain, tables, where
    )
    gain_first, gain_second = gains[0], gains[8]
    other_half = matmul(mixed[512:], out_slot).astype(bf16)
    other_half, mixed, feed_came = join(other_half, mixed, feed_came)
    got = send(other_half, other_core)
    own_half = matmul(mixed[:512], out_slot)
    lower, upper = send(feed_came[:2], z_up), send(feed_came[2:], z_down)
    parts = scatter_sums(own_half, got)
    parts, lower, upper = join(parts, lower, upper)

    middle = inputs + add_up(parts)
    second_scale = rms_scale(middle)
    half = gather_half((middle * second_scale * gain_second).astype(bf16)).reshape(512, 1024)
    far = send(half, other_core)
    other_half, own_half, hidden, pre_grad, normed_all = feed(
        half, far, upstream, (feed_came, lower, upper), down_slot, where
    )
    first, rest = scatter_parts(own_half, send(other_half, other_core))
    first, rest, pre_grad, hidden, normed_all = join(first, rest, pre_grad, hidden, normed_all)

    parts = send_x(*rest)
    feed_weight_grad = matmul_tn(normed_all, pre_grad)
    down_weight_grad = matmul_tn(hidden, upstream)
    feed_parts = cat(
        [
            rows_for_planes(feed_weight_grad).reshape(16, 72, 8, 128),
            block_for_planes(down_weight_grad).reshape(16, 36, 8, 128),
        ],
        1,
    )
    first, parts, feed_parts, hidden = join(first, parts, feed_parts, hidden)
    feed_parts = exchange(feed_parts, planes)
    second_grad = first + add_up(jnp.stack(parts))
    middle_norm_grad, second_gain_terms = norm_back(middle, second_scale, gain_second, second_grad)
    middle_grad = upstream_own.astype(f32) + middle_norm_grad
    second_gain_grad = jnp.sum(second_gain_terms, axis=0)
    near = gather_x(middle_grad.astype(bf16))
    result_rows = matmul(hidden, down_slot).astype(bf16)
    near, result_rows = join(near, result_rows)
    near = cat(near)
    far = send(near, other_core)
    result_sum = lax.psum_scatter(
        result_rows, AXES, scatter_dimension=0, axis_index_groups=x_groups, tiled=True
    )
    other_half, own_half, pre_grad, out_weight_grad, gain_terms, first_terms = attend_back(
        near,
        far,
        out_slot,
        (attention_slice, first_normed, qkv, heads, scales, mixed, logs),
        gain,
        tables,
        where,
    )
    first, rest = scatter_parts(own_half, send(other_half, other_core))
    first, rest, pre_grad, feed_parts = join(first, rest, pre_grad, feed_parts)

    parts = send_x(*rest)
    feed_rows = add_up(feed_parts).astype(bf16)
    feed_got = exchange_rows(feed_rows[:72].reshape(8, 9, 8, 128))
    attention_weight_grad = matmul_tn(first_normed, pre_grad)
    first_gain_grad = first_terms[0] / gain_first
    small = jnp.stack([gain_terms[0, :64] + gain_terms[0, 64:128], gain_terms[0, 128:192]], 1)
    small = jnp.pad(small.reshape(8, 8, 2), ((0, 0), (0, 120), (0, 0))).reshape(1024, 2)
    extra = cat([first_gain_grad[:, None], second_gain_grad[:, None], small], 1)
    extra = jnp.pad(extra, ((0, 0), (0, 124)))
    by_row = rows_for_planes(cat([attention_weight_grad, extra], 1)).reshape(4, 4, 24, 8, 128)
    by_block = block_for_planes(out_weight_grad).reshape(4, 4, 8, 8, 128)
    attention_parts = cat([by_row, by_block], 2)
    first, parts, attention_parts, feed_got, feed_rows = join(
        first, parts, attention_parts, feed_got, feed_rows
    )
    pieces = [pick(attention_parts, (y + step) % 4, 0) for step in range(4)]
    ring = send_ring(pieces, y_up, y_down, y_far)
    first_grad = first + add_up(jnp.stack(parts))
    input_norm_grad, _ = norm_back(inputs, rms_scale(inputs), gain_first, first_grad)
    input_grad = (middle_grad + input_norm_grad).astype(bf16)
    ring, feed_got, feed_rows, input_grad = join(ring, feed_got, feed_rows, input_grad)

    rows = pieces[0].astype(f32) + add_up(jnp.stack(ring))
    pieces = [pick(rows, (z + step) % 4, 0) for step in range(4)]
    ring = send_ring(pieces, z_up, z_down, z_far)
    feed_mine = return_planes(feed_got, feed_rows[72:])
    result = (middle + result_sum.astype(f32)).astype(bf16)
    ring, input_grad, result = join(ring, input_grad, result)

    rows = (pieces[0] + add_up(jnp.stack(ring))).astype(bf16)
    attention_got = exchange_x(rows[:24].reshape(8, 3, 8, 128), x)
    result = send(result, regroup)
    attention_got, result = join(attention_got, result)
    input_grad = send(input_grad, regroup)
    block, input_grad, feed_mine = join(
        gather_z(attention_got, rows[24:], z_low), input_grad, feed_mine
    )
    mine = gather_y(block)
    query_sum, key_sum, value_sum, out_sum, gain_sums = attention_grads(
        mine, send(mine, other_core), where
    )
    gate_sum, up_sum, down_sum = feed_grads(feed_mine, send(feed_mine, other_core), where)
    return (
        result[None],
        input_grad.astype(f32)[None],
        gain_sums[:, 0],
        query_sum,
        key_sum,
        value_sum,
        gain_sums[:8, 2],
        gain_sums[:8, 3],
        out_sum,
        gain_sums[:, 1],
        gate_sum,
        up_sum,
        down_sum,
    )


def solution(mesh):
    placed = (
        P("replica", "shard", None),
        P("replica", None),
        P("replica", None),
        P("shard"),
        P("shard", None),
        P("shard", None),
        P("shard", None),
        P("shard"),
        P("shard"),
        P("shard", None),
        P("shard"),
        P("shard", None),
        P("shard", None),
        P("shard", None),
        P("replica", "shard", None),
    )
    return jax.shard_map(
        on_device,
        mesh=mesh,
        in_specs=placed,
        out_specs=(
            P("replica", "shard", None),
            P("replica", "shard", None),
            P("shard"),
            P("shard", None),
            P("shard", None),
            P("shard", None),
            P("shard"),
            P("shard"),
            P("shard", None),
            P("shard"),
            P("shard", None),
            P("shard", None),
            P("shard", None),
        ),
        check_vma=False,
    )
```

```python
import jax
import jax.numpy as jnp
from jax import lax
from jax.experimental import pallas as pl
from jax.experimental.pallas import tpu as pltpu
from jax.sharding import PartitionSpec as P

HEADS = 16
KV_HEADS = 8
HD = 64
AXES = ("shard", "replica")

norm_eps = 1e-05
rope_base = 1000000.0
bf16 = jnp.bfloat16
f32 = jnp.float32


def place(x, y, z, core):
    return ((x % 4) * 2 + (z % 4) % 2) * 16 + ((y % 4) * 2 + (z % 4) // 2) * 2 + core % 2


def pairs(move, keep=lambda x, y, z, c: True):
    found = []
    for x in range(4):
        for y in range(4):
            for z in range(4):
                for c in range(2):
                    if keep(x, y, z, c):
                        found.append((place(x, y, z, c), place(*move(x, y, z, c))))
    return found


def home(x, y, z, c):
    return c == z % 2


x_up = pairs(lambda x, y, z, c: (x + 1, y, z, c))
x_down = pairs(lambda x, y, z, c: (x - 1, y, z, c))
x_far = pairs(lambda x, y, z, c: (x + 2, y, z, c))
y_up = pairs(lambda x, y, z, c: (x, y + 1, z, c))
y_down = pairs(lambda x, y, z, c: (x, y - 1, z, c))
y_far = pairs(lambda x, y, z, c: (x, y + 2, z, c))
z_up = pairs(lambda x, y, z, c: (x, y, z + 1, c))
z_down = pairs(lambda x, y, z, c: (x, y, z - 1, c))
z_far = pairs(lambda x, y, z, c: (x, y, z + 2, c))
z_up_home = pairs(lambda x, y, z, c: (x, y, z + 1, c), home)
z_down_home = pairs(lambda x, y, z, c: (x, y, z - 1, c), home)
other_core = pairs(lambda x, y, z, c: (x, y, z, 1 - c))
from_home = pairs(lambda x, y, z, c: (x, y, z, 1 - c), home)
regroup = pairs(lambda x, y, z, c: (x, y, (z // 2) * 2 + c, z % 2))


def send(values, moves):
    return lax.ppermute(values, AXES, moves)


def cat(pieces, axis=0):
    return jnp.concatenate(pieces, axis=axis)


def pick(values, index, axis):
    return lax.dynamic_index_in_dim(values, index, axis, keepdims=False)


def unroll(values, index, axis):
    doubled = cat([values, values], axis)
    return lax.dynamic_slice_in_dim(doubled, (4 - index) % 4, 4, axis)


x_rings = [
    [place(x, y, z, core) for x in range(4)] for core in range(2) for y in range(4) for z in range(4)
]
planes = [
    [place(x, y, z, core) for y in range(4) for z in range(4)] for x in range(4) for core in range(2)
]
x_groups = [
    [place(x, y, z, core) for x in range(4) for core in range(2)]
    for y in range(4)
    for z in range(4)
]


def join(*values):
    return lax.optimization_barrier(values)


def exchange(values, groups):
    return lax.all_to_all(values, AXES, 0, 0, axis_index_groups=groups)


def gather_half(block):
    return exchange(jnp.broadcast_to(block[None], (4, *block.shape)), x_rings)


def scatter_sums(own, got):
    summed = (own + got.astype(f32)).astype(bf16).reshape(4, 128, own.shape[1])
    return exchange(summed, x_rings)


def add_up(parts):
    return jnp.sum(parts.astype(f32), axis=0)


def units(values, rows, columns):
    height, width = values.shape
    return values.reshape(rows, height // rows // 8, 8, columns, width // columns // 128, 128)


def rows_for_planes(by_row):
    grid = by_row.astype(bf16).reshape(8, 4, 4, 8, by_row.shape[1] // 128, 128)
    return grid.transpose(1, 2, 0, 4, 3, 5)


def block_for_planes(by_block):
    return units(by_block.astype(bf16), 4, 4).transpose(0, 3, 1, 4, 2, 5)


def exchange_rows(by_row):
    return exchange(by_row.reshape(4, 2, *by_row.shape[1:]), x_rings)


def return_planes(got, by_block):
    both = [cat([got[:, parity].reshape(-1, 128), by_block.reshape(-1, 128)]) for parity in range(2)]
    both = jnp.stack(both)
    return exchange(
        jnp.broadcast_to(both[None], (8, *both.shape)).reshape(16, *both.shape[1:]), planes
    )


def exchange_x(by_row, x):
    own = by_row.reshape(4, 2, *by_row.shape[1:])
    near = [pick(own, (x + step) % 4, 0) for step in range(4)]
    return jnp.stack([near[0]] + send_x(*near[1:])[::-1])


def send_ring(pieces, up, down, far):
    low = [piece.astype(bf16) for piece in pieces[1:]]
    return [send(low[0], up), send(low[1], far), send(low[2], down)]


def gather_z(got, by_block, z_low):
    same = cat([pick(got, z_low, 1).reshape(-1, 128), by_block.reshape(-1, 128)])
    odd = cat([pick(got, 1 - z_low, 1).reshape(-1, 128), by_block.reshape(-1, 128)])
    return jnp.stack([same, send(odd, z_down), send(same, z_far), send(odd, z_up)])


def gather_y(block):
    return jnp.stack([block, send(block, y_down), send(block, y_far), send(block, y_up)])


def send_x(first, second, third):
    return [send(first, x_up), send(second, x_far), send(third, x_down)]


def gather_x(block):
    return [block, send(block, x_down), send(block, x_far), send(block, x_up)]


def quarter(values, step):
    return values[step * 128 : (step + 1) * 128]


def scatter_parts(own, got):
    sums = [quarter(own, step).astype(f32) + quarter(got, step).astype(f32) for step in range(4)]
    return sums[0], [part.astype(bf16) for part in sums[1:]]


def whole(shape):
    return pl.BlockSpec(shape, lambda i: (0,) * len(shape), pipeline_mode=pl.Buffered(1))


def spot(values):
    return jnp.stack(values).astype(jnp.int32)


def call(kernel, scalars, arrays, outs, scratch=(), limit=40, flops=0):
    size = sum(a.size * a.dtype.itemsize for a in arrays)
    return pl.pallas_call(
        kernel,
        out_shape=[jax.ShapeDtypeStruct(shape, kind) for shape, kind in outs],
        grid=(1,),
        in_specs=[pl.BlockSpec(memory_space=pltpu.SMEM)] + [whole(a.shape) for a in arrays],
        out_specs=[whole(shape) for shape, _ in outs],
        scratch_shapes=list(scratch),
        compiler_params=pltpu.CompilerParams(vmem_limit_bytes=limit * 2**20),
        cost_estimate=pl.CostEstimate(flops=flops, bytes_accessed=size, transcendentals=0),
    )(scalars, *arrays)


def rms_scale(values):
    return lax.rsqrt(jnp.mean(values * values, axis=-1, keepdims=True) + norm_eps)


def norm_back(inputs, scale_rows, gain_vector, upstream):
    normed = inputs * scale_rows
    scaled = upstream * gain_vector
    entry_grad = scale_rows * (scaled - normed * jnp.mean(scaled * normed, axis=-1, keepdims=True))
    return (entry_grad, upstream * normed)


def matmul(left_side, right_side):
    return jnp.dot(left_side, right_side, preferred_element_type=f32)


def matmul_tn(left_side, right_side):
    return lax.dot_general(
        left_side, right_side, (((0,), (0,)), ((), ())), preferred_element_type=f32
    )


def matmul_nt(left_side, right_side):
    return lax.dot_general(
        left_side, right_side, (((1,), (1,)), ((), ())), preferred_element_type=f32
    )


def columns_kernel(spot_ref, q_ref, k_ref, v_ref, gate_ref, up_ref, packed_ref, out_ref, feed_ref):
    core = spot_ref[0]
    for at in range(4):
        out_ref[at, :, :1024] = packed_ref[...]
        out_ref[at, 128:, 1024:] = jnp.zeros((16, 256), bf16)
        out_ref[at, :128, 1024:1152] = jnp.where(
            core == 0,
            q_ref[:, at * 256 : at * 256 + 128],
            q_ref[:, at * 256 + 128 : at * 256 + 256],
        )
        for ref, low in ((k_ref, 1152), (v_ref, 1216)):
            pair = ref[:, at * 128 : at * 128 + 128]
            out_ref[at, :128, low : low + 64] = jnp.where(core == 0, pair[:, :64], pair[:, 64:])
        for row, ref in enumerate((gate_ref, up_ref)):
            some = ref[:, at * 1152 : at * 1152 + 1152]
            feed_ref[at, :, row * 576 : row * 576 + 576] = jnp.where(
                core == 0, some[:, :576], some[:, 576:]
            )


def pick_columns(query_weight, key_weight, value_weight, gate_weight, up_weight, packed, core):
    outs = [((4, 144, 1280), bf16), ((4, 128, 1152), bf16)]
    arrays = (query_weight, key_weight, value_weight, gate_weight, up_weight, packed)
    return call(columns_kernel, spot([core]), arrays, outs, limit=58)


def pack_kernel(tokens_ref, first_ref, second_ref, small_ref, out_ref):
    out_ref[:128, :] = tokens_ref[...]
    out_ref[128:, :] = jnp.zeros((16, 1024), bf16)
    for step, ref in enumerate((first_ref, second_ref, small_ref)):
        row = jnp.broadcast_to(ref[...].astype(f32), (16, 128)).astype(bf16)
        out_ref[128:, step * 128 : step * 128 + 128] = row


def pack(*arrays):
    return pl.pallas_call(
        pack_kernel, out_shape=jax.ShapeDtypeStruct((144, 1024), bf16)
    )(*arrays)


def place_tables(facts, core):
    places = facts[0, :1024].reshape(4, 2, 128)
    places = jnp.stack([pick(places, core, 1), pick(places, 1 - core, 1)]).reshape(1, 1024)
    starts = jnp.where(places >= facts[:, 1024:1025], facts[:, 1024:1025], 0)
    lane = jnp.arange(128)
    frequency = rope_base ** (-2.0 * (lane % 32).astype(f32) / HD)
    angles = (places - starts).astype(f32).reshape(1024, 1) * frequency[None, :]
    cosine, sine = jnp.cos(angles), jnp.sin(angles) * jnp.where(lane % 64 < 32, -1.0, 1.0)
    places = places.astype(f32)
    return cosine, sine, places.reshape(1024, 1), places, starts.astype(f32)


def lanes(width):
    return lax.broadcasted_iota(jnp.int32, (1, width), 1)


def swap_halves(values):
    first = lanes(256) % 64 < 32
    return jnp.where(first, pltpu.roll(values, 224, 1), pltpu.roll(values, 32, 1))


def head_means(values):
    lane = lanes(256)
    found = jnp.zeros_like(values)
    for head in range(3):
        inside = (lane >= head * 64) & (lane < head * 64 + 64)
        mean = jnp.sum(jnp.where(inside, values, 0.0), axis=1, keepdims=True) * (1.0 / 64)
        found = jnp.where(inside, mean, found)
    return found


def twice(values):
    return jnp.concatenate([values, values], axis=1)


def attend_kernel(
    spot_ref,
    half_ref,
    far_ref,
    across_ref,
    gain_ref,
    cosine_ref,
    sine_ref,
    place_ref,
    place_row_ref,
    start_row_ref,
    weight_ref,
    normed_ref,
    qkv_ref,
    head_ref,
    scale_ref,
    mixed_ref,
    logs_ref,
    gains_ref,
    turned_ref,
):
    z_low, core = spot_ref[0], spot_ref[1]
    for at in range(4):
        for piece, parity in ((half_ref[at, :128, 1024:], z_low), (across_ref[at], 1 - z_low)):
            weight_ref[pl.ds(pl.multiple_of((at * 2 + parity) * 128, 128), 128), :] = piece
        for ref, slot in ((half_ref, at * 2 + core), (far_ref, at * 2 + 1 - core)):
            to = pl.ds(pl.multiple_of(slot * 128, 128), 128)
            gains_ref[:8, to] = ref[at, 128:, :128].astype(f32)[:8]
            gains_ref[8:, to] = ref[at, 128:, 128:256].astype(f32)[:8]
    gain = gain_ref[...]
    lane = lanes(256)
    for block in range(8):
        ref = half_ref if block < 4 else far_ref
        rows = slice(block * 128, block * 128 + 128)
        inputs = ref[block % 4, :128, :1024].astype(f32)
        scale = lax.rsqrt(jnp.mean(inputs * inputs, axis=1, keepdims=True) + norm_eps)
        normed = (inputs * scale * gains_ref[0:1, :]).astype(bf16)
        normed_ref[rows, :] = normed
        pre = matmul(normed, weight_ref[...])
        scales = lax.rsqrt(head_means(pre * pre) + norm_eps)
        heads = pre * scales
        head_ref[rows, :] = heads
        scale_ref[rows, :] = scales
        gained = heads * gain
        turned = gained * twice(cosine_ref[rows, :]) + swap_halves(gained) * twice(sine_ref[rows, :])
        qkv_ref[rows, :] = jnp.where(lane < 192, turned, pre).astype(bf16)
        turned_ref[:, rows] = jnp.where(lane < 192, turned, pre)[:, 128:].T.astype(bf16)

    keys = qkv_ref[:, 128:192]
    values = turned_ref[64:, :]
    place = place_ref[...]
    for part in range(4):
        rows = slice(part * 256, part * 256 + 256)
        allowed = (place <= place_row_ref[:, rows]) & (place >= start_row_ref[:, rows])
        for head in range(2):
            columns = slice(head * 64, head * 64 + 64)
            scores = matmul_nt(keys, qkv_ref[rows, columns]) * HD**-0.5
            scores = jnp.where(allowed, scores, -1e30)
            top = jnp.max(scores, axis=0, keepdims=True)
            exponent = jnp.exp(scores - top)
            total = jnp.sum(exponent, axis=0, keepdims=True)
            probs = (exponent * (1.0 / total)).astype(bf16)
            mixed_ref[rows, columns] = matmul(values, probs).T.astype(bf16)
            logs_ref[head : head + 1, rows] = top + jnp.log(total)


def attend(half, far, across, gain, tables, where):
    outs = [
        ((1024, 256), bf16),
        ((1024, 1024), bf16),
        ((1024, 256), bf16),
        ((1024, 256), f32),
        ((1024, 256), f32),
        ((1024, 128), bf16),
        ((8, 1024), f32),
        ((16, 1024), f32),
    ]
    arrays = (half, far, across, gain, *tables)
    scratch = [pltpu.VMEM((128, 1024), bf16)]
    scalars = spot([where[4], where[3]])
    return call(attend_kernel, scalars, arrays, outs, scratch, 58, 2 * 1024**3)


def attend_back_kernel(
    spot_ref,
    near_ref,
    far_ref,
    out_weight_ref,
    weight_ref,
    normed_ref,
    qkv_ref,
    head_ref,
    scale_ref,
    mixed_ref,
    logs_ref,
    gain_ref,
    cosine_ref,
    sine_ref,
    place_ref,
    place_row_ref,
    start_row_ref,
    other_ref,
    own_ref,
    pre_grad_ref,
    out_grad_ref,
    sums_ref,
    first_ref,
    branch_ref,
    mixed_grad_ref,
    grad_ref,
    turned_ref,
):
    x = spot_ref[0]
    for step in range(4):
        to = pl.multiple_of(((x + step) % 4) * 128, 128)
        piece = slice(step * 128, step * 128 + 128)
        branch_ref[pl.ds(to, 128), :] = near_ref[piece, :]
        branch_ref[pl.ds(to + 512, 128), :] = far_ref[piece, :]
    mixed_grad_ref[...] = matmul_nt(branch_ref[...], out_weight_ref[...]).astype(bf16)
    keys, values = qkv_ref[:, 128:192], qkv_ref[:, 192:]
    turned_ref[...] = qkv_ref[:, 128:].astype(f32).T.astype(bf16)
    keys_turned = turned_ref[:64, :]
    place = place_ref[...]
    grad_ref[:, 128:] = jnp.zeros((1024, 128), f32)
    for part in range(4):
        rows = slice(part * 256, part * 256 + 256)
        allowed = (place <= place_row_ref[:, rows]) & (place >= start_row_ref[:, rows])
        for head in range(2):
            columns = slice(head * 64, head * 64 + 64)
            queries, upstream = qkv_ref[rows, columns], mixed_grad_ref[rows, columns]
            scores = matmul_nt(keys, queries) * HD**-0.5
            probs = jnp.where(allowed, jnp.exp(scores - logs_ref[head : head + 1, rows]), 0.0)
            prob_grad = matmul_nt(values, upstream)
            inner = jnp.sum(probs * prob_grad, axis=0, keepdims=True)
            score_grad = (probs * (prob_grad - inner)).astype(bf16)
            grad_ref[:, 128:192] += matmul(score_grad, queries) * HD**-0.5
            grad_ref[:, 192:] += matmul(probs.astype(bf16), upstream)
            grad_ref[rows, columns] = matmul(keys_turned, score_grad).T * HD**-0.5
    out_grad_ref[...] = matmul(mixed_ref[...].astype(f32).T.astype(bf16), branch_ref[...])
    gain = gain_ref[...]
    lane = lanes(256)
    sums_ref[...] = jnp.zeros((8, 256), f32)
    first_ref[...] = jnp.zeros((8, 1024), f32)
    for block in (4, 5, 6, 7, 0, 1, 2, 3):
        rows = slice(block * 128, block * 128 + 128)
        grads = grad_ref[rows, :]
        back = grads * twice(cosine_ref[rows, :]) - swap_halves(grads) * twice(sine_ref[rows, :])
        heads = head_ref[rows, :]
        sums_ref[0:1, :] += jnp.sum(back * heads, axis=0, keepdims=True)
        gained = back * gain
        entry = scale_ref[rows, :] * (gained - heads * head_means(gained * heads))
        pre_grad = jnp.where(lane < 192, entry, grads).astype(bf16)
        pre_grad_ref[rows, :] = pre_grad
        partial = matmul_nt(pre_grad, weight_ref[...])
        first_ref[0:1, :] += jnp.sum(partial * normed_ref[rows, :].astype(f32), axis=0, keepdims=True)
        to = pl.ds(pl.multiple_of(((block % 4 + 4 - x) % 4) * 128, 128), 128)
        if block < 4:
            own_ref[to, :] = partial.astype(bf16)
        else:
            other_ref[to, :] = partial.astype(bf16)


def attend_back(near, far, out_slot, kept, gain, tables, where):
    outs = [
        ((512, 1024), bf16),
        ((512, 1024), bf16),
        ((1024, 256), bf16),
        ((128, 1024), f32),
        ((8, 256), f32),
        ((8, 1024), f32),
    ]
    arrays = (near, far, out_slot, *kept, gain, *tables)
    scratch = [
        pltpu.VMEM((1024, 1024), bf16),
        pltpu.VMEM((1024, 128), bf16),
        pltpu.VMEM((1024, 256), f32),
        pltpu.VMEM((128, 1024), bf16),
    ]
    return call(attend_back_kernel, spot([where[0]]), arrays, outs, scratch, 58, 4 * 1024**3)


def feed_kernel(
    spot_ref,
    half_ref,
    far_ref,
    upstream_ref,
    upstream_far_ref,
    came_ref,
    lower_ref,
    upper_ref,
    down_ref,
    other_ref,
    own_ref,
    hidden_ref,
    pre_grad_ref,
    normed_ref,
    turned_ref,
    weight_ref,
):
    z_low, core, x = spot_ref[0], spot_ref[1], spot_ref[2]
    for at in range(4):
        across = lower_ref if at < 2 else upper_ref
        for piece, parity in ((came_ref[at], z_low), (across[at % 2], 1 - z_low)):
            weight_ref[pl.ds(pl.multiple_of((at * 2 + parity) * 128, 128), 128), :] = piece
    normed_ref[:512] = half_ref[...]
    normed_ref[512:] = far_ref[...]

    def work(start, part, slot_core, from_ref):
        rows = pl.ds(pl.multiple_of(start, 256), 256)
        upstream = from_ref[pl.ds(pl.multiple_of(part * 256, 256), 256), :]
        slots = [
            pl.ds(pl.multiple_of((part * 4 + step * 2 + slot_core) * 128, 128), 128)
            for step in range(2)
        ]
        pre = matmul(normed_ref[rows, :], weight_ref[...])
        gate, up = pre[:, :576], pre[:, 576:]
        hidden_grad = matmul_nt(upstream, down_ref[...]).astype(bf16).astype(f32)
        sigmoid = 1.0 / (1.0 + jnp.exp(-gate))
        silu = gate * sigmoid
        hidden = (silu * up).astype(bf16)
        for step, slot in enumerate(slots):
            hidden_ref[slot, :] = hidden[step * 128 : step * 128 + 128]
            turned_ref[slot, :] = upstream[step * 128 : step * 128 + 128]
        gate_grad = hidden_grad * up * sigmoid * (1.0 + gate * (1.0 - sigmoid))
        pre_grad = jnp.concatenate([gate_grad, hidden_grad * silu], axis=1).astype(bf16)
        pre_grad_ref[rows, :] = pre_grad
        return matmul_nt(pre_grad, weight_ref[...])

    def keep(ref, part, partial):
        for step in range(2):
            to = pl.multiple_of(((part * 2 + step + 4 - x) % 4) * 128, 128)
            ref[pl.ds(to, 128), :] = partial[step * 128 : step * 128 + 128].astype(bf16)

    def other_half(part, carry):
        keep(other_ref, part, work(part * 256 + 512, part, 1 - core, upstream_far_ref))
        return carry

    def own_half(part, carry):
        keep(own_ref, part, work(part * 256, part, core, upstream_ref))
        return carry

    lax.fori_loop(0, 2, other_half, 0)
    lax.fori_loop(0, 2, own_half, 0)


def feed(half, far, upstream, upstream_far, weights, down_slot, where):
    arrays = (half, far, upstream, upstream_far, *weights, down_slot)
    outs = [
        ((512, 1024), bf16),
        ((512, 1024), bf16),
        ((1024, 576), bf16),
        ((1024, 1152), bf16),
        ((1024, 1024), bf16),
        ((1024, 1024), bf16),
    ]
    scratch = [pltpu.VMEM((1024, 1152), bf16)]
    scalars = spot([where[4], where[3], where[0]])
    return call(feed_kernel, scalars, arrays, outs, scratch, 58, 6 * 1024**3)


def feed_grads_kernel(spot_ref, mine_ref, other_ref, gate_ref, up_ref, down_ref):
    core, z_low = spot_ref[0], spot_ref[1]
    home = core == z_low
    for at in range(16):
        mine = mine_ref[at].astype(f32)
        other = other_ref[at].astype(f32)
        first = jnp.where(core == 0, mine[:288], other[:288])
        second = jnp.where(core == 0, other[:288], mine[:288])
        block = jnp.where(home, mine[288:], other[288:])
        rows = slice(at * 8, at * 8 + 8)
        for x in range(4):
            wide = [
                jnp.concatenate(
                    [one[(x * 9 + i) * 8 : (x * 9 + i) * 8 + 8] for i in range(9)], axis=1
                )
                for one in (first, second)
            ]
            columns = slice(x * 1152, x * 1152 + 1152)
            gate_ref[rows, columns] = jnp.concatenate([one[:, :576] for one in wide], axis=1)
            up_ref[rows, columns] = jnp.concatenate([one[:, 576:] for one in wide], axis=1)
        for i in range(18):
            for j in range(2):
                piece = block[(i * 2 + j) * 8 : (i * 2 + j) * 8 + 8]
                low, left = at // 4 * 144 + i * 8, at % 4 * 256 + j * 128
                down_ref[low : low + 8, left : left + 128] = piece


def feed_grads(mine, other, where):
    outs = [((128, 4608), f32), ((128, 4608), f32), ((576, 1024), f32)]
    return call(feed_grads_kernel, spot(where[3:]), (mine, other), outs, (), 40)


def attention_grads_kernel(spot_ref, mine_ref, other_ref, q_ref, k_ref, v_ref, out_ref, extra_ref):
    core, z_low, x, y, z = (spot_ref[i] for i in range(5))
    home = core == z_low
    for y_step in range(4):
        for z_step in range(4):
            mine = mine_ref[y_step, z_step].astype(f32)
            other = other_ref[y_step, z_step].astype(f32)
            first = jnp.where(core == 0, mine[:96], other[:96])
            second = jnp.where(core == 0, other[:96], mine[:96])
            block = jnp.where(home, mine[96:], other[96:])
            y_at, z_at = (y + y_step) % 4, (z + z_step) % 4
            rows = pl.ds(pl.multiple_of((y_at * 4 + z_at) * 8, 8), 8)
            extra = jnp.zeros((8, 128), f32)
            for step in range(4):
                slot, low = (x + step) % 4, step * 24
                to = pl.multiple_of(slot * 256, 128)
                q_ref[rows, pl.ds(to, 128)] = first[low : low + 8]
                q_ref[rows, pl.ds(to + 128, 128)] = second[low : low + 8]
                one, two = first[low + 8 : low + 16], second[low + 8 : low + 16]
                columns = pl.ds(pl.multiple_of(slot * 128, 128), 128)
                k_ref[rows, columns] = jnp.concatenate([one[:, :64], two[:, :64]], axis=1)
                v_ref[rows, columns] = jnp.concatenate([one[:, 64:], two[:, 64:]], axis=1)
                extra = extra + first[low + 16 : low + 24] + second[low + 16 : low + 24]
            extra_ref[rows, :] = extra
            for i in range(4):
                for j in range(2):
                    to = pl.ds(pl.multiple_of(y_at * 32 + i * 8, 8), 8)
                    columns = pl.ds(pl.multiple_of(z_at * 256 + j * 128, 128), 128)
                    out_ref[to, columns] = block[(i * 2 + j) * 8 : (i * 2 + j) * 8 + 8]


def attention_grads(mine, other, where):
    outs = [
        ((128, 1024), f32),
        ((128, 512), f32),
        ((128, 512), f32),
        ((128, 1024), f32),
        ((128, 128), f32),
    ]
    x, y, z, core, z_low = where
    return call(
        attention_grads_kernel, spot([core, z_low, x, y, z]), (mine, other), outs, (), 24
    )


def on_device(
    tokens,
    seq_lengths,
    token_places,
    attention_gain,
    query_weight,
    key_weight,
    value_weight,
    query_gain,
    key_gain,
    out_weight,
    feedforward_gain,
    gate_weight,
    up_weight,
    down_weight,
    cotangent,
):
    shard, replica = lax.axis_index("shard"), lax.axis_index("replica")
    x, z_low = shard // 2, shard % 2
    y, z, core = replica // 4, (replica // 2) % 2 * 2 + z_low, replica % 2
    where = (x, y, z, core, z_low)

    facts = cat([token_places, jnp.broadcast_to(seq_lengths[:, :1], (1, 128))], 1)
    small = cat([query_gain, key_gain, jnp.zeros((112,), bf16)])
    packed = pack(tokens[0], attention_gain[None], feedforward_gain[None], small[None])
    packed = send(packed, regroup)
    facts = jnp.where(core == z_low, facts, send(facts, other_core))
    packed_out, for_feed = pick_columns(
        query_weight, key_weight, value_weight, gate_weight, up_weight, packed, core
    )
    packed_out, for_feed, facts, out_mine, cotangent = join(
        packed_out, for_feed, facts, out_weight, cotangent
    )
    half = exchange(packed_out, x_rings)
    tables = place_tables(facts, core)
    upstream_own = send(cotangent[0], regroup)
    out_slot = jnp.where(core == z_low, out_mine, send(out_mine, z_up_home))
    half, for_feed, upstream_own, out_slot, tables, down_mine = join(
        half, for_feed, upstream_own, out_slot, tables, down_weight
    )

    upstream = lax.all_gather(upstream_own, AXES, axis=0, axis_index_groups=x_rings, tiled=True)
    down_got = send(down_mine, z_down_home)
    far = send(half, other_core)
    across = send(half[:, :128, 1024:], z_up)
    feed_came = exchange(for_feed, x_rings)
    far, across = join(far, across)
    inputs = packed[:128].astype(f32)
    notes = jnp.stack([half[:, 128, 256:272], far[:, 128, 256:272]], axis=1)
    notes = jnp.where(core == 0, notes, notes[:, ::-1]).astype(f32)
    gain_query, gain_key = notes[..., :8].reshape(64), notes[..., 8:].reshape(64)
    gain = cat([gain_query, gain_query, gain_key, jnp.ones((64,), f32)])[None]

    attention_slice, first_normed, qkv, heads, scales, mixed, logs, gains = attend(
        half, far, across, gain, tables, where
    )
    gain_first, gain_second = gains[0], gains[8]
    other_half = matmul(mixed[512:], out_slot).astype(bf16)
    other_half, mixed, feed_came, down_got = join(other_half, mixed, feed_came, down_got)
    down_slot = jnp.where(core == z_low, down_mine, down_got)
    got = send(other_half, other_core)
    own_half = matmul(mixed[:512], out_slot)
    lower, upper = send(feed_came[:2], z_up), send(feed_came[2:], z_down)
    parts = scatter_sums(own_half, got)
    parts, lower, upper, down_slot = join(parts, lower, upper, down_slot)

    middle = inputs + add_up(parts)
    second_scale = rms_scale(middle)
    half = gather_half((middle * second_scale * gain_second).astype(bf16)).reshape(512, 1024)
    half, upstream = join(half, upstream)
    far = send(half, other_core)
    upstream_far = send(upstream, other_core)
    other_half, own_half, hidden, pre_grad, normed_all, upstream = feed(
        half, far, upstream, upstream_far, (feed_came, lower, upper), down_slot, where
    )
    first, rest = scatter_parts(own_half, send(other_half, other_core))
    first, rest, pre_grad, hidden, normed_all = join(first, rest, pre_grad, hidden, normed_all)

    parts = send_x(*rest)
    feed_weight_grad = matmul_tn(normed_all, pre_grad)
    down_weight_grad = matmul_tn(hidden, upstream)
    feed_parts = cat(
        [
            rows_for_planes(feed_weight_grad).reshape(16, 72, 8, 128),
            block_for_planes(down_weight_grad).reshape(16, 36, 8, 128),
        ],
        1,
    )
    first, parts, feed_parts, hidden = join(first, parts, feed_parts, hidden)
    feed_parts = exchange(feed_parts, planes)
    second_grad = first + add_up(jnp.stack(parts))
    middle_norm_grad, second_gain_terms = norm_back(middle, second_scale, gain_second, second_grad)
    middle_grad = upstream_own.astype(f32) + middle_norm_grad
    second_gain_grad = jnp.sum(second_gain_terms, axis=0)
    near = gather_x(middle_grad.astype(bf16))
    result_rows = matmul(hidden, down_slot).astype(bf16)
    near, result_rows = join(near, result_rows)
    near = cat(near)
    far = send(near, other_core)
    result_sum = lax.psum_scatter(
        result_rows, AXES, scatter_dimension=0, axis_index_groups=x_groups, tiled=True
    )
    other_half, own_half, pre_grad, out_weight_grad, gain_terms, first_terms = attend_back(
        near,
        far,
        out_slot,
        (attention_slice, first_normed, qkv, heads, scales, mixed, logs),
        gain,
        tables,
        where,
    )
    first, rest = scatter_parts(own_half, send(other_half, other_core))
    first, rest, pre_grad = join(first, rest, pre_grad)

    parts = send_x(*rest)
    attention_weight_grad = matmul_tn(first_normed, pre_grad)
    first_gain_grad = first_terms[0] / gain_first
    small = jnp.stack([gain_terms[0, :64] + gain_terms[0, 64:128], gain_terms[0, 128:192]], 1)
    small = jnp.pad(small.reshape(8, 8, 2), ((0, 0), (0, 120), (0, 0))).reshape(1024, 2)
    extra = cat([first_gain_grad[:, None], second_gain_grad[:, None], small], 1)
    extra = jnp.pad(extra, ((0, 0), (0, 124)))
    by_row = rows_for_planes(cat([attention_weight_grad, extra], 1)).reshape(4, 4, 24, 8, 128)
    by_block = block_for_planes(out_weight_grad).reshape(4, 4, 8, 8, 128)
    attention_parts = cat([by_row, by_block], 2)
    pieces = [pick(attention_parts, (y + step) % 4, 0) for step in range(4)]
    ring = send_ring(pieces, y_up, y_down, y_far)
    feed_rows = add_up(feed_parts).astype(bf16)
    feed_got = exchange_rows(feed_rows[:72].reshape(8, 9, 8, 128))
    first, parts, ring, feed_got, feed_rows = join(first, parts, ring, feed_got, feed_rows)

    first_grad = first + add_up(jnp.stack(parts))
    input_norm_grad, _ = norm_back(inputs, rms_scale(inputs), gain_first, first_grad)
    input_grad = (middle_grad + input_norm_grad).astype(bf16)
    rows = pieces[0].astype(f32) + add_up(jnp.stack(ring))
    pieces = [pick(rows, (z + step) % 4, 0) for step in range(4)]
    ring = send_ring(pieces, z_up, z_down, z_far)
    feed_mine = return_planes(feed_got, feed_rows[72:])
    result = (middle + result_sum.astype(f32)).astype(bf16)
    ring, input_grad, result = join(ring, input_grad, result)

    rows = (pieces[0] + add_up(jnp.stack(ring))).astype(bf16)
    attention_got = exchange_x(rows[:24].reshape(8, 3, 8, 128), x)
    result = send(result, regroup)
    attention_got, result = join(attention_got, result)
    input_grad = send(input_grad, regroup)
    block, input_grad, feed_mine = join(
        gather_z(attention_got, rows[24:], z_low), input_grad, feed_mine
    )
    mine = gather_y(block)
    query_sum, key_sum, value_sum, out_sum, gain_sums = attention_grads(
        mine, send(mine, other_core), where
    )
    gate_sum, up_sum, down_sum = feed_grads(feed_mine, send(feed_mine, other_core), where)
    return (
        result[None],
        input_grad.astype(f32)[None],
        gain_sums[:, 0],
        query_sum,
        key_sum,
        value_sum,
        gain_sums[:8, 2],
        gain_sums[:8, 3],
        out_sum,
        gain_sums[:, 1],
        gate_sum,
        up_sum,
        down_sum,
    )


def solution(mesh):
    placed = (
        P("replica", "shard", None),
        P("replica", None),
        P("replica", None),
        P("shard"),
        P("shard", None),
        P("shard", None),
        P("shard", None),
        P("shard"),
        P("shard"),
        P("shard", None),
        P("shard"),
        P("shard", None),
        P("shard", None),
        P("shard", None),
        P("replica", "shard", None),
    )
    return jax.shard_map(
        on_device,
        mesh=mesh,
        in_specs=placed,
        out_specs=(
            P("replica", "shard", None),
            P("replica", "shard", None),
            P("shard"),
            P("shard", None),
            P("shard", None),
            P("shard", None),
            P("shard"),
            P("shard"),
            P("shard", None),
            P("shard"),
            P("shard", None),
            P("shard", None),
            P("shard", None),
        ),
        check_vma=False,
    )
```

```python
import jax
import jax.numpy as jnp
from jax import lax
from jax.experimental import pallas as pl
from jax.experimental.pallas import tpu as pltpu
from jax.sharding import PartitionSpec as P

HEADS = 16
KV_HEADS = 8
HD = 64
AXES = ("shard", "replica")

norm_eps = 1e-05
rope_base = 1000000.0
bf16 = jnp.bfloat16
f32 = jnp.float32


def place(x, y, z, core):
    return ((x % 4) * 2 + (z % 4) % 2) * 16 + ((y % 4) * 2 + (z % 4) // 2) * 2 + core % 2


def pairs(move, keep=lambda x, y, z, c: True):
    found = []
    for x in range(4):
        for y in range(4):
            for z in range(4):
                for c in range(2):
                    if keep(x, y, z, c):
                        found.append((place(x, y, z, c), place(*move(x, y, z, c))))
    return found


def home(x, y, z, c):
    return c == z % 2


x_up = pairs(lambda x, y, z, c: (x + 1, y, z, c))
x_down = pairs(lambda x, y, z, c: (x - 1, y, z, c))
x_far = pairs(lambda x, y, z, c: (x + 2, y, z, c))
y_up = pairs(lambda x, y, z, c: (x, y + 1, z, c))
y_down = pairs(lambda x, y, z, c: (x, y - 1, z, c))
y_far = pairs(lambda x, y, z, c: (x, y + 2, z, c))
z_up = pairs(lambda x, y, z, c: (x, y, z + 1, c))
z_down = pairs(lambda x, y, z, c: (x, y, z - 1, c))
z_far = pairs(lambda x, y, z, c: (x, y, z + 2, c))
z_up_home = pairs(lambda x, y, z, c: (x, y, z + 1, c), home)
z_down_home = pairs(lambda x, y, z, c: (x, y, z - 1, c), home)
other_core = pairs(lambda x, y, z, c: (x, y, z, 1 - c))
from_home = pairs(lambda x, y, z, c: (x, y, z, 1 - c), home)
regroup = pairs(lambda x, y, z, c: (x, y, (z // 2) * 2 + c, z % 2))


def send(values, moves):
    return lax.ppermute(values, AXES, moves)


def cat(pieces, axis=0):
    return jnp.concatenate(pieces, axis=axis)


def pick(values, index, axis):
    return lax.dynamic_index_in_dim(values, index, axis, keepdims=False)


def unroll(values, index, axis):
    doubled = cat([values, values], axis)
    return lax.dynamic_slice_in_dim(doubled, (4 - index) % 4, 4, axis)


x_rings = [
    [place(x, y, z, core) for x in range(4)] for core in range(2) for y in range(4) for z in range(4)
]
planes = [
    [place(x, y, z, core) for y in range(4) for z in range(4)] for x in range(4) for core in range(2)
]
x_groups = [
    [place(x, y, z, core) for x in range(4) for core in range(2)]
    for y in range(4)
    for z in range(4)
]


def join(*values):
    return lax.optimization_barrier(values)


def exchange(values, groups):
    return lax.all_to_all(values, AXES, 0, 0, axis_index_groups=groups)


def gather_half(block):
    return exchange(jnp.broadcast_to(block[None], (4, *block.shape)), x_rings)


def scatter_sums(own, got):
    summed = (own + got.astype(f32)).astype(bf16).reshape(4, 128, own.shape[1])
    return exchange(summed, x_rings)


def add_up(parts):
    return jnp.sum(parts.astype(f32), axis=0)


def units(values, rows, columns):
    height, width = values.shape
    return values.reshape(rows, height // rows // 8, 8, columns, width // columns // 128, 128)


def rows_for_planes(by_row):
    grid = by_row.astype(bf16).reshape(8, 4, 4, 8, by_row.shape[1] // 128, 128)
    return grid.transpose(1, 2, 0, 4, 3, 5)


def block_for_planes(by_block):
    return units(by_block.astype(bf16), 4, 4).transpose(0, 3, 1, 4, 2, 5)


def exchange_rows(by_row):
    return exchange(by_row.reshape(4, 2, *by_row.shape[1:]), x_rings)


def return_planes(got, by_block):
    both = [cat([got[:, parity].reshape(-1, 128), by_block.reshape(-1, 128)]) for parity in range(2)]
    both = jnp.stack(both)
    return exchange(
        jnp.broadcast_to(both[None], (8, *both.shape)).reshape(16, *both.shape[1:]), planes
    )


def exchange_x(by_row, x):
    own = by_row.reshape(4, 2, *by_row.shape[1:])
    near = [pick(own, (x + step) % 4, 0) for step in range(4)]
    return jnp.stack([near[0]] + send_x(*near[1:])[::-1])


def send_ring(pieces, up, down, far):
    low = [piece.astype(bf16) for piece in pieces[1:]]
    return [send(low[0], up), send(low[1], far), send(low[2], down)]


def gather_z(got, by_block, z_low):
    same = cat([pick(got, z_low, 1).reshape(-1, 128), by_block.reshape(-1, 128)])
    odd = cat([pick(got, 1 - z_low, 1).reshape(-1, 128), by_block.reshape(-1, 128)])
    return jnp.stack([same, send(odd, z_down), send(same, z_far), send(odd, z_up)])


def gather_y(block):
    return jnp.stack([block, send(block, y_down), send(block, y_far), send(block, y_up)])


def send_x(first, second, third):
    return [send(first, x_up), send(second, x_far), send(third, x_down)]


def gather_x(block):
    return [block, send(block, x_down), send(block, x_far), send(block, x_up)]


def quarter(values, step):
    return values[step * 128 : (step + 1) * 128]


def scatter_parts(own, got):
    sums = [quarter(own, step).astype(f32) + quarter(got, step).astype(f32) for step in range(4)]
    return sums[0], [part.astype(bf16) for part in sums[1:]]


def whole(shape):
    return pl.BlockSpec(shape, lambda i: (0,) * len(shape), pipeline_mode=pl.Buffered(1))


def spot(values):
    return jnp.stack(values).astype(jnp.int32)


def call(kernel, scalars, arrays, outs, scratch=(), limit=40, flops=0):
    size = sum(a.size * a.dtype.itemsize for a in arrays)
    return pl.pallas_call(
        kernel,
        out_shape=[jax.ShapeDtypeStruct(shape, kind) for shape, kind in outs],
        grid=(1,),
        in_specs=[pl.BlockSpec(memory_space=pltpu.SMEM)] + [whole(a.shape) for a in arrays],
        out_specs=[whole(shape) for shape, _ in outs],
        scratch_shapes=list(scratch),
        compiler_params=pltpu.CompilerParams(vmem_limit_bytes=limit * 2**20),
        cost_estimate=pl.CostEstimate(flops=flops, bytes_accessed=size, transcendentals=0),
    )(scalars, *arrays)


def rms_scale(values):
    return lax.rsqrt(jnp.mean(values * values, axis=-1, keepdims=True) + norm_eps)


def norm_back(inputs, scale_rows, gain_vector, upstream):
    normed = inputs * scale_rows
    scaled = upstream * gain_vector
    entry_grad = scale_rows * (scaled - normed * jnp.mean(scaled * normed, axis=-1, keepdims=True))
    return (entry_grad, upstream * normed)


def matmul(left_side, right_side):
    return jnp.dot(left_side, right_side, preferred_element_type=f32)


def matmul_tn(left_side, right_side):
    return lax.dot_general(
        left_side, right_side, (((0,), (0,)), ((), ())), preferred_element_type=f32
    )


def matmul_nt(left_side, right_side):
    return lax.dot_general(
        left_side, right_side, (((1,), (1,)), ((), ())), preferred_element_type=f32
    )


def columns_kernel(spot_ref, q_ref, k_ref, v_ref, gate_ref, up_ref, packed_ref, out_ref, feed_ref):
    core = spot_ref[0]
    for at in range(4):
        out_ref[at, :, :1024] = packed_ref[...]
        out_ref[at, 128:, 1024:] = jnp.zeros((16, 256), bf16)
        out_ref[at, :128, 1024:1152] = jnp.where(
            core == 0,
            q_ref[:, at * 256 : at * 256 + 128],
            q_ref[:, at * 256 + 128 : at * 256 + 256],
        )
        for ref, low in ((k_ref, 1152), (v_ref, 1216)):
            pair = ref[:, at * 128 : at * 128 + 128]
            out_ref[at, :128, low : low + 64] = jnp.where(core == 0, pair[:, :64], pair[:, 64:])
        for row, ref in enumerate((gate_ref, up_ref)):
            some = ref[:, at * 1152 : at * 1152 + 1152]
            feed_ref[at, :, row * 576 : row * 576 + 576] = jnp.where(
                core == 0, some[:, :576], some[:, 576:]
            )


def pick_columns(query_weight, key_weight, value_weight, gate_weight, up_weight, packed, core):
    outs = [((4, 144, 1280), bf16), ((4, 128, 1152), bf16)]
    arrays = (query_weight, key_weight, value_weight, gate_weight, up_weight, packed)
    return call(columns_kernel, spot([core]), arrays, outs, limit=58)


def pack_kernel(tokens_ref, first_ref, second_ref, small_ref, out_ref):
    out_ref[:128, :] = tokens_ref[...]
    out_ref[128:, :] = jnp.zeros((16, 1024), bf16)
    for step, ref in enumerate((first_ref, second_ref, small_ref)):
        row = jnp.broadcast_to(ref[...].astype(f32), (16, 128)).astype(bf16)
        out_ref[128:, step * 128 : step * 128 + 128] = row


def pack(*arrays):
    return pl.pallas_call(
        pack_kernel, out_shape=jax.ShapeDtypeStruct((144, 1024), bf16)
    )(*arrays)


def place_tables(facts, core):
    places = facts[0, :1024].reshape(4, 2, 128)
    places = jnp.stack([pick(places, core, 1), pick(places, 1 - core, 1)]).reshape(1, 1024)
    starts = jnp.where(places >= facts[:, 1024:1025], facts[:, 1024:1025], 0)
    lane = jnp.arange(128)
    frequency = rope_base ** (-2.0 * (lane % 32).astype(f32) / HD)
    angles = (places - starts).astype(f32).reshape(1024, 1) * frequency[None, :]
    cosine, sine = jnp.cos(angles), jnp.sin(angles) * jnp.where(lane % 64 < 32, -1.0, 1.0)
    places = places.astype(f32)
    return cosine, sine, places.reshape(1024, 1), places, starts.astype(f32)


def lanes(width):
    return lax.broadcasted_iota(jnp.int32, (1, width), 1)


def swap_halves(values):
    first = lanes(256) % 64 < 32
    return jnp.where(first, pltpu.roll(values, 224, 1), pltpu.roll(values, 32, 1))


def head_means(values):
    lane = lanes(256)
    found = jnp.zeros_like(values)
    for head in range(3):
        inside = (lane >= head * 64) & (lane < head * 64 + 64)
        mean = jnp.sum(jnp.where(inside, values, 0.0), axis=1, keepdims=True) * (1.0 / 64)
        found = jnp.where(inside, mean, found)
    return found


def twice(values):
    return jnp.concatenate([values, values], axis=1)


def attend_kernel(
    spot_ref,
    half_ref,
    far_ref,
    across_ref,
    gain_ref,
    cosine_ref,
    sine_ref,
    place_ref,
    place_row_ref,
    start_row_ref,
    weight_ref,
    normed_ref,
    qkv_ref,
    head_ref,
    scale_ref,
    mixed_ref,
    logs_ref,
    gains_ref,
    turned_ref,
):
    z_low, core = spot_ref[0], spot_ref[1]
    for at in range(4):
        for piece, parity in ((half_ref[at, :128, 1024:], z_low), (across_ref[at], 1 - z_low)):
            weight_ref[pl.ds(pl.multiple_of((at * 2 + parity) * 128, 128), 128), :] = piece
        for ref, slot in ((half_ref, at * 2 + core), (far_ref, at * 2 + 1 - core)):
            to = pl.ds(pl.multiple_of(slot * 128, 128), 128)
            gains_ref[:8, to] = ref[at, 128:, :128].astype(f32)[:8]
            gains_ref[8:, to] = ref[at, 128:, 128:256].astype(f32)[:8]
    gain = gain_ref[...]
    lane = lanes(256)
    for block in range(8):
        ref = half_ref if block < 4 else far_ref
        rows = slice(block * 128, block * 128 + 128)
        inputs = ref[block % 4, :128, :1024].astype(f32)
        scale = lax.rsqrt(jnp.mean(inputs * inputs, axis=1, keepdims=True) + norm_eps)
        normed = (inputs * scale * gains_ref[0:1, :]).astype(bf16)
        normed_ref[rows, :] = normed
        pre = matmul(normed, weight_ref[...])
        scales = lax.rsqrt(head_means(pre * pre) + norm_eps)
        heads = pre * scales
        head_ref[rows, :] = heads
        scale_ref[rows, :] = scales
        gained = heads * gain
        turned = gained * twice(cosine_ref[rows, :]) + swap_halves(gained) * twice(sine_ref[rows, :])
        qkv_ref[rows, :] = jnp.where(lane < 192, turned, pre).astype(bf16)
        turned_ref[:, rows] = jnp.where(lane < 192, turned, pre)[:, 128:].T.astype(bf16)

    keys = qkv_ref[:, 128:192]
    values = turned_ref[64:, :]
    place = place_ref[...]
    for part in range(4):
        rows = slice(part * 256, part * 256 + 256)
        allowed = (place <= place_row_ref[:, rows]) & (place >= start_row_ref[:, rows])
        for head in range(2):
            columns = slice(head * 64, head * 64 + 64)
            scores = matmul_nt(keys, qkv_ref[rows, columns]) * HD**-0.5
            scores = jnp.where(allowed, scores, -1e30)
            top = jnp.max(scores, axis=0, keepdims=True)
            exponent = jnp.exp(scores - top)
            total = jnp.sum(exponent, axis=0, keepdims=True)
            probs = (exponent * (1.0 / total)).astype(bf16)
            mixed_ref[rows, columns] = matmul(values, probs).T.astype(bf16)
            logs_ref[head : head + 1, rows] = top + jnp.log(total)


def attend(half, far, across, gain, tables, where):
    outs = [
        ((1024, 256), bf16),
        ((1024, 1024), bf16),
        ((1024, 256), bf16),
        ((1024, 256), f32),
        ((1024, 256), f32),
        ((1024, 128), bf16),
        ((8, 1024), f32),
        ((16, 1024), f32),
    ]
    arrays = (half, far, across, gain, *tables)
    scratch = [pltpu.VMEM((128, 1024), bf16)]
    scalars = spot([where[4], where[3]])
    return call(attend_kernel, scalars, arrays, outs, scratch, 58, 2 * 1024**3)


def attend_back_kernel(
    spot_ref,
    near_ref,
    far_ref,
    out_weight_ref,
    weight_ref,
    normed_ref,
    qkv_ref,
    head_ref,
    scale_ref,
    mixed_ref,
    logs_ref,
    gain_ref,
    cosine_ref,
    sine_ref,
    place_ref,
    place_row_ref,
    start_row_ref,
    gains_ref,
    second_ref,
    other_ref,
    own_ref,
    parts_ref,
    sums_ref,
    first_ref,
    out_grad_ref,
    pre_grad_ref,
    branch_ref,
    mixed_grad_ref,
    grad_ref,
    turned_ref,
):
    x = spot_ref[0]
    for step in range(4):
        to = pl.multiple_of(((x + step) % 4) * 128, 128)
        piece = slice(step * 128, step * 128 + 128)
        branch_ref[pl.ds(to, 128), :] = near_ref[piece, :]
        branch_ref[pl.ds(to + 512, 128), :] = far_ref[piece, :]
    mixed_grad_ref[...] = matmul_nt(branch_ref[...], out_weight_ref[...]).astype(bf16)
    keys, values = qkv_ref[:, 128:192], qkv_ref[:, 192:]
    turned_ref[...] = qkv_ref[:, 128:].astype(f32).T.astype(bf16)
    keys_turned = turned_ref[:64, :]
    place = place_ref[...]
    grad_ref[:, 128:] = jnp.zeros((1024, 128), f32)
    for part in range(4):
        rows = slice(part * 256, part * 256 + 256)
        allowed = (place <= place_row_ref[:, rows]) & (place >= start_row_ref[:, rows])
        for head in range(2):
            columns = slice(head * 64, head * 64 + 64)
            queries, upstream = qkv_ref[rows, columns], mixed_grad_ref[rows, columns]
            scores = matmul_nt(keys, queries) * HD**-0.5
            probs = jnp.where(allowed, jnp.exp(scores - logs_ref[head : head + 1, rows]), 0.0)
            prob_grad = matmul_nt(values, upstream)
            inner = jnp.sum(probs * prob_grad, axis=0, keepdims=True)
            score_grad = (probs * (prob_grad - inner)).astype(bf16)
            grad_ref[:, 128:192] += matmul(score_grad, queries) * HD**-0.5
            grad_ref[:, 192:] += matmul(probs.astype(bf16), upstream)
            grad_ref[rows, columns] = matmul(keys_turned, score_grad).T * HD**-0.5
    out_grad_ref[...] = matmul(mixed_ref[...].astype(f32).T.astype(bf16), branch_ref[...])
    gain = gain_ref[...]
    lane = lanes(256)
    sums_ref[...] = jnp.zeros((8, 256), f32)
    first_ref[...] = jnp.zeros((8, 1024), f32)
    for block in (4, 5, 6, 7, 0, 1, 2, 3):
        rows = slice(block * 128, block * 128 + 128)
        grads = grad_ref[rows, :]
        back = grads * twice(cosine_ref[rows, :]) - swap_halves(grads) * twice(sine_ref[rows, :])
        heads = head_ref[rows, :]
        sums_ref[0:1, :] += jnp.sum(back * heads, axis=0, keepdims=True)
        gained = back * gain
        entry = scale_ref[rows, :] * (gained - heads * head_means(gained * heads))
        pre_grad = jnp.where(lane < 192, entry, grads).astype(bf16)
        pre_grad_ref[rows, :] = pre_grad
        partial = matmul_nt(pre_grad, weight_ref[...])
        first_ref[0:1, :] += jnp.sum(partial * normed_ref[rows, :].astype(f32), axis=0, keepdims=True)
        to = pl.ds(pl.multiple_of(((block % 4 + 4 - x) % 4) * 128, 128), 128)
        if block < 4:
            own_ref[to, :] = partial.astype(bf16)
        else:
            other_ref[to, :] = partial.astype(bf16)

    turned_grad = matmul(pre_grad_ref[...].astype(f32).T.astype(bf16), normed_ref[...])
    column = lax.broadcasted_iota(jnp.int32, (256, 1024), 1)
    entry = lax.broadcasted_iota(jnp.int32, (256, 1024), 0)
    wanted = jnp.where(column % 128 < 8, column // 128 * 8 + column % 128, -1)
    row = lax.broadcasted_iota(jnp.int32, (128, 1024), 0)
    rows = []
    for inside in (entry < 128, (entry >= 128) & (entry < 192)):
        chosen = jnp.where(inside & (entry % 64 == wanted), 1.0, 0.0).astype(bf16)
        rows.append(matmul(sums_ref[...].astype(bf16), chosen)[0:1, :])
    rows = [first_ref[0:1, :] / gains_ref[0:1, :], second_ref[...]] + rows
    extra = jnp.zeros((128, 1024), f32)
    for at, some in enumerate(rows):
        extra = jnp.where(row == at, some, extra)
    for shard in range(8):
        span = slice(shard * 128, shard * 128 + 128)
        tiles = (turned_grad[:128, span].T, turned_grad[128:, span].T, extra[:, span].T)
        for j, tile in enumerate(tiles):
            for at in range(16):
                parts_ref[at // 4, at % 4, shard * 3 + j] = tile[at * 8 : at * 8 + 8]
    for y in range(4):
        for i in range(4):
            for z in range(4):
                for j in range(2):
                    low, left = y * 32 + i * 8, z * 256 + j * 128
                    parts_ref[y, z, 24 + i * 2 + j] = out_grad_ref[
                        low : low + 8, left : left + 128
                    ]


def attend_back(near, far, out_slot, kept, gain, tables, gains, second, where):
    outs = [((512, 1024), bf16), ((512, 1024), bf16), ((4, 4, 32, 8, 128), f32)]
    arrays = (near, far, out_slot, *kept, gain, *tables, gains, second)
    scratch = [
        pltpu.VMEM((8, 256), f32),
        pltpu.VMEM((8, 1024), f32),
        pltpu.VMEM((128, 1024), f32),
        pltpu.VMEM((1024, 256), bf16),
        pltpu.VMEM((1024, 1024), bf16),
        pltpu.VMEM((1024, 128), bf16),
        pltpu.VMEM((1024, 256), f32),
        pltpu.VMEM((128, 1024), bf16),
    ]
    return call(attend_back_kernel, spot([where[0]]), arrays, outs, scratch, 58, 4 * 1024**3)


def feed_kernel(
    spot_ref,
    half_ref,
    far_ref,
    upstream_ref,
    upstream_far_ref,
    came_ref,
    lower_ref,
    upper_ref,
    down_ref,
    other_ref,
    own_ref,
    hidden_ref,
    pre_grad_ref,
    normed_ref,
    turned_ref,
    weight_ref,
):
    z_low, core, x = spot_ref[0], spot_ref[1], spot_ref[2]
    for at in range(4):
        across = lower_ref if at < 2 else upper_ref
        for piece, parity in ((came_ref[at], z_low), (across[at % 2], 1 - z_low)):
            weight_ref[pl.ds(pl.multiple_of((at * 2 + parity) * 128, 128), 128), :] = piece
    normed_ref[:512] = half_ref[...]
    normed_ref[512:] = far_ref[...]

    def work(start, part, slot_core, from_ref):
        rows = pl.ds(pl.multiple_of(start, 256), 256)
        upstream = from_ref[pl.ds(pl.multiple_of(part * 256, 256), 256), :]
        slots = [
            pl.ds(pl.multiple_of((part * 4 + step * 2 + slot_core) * 128, 128), 128)
            for step in range(2)
        ]
        pre = matmul(normed_ref[rows, :], weight_ref[...])
        gate, up = pre[:, :576], pre[:, 576:]
        hidden_grad = matmul_nt(upstream, down_ref[...]).astype(bf16).astype(f32)
        sigmoid = 1.0 / (1.0 + jnp.exp(-gate))
        silu = gate * sigmoid
        hidden = (silu * up).astype(bf16)
        for step, slot in enumerate(slots):
            hidden_ref[slot, :] = hidden[step * 128 : step * 128 + 128]
            turned_ref[slot, :] = upstream[step * 128 : step * 128 + 128]
        gate_grad = hidden_grad * up * sigmoid * (1.0 + gate * (1.0 - sigmoid))
        pre_grad = jnp.concatenate([gate_grad, hidden_grad * silu], axis=1).astype(bf16)
        pre_grad_ref[rows, :] = pre_grad
        return matmul_nt(pre_grad, weight_ref[...])

    def keep(ref, part, partial):
        for step in range(2):
            to = pl.multiple_of(((part * 2 + step + 4 - x) % 4) * 128, 128)
            ref[pl.ds(to, 128), :] = partial[step * 128 : step * 128 + 128].astype(bf16)

    def other_half(part, carry):
        keep(other_ref, part, work(part * 256 + 512, part, 1 - core, upstream_far_ref))
        return carry

    def own_half(part, carry):
        keep(own_ref, part, work(part * 256, part, core, upstream_ref))
        return carry

    lax.fori_loop(0, 2, other_half, 0)
    lax.fori_loop(0, 2, own_half, 0)


def feed(half, far, upstream, upstream_far, weights, down_slot, where):
    arrays = (half, far, upstream, upstream_far, *weights, down_slot)
    outs = [
        ((512, 1024), bf16),
        ((512, 1024), bf16),
        ((1024, 576), bf16),
        ((1024, 1152), bf16),
        ((1024, 1024), bf16),
        ((1024, 1024), bf16),
    ]
    scratch = [pltpu.VMEM((1024, 1152), bf16)]
    scalars = spot([where[4], where[3], where[0]])
    return call(feed_kernel, scalars, arrays, outs, scratch, 58, 6 * 1024**3)


def feed_grads_kernel(spot_ref, mine_ref, other_ref, gate_ref, up_ref, down_ref):
    core, z_low = spot_ref[0], spot_ref[1]
    home = core == z_low
    for at in range(16):
        mine = mine_ref[at].astype(f32)
        other = other_ref[at].astype(f32)
        first = jnp.where(core == 0, mine[:288], other[:288])
        second = jnp.where(core == 0, other[:288], mine[:288])
        block = jnp.where(home, mine[288:], other[288:])
        rows = slice(at * 8, at * 8 + 8)
        for x in range(4):
            wide = [
                jnp.concatenate(
                    [one[(x * 9 + i) * 8 : (x * 9 + i) * 8 + 8] for i in range(9)], axis=1
                )
                for one in (first, second)
            ]
            columns = slice(x * 1152, x * 1152 + 1152)
            gate_ref[rows, columns] = jnp.concatenate([one[:, :576] for one in wide], axis=1)
            up_ref[rows, columns] = jnp.concatenate([one[:, 576:] for one in wide], axis=1)
        for i in range(18):
            for j in range(2):
                piece = block[(i * 2 + j) * 8 : (i * 2 + j) * 8 + 8]
                low, left = at // 4 * 144 + i * 8, at % 4 * 256 + j * 128
                down_ref[low : low + 8, left : left + 128] = piece


def feed_grads(mine, other, where):
    outs = [((128, 4608), f32), ((128, 4608), f32), ((576, 1024), f32)]
    return call(feed_grads_kernel, spot(where[3:]), (mine, other), outs, (), 40)


def attention_grads_kernel(spot_ref, mine_ref, other_ref, q_ref, k_ref, v_ref, out_ref, extra_ref):
    core, z_low, x, y, z = (spot_ref[i] for i in range(5))
    home = core == z_low
    for y_step in range(4):
        for z_step in range(4):
            mine = mine_ref[y_step, z_step].astype(f32)
            other = other_ref[y_step, z_step].astype(f32)
            first = jnp.where(core == 0, mine[:96], other[:96])
            second = jnp.where(core == 0, other[:96], mine[:96])
            block = jnp.where(home, mine[96:], other[96:])
            y_at, z_at = (y + y_step) % 4, (z + z_step) % 4
            rows = pl.ds(pl.multiple_of((y_at * 4 + z_at) * 8, 8), 8)
            extra = jnp.zeros((8, 128), f32)
            for step in range(4):
                slot, low = (x + step) % 4, step * 24
                to = pl.multiple_of(slot * 256, 128)
                q_ref[rows, pl.ds(to, 128)] = first[low : low + 8]
                q_ref[rows, pl.ds(to + 128, 128)] = second[low : low + 8]
                one, two = first[low + 8 : low + 16], second[low + 8 : low + 16]
                columns = pl.ds(pl.multiple_of(slot * 128, 128), 128)
                k_ref[rows, columns] = jnp.concatenate([one[:, :64], two[:, :64]], axis=1)
                v_ref[rows, columns] = jnp.concatenate([one[:, 64:], two[:, 64:]], axis=1)
                extra = extra + first[low + 16 : low + 24] + second[low + 16 : low + 24]
            extra_ref[rows, :] = extra
            for i in range(4):
                for j in range(2):
                    to = pl.ds(pl.multiple_of(y_at * 32 + i * 8, 8), 8)
                    columns = pl.ds(pl.multiple_of(z_at * 256 + j * 128, 128), 128)
                    out_ref[to, columns] = block[(i * 2 + j) * 8 : (i * 2 + j) * 8 + 8]


def attention_grads(mine, other, where):
    outs = [
        ((128, 1024), f32),
        ((128, 512), f32),
        ((128, 512), f32),
        ((128, 1024), f32),
        ((128, 128), f32),
    ]
    x, y, z, core, z_low = where
    return call(
        attention_grads_kernel, spot([core, z_low, x, y, z]), (mine, other), outs, (), 24
    )


def on_device(
    tokens,
    seq_lengths,
    token_places,
    attention_gain,
    query_weight,
    key_weight,
    value_weight,
    query_gain,
    key_gain,
    out_weight,
    feedforward_gain,
    gate_weight,
    up_weight,
    down_weight,
    cotangent,
):
    shard, replica = lax.axis_index("shard"), lax.axis_index("replica")
    x, z_low = shard // 2, shard % 2
    y, z, core = replica // 4, (replica // 2) % 2 * 2 + z_low, replica % 2
    where = (x, y, z, core, z_low)

    facts = cat([token_places, jnp.broadcast_to(seq_lengths[:, :1], (1, 128))], 1)
    small = cat([query_gain, key_gain, jnp.zeros((112,), bf16)])
    packed = pack(tokens[0], attention_gain[None], feedforward_gain[None], small[None])
    packed = send(packed, regroup)
    facts = jnp.where(core == z_low, facts, send(facts, other_core))
    packed_out, for_feed = pick_columns(
        query_weight, key_weight, value_weight, gate_weight, up_weight, packed, core
    )
    packed_out, for_feed, facts, out_mine, cotangent = join(
        packed_out, for_feed, facts, out_weight, cotangent
    )
    half = exchange(packed_out, x_rings)
    tables = place_tables(facts, core)
    upstream_own = send(cotangent[0], regroup)
    out_slot = jnp.where(core == z_low, out_mine, send(out_mine, z_up_home))
    half, for_feed, upstream_own, out_slot, tables = join(
        half, for_feed, upstream_own, out_slot, tables
    )

    upstream = lax.all_gather(upstream_own, AXES, axis=0, axis_index_groups=x_rings, tiled=True)
    far = send(half, other_core)
    across = send(half[:, :128, 1024:], z_up)
    feed_came = exchange(for_feed, x_rings)
    far, across = join(far, across)
    inputs = packed[:128].astype(f32)
    notes = jnp.stack([half[:, 128, 256:272], far[:, 128, 256:272]], axis=1)
    notes = jnp.where(core == 0, notes, notes[:, ::-1]).astype(f32)
    gain_query, gain_key = notes[..., :8].reshape(64), notes[..., 8:].reshape(64)
    gain = cat([gain_query, gain_query, gain_key, jnp.ones((64,), f32)])[None]

    attention_slice, first_normed, qkv, heads, scales, mixed, logs, gains = attend(
        half, far, across, gain, tables, where
    )
    gain_first, gain_second = gains[0], gains[8]
    other_half = matmul(mixed[512:], out_slot).astype(bf16)
    other_half, mixed, feed_came = join(other_half, mixed, feed_came)
    got = send(other_half, other_core)
    own_half = matmul(mixed[:512], out_slot)
    lower, upper = send(feed_came[:2], z_up), send(feed_came[2:], z_down)
    parts = scatter_sums(own_half, got)
    parts, lower, upper, down_mine = join(parts, lower, upper, down_weight)

    middle = inputs + add_up(parts)
    second_scale = rms_scale(middle)
    half = gather_half((middle * second_scale * gain_second).astype(bf16)).reshape(512, 1024)
    down_got = send(down_mine, z_down_home)
    half, upstream, down_got = join(half, upstream, down_got)
    down_slot = jnp.where(core == z_low, down_mine, down_got)
    far = send(half, other_core)
    upstream_far = send(upstream, other_core)
    other_half, own_half, hidden, pre_grad, normed_all, upstream = feed(
        half, far, upstream, upstream_far, (feed_came, lower, upper), down_slot, where
    )
    first, rest = scatter_parts(own_half, send(other_half, other_core))
    first, rest, pre_grad, hidden, normed_all = join(first, rest, pre_grad, hidden, normed_all)

    parts = send_x(*rest)
    feed_weight_grad = matmul_tn(normed_all, pre_grad)
    down_weight_grad = matmul_tn(hidden, upstream)
    feed_parts = rows_for_planes(feed_weight_grad).reshape(16, 72, 8, 128)
    down_parts = block_for_planes(down_weight_grad).reshape(16, 36, 8, 128)
    first, parts, feed_parts, down_parts, hidden = join(
        first, parts, feed_parts, down_parts, hidden
    )
    down_parts = exchange(down_parts, planes)
    second_grad = first + add_up(jnp.stack(parts))
    middle_norm_grad, second_gain_terms = norm_back(middle, second_scale, gain_second, second_grad)
    middle_grad = upstream_own.astype(f32) + middle_norm_grad
    second_gain_grad = jnp.sum(second_gain_terms, axis=0)
    near = gather_x(middle_grad.astype(bf16))
    result_rows = matmul(hidden, down_slot).astype(bf16)
    near, result_rows, down_parts, feed_parts = join(near, result_rows, down_parts, feed_parts)
    feed_parts = exchange(feed_parts, planes)
    near = cat(near)
    far = send(near, other_core)
    result_sum = lax.psum_scatter(
        result_rows, AXES, scatter_dimension=0, axis_index_groups=x_groups, tiled=True
    )
    other_half, own_half, attention_parts = attend_back(
        near,
        far,
        out_slot,
        (attention_slice, first_normed, qkv, heads, scales, mixed, logs),
        gain,
        tables,
        gains,
        second_gain_grad[None],
        where,
    )
    first, rest = scatter_parts(own_half, send(other_half, other_core))
    first, rest, attention_parts = join(first, rest, attention_parts)

    parts = send_x(*rest)
    pieces = [pick(attention_parts, (y + step) % 4, 0) for step in range(4)]
    ring = send_ring(pieces, y_up, y_down, y_far)
    feed_got = exchange_rows(add_up(feed_parts).astype(bf16).reshape(8, 9, 8, 128))
    down_rows = add_up(down_parts).astype(bf16)
    first, parts, ring, feed_got, down_rows = join(first, parts, ring, feed_got, down_rows)

    first_grad = first + add_up(jnp.stack(parts))
    input_norm_grad, _ = norm_back(inputs, rms_scale(inputs), gain_first, first_grad)
    input_grad = (middle_grad + input_norm_grad).astype(bf16)
    rows = pieces[0].astype(f32) + add_up(jnp.stack(ring))
    pieces = [pick(rows, (z + step) % 4, 0) for step in range(4)]
    ring = send_ring(pieces, z_up, z_down, z_far)
    feed_mine = return_planes(feed_got, down_rows)
    result = (middle + result_sum.astype(f32)).astype(bf16)
    ring, input_grad, result = join(ring, input_grad, result)

    rows = (pieces[0] + add_up(jnp.stack(ring))).astype(bf16)
    attention_got = exchange_x(rows[:24].reshape(8, 3, 8, 128), x)
    result = send(result, regroup)
    attention_got, result = join(attention_got, result)
    input_grad = send(input_grad, regroup)
    block, input_grad, feed_mine = join(
        gather_z(attention_got, rows[24:], z_low), input_grad, feed_mine
    )
    mine = gather_y(block)
    gate_sum, up_sum, down_sum = feed_grads(feed_mine, send(feed_mine, other_core), where)
    mine, gate_sum, up_sum, down_sum = join(mine, gate_sum, up_sum, down_sum)
    query_sum, key_sum, value_sum, out_sum, gain_sums = attention_grads(
        mine, send(mine, other_core), where
    )
    return (
        result[None],
        input_grad.astype(f32)[None],
        gain_sums[:, 0],
        query_sum,
        key_sum,
        value_sum,
        gain_sums[:8, 2],
        gain_sums[:8, 3],
        out_sum,
        gain_sums[:, 1],
        gate_sum,
        up_sum,
        down_sum,
    )


def solution(mesh):
    placed = (
        P("replica", "shard", None),
        P("replica", None),
        P("replica", None),
        P("shard"),
        P("shard", None),
        P("shard", None),
        P("shard", None),
        P("shard"),
        P("shard"),
        P("shard", None),
        P("shard"),
        P("shard", None),
        P("shard", None),
        P("shard", None),
        P("replica", "shard", None),
    )
    return jax.shard_map(
        on_device,
        mesh=mesh,
        in_specs=placed,
        out_specs=(
            P("replica", "shard", None),
            P("replica", "shard", None),
            P("shard"),
            P("shard", None),
            P("shard", None),
            P("shard", None),
            P("shard"),
            P("shard"),
            P("shard", None),
            P("shard"),
            P("shard", None),
            P("shard", None),
            P("shard", None),
        ),
        check_vma=False,
    )
```

```python
import jax
import jax.numpy as jnp
from jax import lax
from jax.experimental import pallas as pl
from jax.experimental.pallas import tpu as pltpu
from jax.sharding import PartitionSpec as P

HEADS = 16
KV_HEADS = 8
HD = 64
AXES = ("shard", "replica")

norm_eps = 1e-05
rope_base = 1000000.0
bf16 = jnp.bfloat16
f32 = jnp.float32


def place(x, y, z, core):
    return ((x % 4) * 2 + (z % 4) % 2) * 16 + ((y % 4) * 2 + (z % 4) // 2) * 2 + core % 2


def pairs(move, keep=lambda x, y, z, c: True):
    found = []
    for x in range(4):
        for y in range(4):
            for z in range(4):
                for c in range(2):
                    if keep(x, y, z, c):
                        found.append((place(x, y, z, c), place(*move(x, y, z, c))))
    return found


def home(x, y, z, c):
    return c == z % 2


x_up = pairs(lambda x, y, z, c: (x + 1, y, z, c))
x_down = pairs(lambda x, y, z, c: (x - 1, y, z, c))
x_far = pairs(lambda x, y, z, c: (x + 2, y, z, c))
y_up = pairs(lambda x, y, z, c: (x, y + 1, z, c))
y_down = pairs(lambda x, y, z, c: (x, y - 1, z, c))
y_far = pairs(lambda x, y, z, c: (x, y + 2, z, c))
z_up = pairs(lambda x, y, z, c: (x, y, z + 1, c))
z_down = pairs(lambda x, y, z, c: (x, y, z - 1, c))
z_far = pairs(lambda x, y, z, c: (x, y, z + 2, c))
z_up_home = pairs(lambda x, y, z, c: (x, y, z + 1, c), home)
z_down_home = pairs(lambda x, y, z, c: (x, y, z - 1, c), home)
other_core = pairs(lambda x, y, z, c: (x, y, z, 1 - c))
from_home = pairs(lambda x, y, z, c: (x, y, z, 1 - c), home)
regroup = pairs(lambda x, y, z, c: (x, y, (z // 2) * 2 + c, z % 2))


def send(values, moves):
    return lax.ppermute(values, AXES, moves)


def cat(pieces, axis=0):
    return jnp.concatenate(pieces, axis=axis)


def pick(values, index, axis):
    return lax.dynamic_index_in_dim(values, index, axis, keepdims=False)


def unroll(values, index, axis):
    doubled = cat([values, values], axis)
    return lax.dynamic_slice_in_dim(doubled, (4 - index) % 4, 4, axis)


x_rings = [
    [place(x, y, z, core) for x in range(4)] for core in range(2) for y in range(4) for z in range(4)
]
planes = [
    [place(x, y, z, core) for y in range(4) for z in range(4)] for x in range(4) for core in range(2)
]
x_groups = [
    [place(x, y, z, core) for x in range(4) for core in range(2)]
    for y in range(4)
    for z in range(4)
]


def join(*values):
    return lax.optimization_barrier(values)


def exchange(values, groups):
    return lax.all_to_all(values, AXES, 0, 0, axis_index_groups=groups)


def gather_half(block):
    return exchange(jnp.broadcast_to(block[None], (4, *block.shape)), x_rings)


def scatter_sums(own, got):
    summed = (own + got.astype(f32)).astype(bf16).reshape(4, 128, own.shape[1])
    return exchange(summed, x_rings)


def add_up(parts):
    return jnp.sum(parts.astype(f32), axis=0)


def units(values, rows, columns):
    height, width = values.shape
    return values.reshape(rows, height // rows // 8, 8, columns, width // columns // 128, 128)


def rows_for_planes(by_row):
    grid = by_row.astype(bf16).reshape(8, 4, 4, 8, by_row.shape[1] // 128, 128)
    return grid.transpose(1, 2, 0, 4, 3, 5)


def block_for_planes(by_block):
    return units(by_block.astype(bf16), 4, 4).transpose(0, 3, 1, 4, 2, 5)


def exchange_rows(by_row):
    return exchange(by_row.reshape(4, 2, *by_row.shape[1:]), x_rings)


def halve_block(by_block, core):
    halves = by_block.reshape(2, 18, 8, 128)
    mine, got = pick(halves, core, 0), send(pick(halves, 1 - core, 0), other_core)
    return [jnp.where(core == at, mine, got) for at in range(2)]


def return_planes(got, blocks):
    both = [
        cat([got[:, parity].reshape(-1, 128), blocks[parity].reshape(-1, 128)])
        for parity in range(2)
    ]
    both = jnp.stack(both)
    return exchange(
        jnp.broadcast_to(both[None], (8, *both.shape)).reshape(16, *both.shape[1:]), planes
    )


def exchange_x(by_row, x):
    own = by_row.reshape(4, 2, *by_row.shape[1:])
    near = [pick(own, (x + step) % 4, 0) for step in range(4)]
    return jnp.stack([near[0]] + send_x(*near[1:])[::-1])


def send_ring(pieces, up, down, far):
    low = [piece.astype(bf16) for piece in pieces[1:]]
    return [send(low[0], up), send(low[1], far), send(low[2], down)]


def gather_z(got, by_block, z_low):
    same = cat([pick(got, z_low, 1).reshape(-1, 128), by_block.reshape(-1, 128)])
    odd = cat([pick(got, 1 - z_low, 1).reshape(-1, 128), by_block.reshape(-1, 128)])
    return jnp.stack([same, send(odd, z_down), send(same, z_far), send(odd, z_up)])


def gather_y(block):
    return jnp.stack([block, send(block, y_down), send(block, y_far), send(block, y_up)])


def send_x(first, second, third):
    return [send(first, x_up), send(second, x_far), send(third, x_down)]


def gather_x(block):
    return [block, send(block, x_down), send(block, x_far), send(block, x_up)]


def quarter(values, step):
    return values[step * 128 : (step + 1) * 128]


def scatter_parts(own, got):
    sums = [quarter(own, step).astype(f32) + quarter(got, step).astype(f32) for step in range(4)]
    return sums[0], [part.astype(bf16) for part in sums[1:]]


def whole(shape):
    return pl.BlockSpec(shape, lambda i: (0,) * len(shape), pipeline_mode=pl.Buffered(1))


def spot(values):
    return jnp.stack(values).astype(jnp.int32)


def call(kernel, scalars, arrays, outs, scratch=(), limit=40, flops=0):
    size = sum(a.size * a.dtype.itemsize for a in arrays)
    return pl.pallas_call(
        kernel,
        out_shape=[jax.ShapeDtypeStruct(shape, kind) for shape, kind in outs],
        grid=(1,),
        in_specs=[pl.BlockSpec(memory_space=pltpu.SMEM)] + [whole(a.shape) for a in arrays],
        out_specs=[whole(shape) for shape, _ in outs],
        scratch_shapes=list(scratch),
        compiler_params=pltpu.CompilerParams(vmem_limit_bytes=limit * 2**20),
        cost_estimate=pl.CostEstimate(flops=flops, bytes_accessed=size, transcendentals=0),
    )(scalars, *arrays)


def rms_scale(values):
    return lax.rsqrt(jnp.mean(values * values, axis=-1, keepdims=True) + norm_eps)


def norm_back(inputs, scale_rows, gain_vector, upstream):
    normed = inputs * scale_rows
    scaled = upstream * gain_vector
    entry_grad = scale_rows * (scaled - normed * jnp.mean(scaled * normed, axis=-1, keepdims=True))
    return (entry_grad, upstream * normed)


def matmul(left_side, right_side):
    return jnp.dot(left_side, right_side, preferred_element_type=f32)


def matmul_tn(left_side, right_side):
    return lax.dot_general(
        left_side, right_side, (((0,), (0,)), ((), ())), preferred_element_type=f32
    )


def matmul_nt(left_side, right_side):
    return lax.dot_general(
        left_side, right_side, (((1,), (1,)), ((), ())), preferred_element_type=f32
    )


def columns_kernel(spot_ref, q_ref, k_ref, v_ref, gate_ref, up_ref, packed_ref, out_ref, feed_ref):
    core = spot_ref[0]
    for at in range(4):
        out_ref[at, :, :1024] = packed_ref[...]
        out_ref[at, 128:, 1024:] = jnp.zeros((16, 256), bf16)
        out_ref[at, :128, 1024:1152] = jnp.where(
            core == 0,
            q_ref[:, at * 256 : at * 256 + 128],
            q_ref[:, at * 256 + 128 : at * 256 + 256],
        )
        for ref, low in ((k_ref, 1152), (v_ref, 1216)):
            pair = ref[:, at * 128 : at * 128 + 128]
            out_ref[at, :128, low : low + 64] = jnp.where(core == 0, pair[:, :64], pair[:, 64:])
        for row, ref in enumerate((gate_ref, up_ref)):
            some = ref[:, at * 1152 : at * 1152 + 1152]
            feed_ref[at, :, row * 576 : row * 576 + 576] = jnp.where(
                core == 0, some[:, :576], some[:, 576:]
            )


def pick_columns(query_weight, key_weight, value_weight, gate_weight, up_weight, packed, core):
    outs = [((4, 144, 1280), bf16), ((4, 128, 1152), bf16)]
    arrays = (query_weight, key_weight, value_weight, gate_weight, up_weight, packed)
    return call(columns_kernel, spot([core]), arrays, outs, limit=58)


def pack_kernel(tokens_ref, first_ref, second_ref, small_ref, out_ref):
    out_ref[:128, :] = tokens_ref[...]
    out_ref[128:, :] = jnp.zeros((16, 1024), bf16)
    for step, ref in enumerate((first_ref, second_ref, small_ref)):
        row = jnp.broadcast_to(ref[...].astype(f32), (16, 128)).astype(bf16)
        out_ref[128:, step * 128 : step * 128 + 128] = row


def pack(*arrays):
    return pl.pallas_call(
        pack_kernel, out_shape=jax.ShapeDtypeStruct((144, 1024), bf16)
    )(*arrays)


def place_tables(facts, core):
    places = facts[0, :1024].reshape(4, 2, 128)
    places = jnp.stack([pick(places, core, 1), pick(places, 1 - core, 1)]).reshape(1, 1024)
    starts = jnp.where(places >= facts[:, 1024:1025], facts[:, 1024:1025], 0)
    lane = jnp.arange(128)
    frequency = rope_base ** (-2.0 * (lane % 32).astype(f32) / HD)
    angles = (places - starts).astype(f32).reshape(1024, 1) * frequency[None, :]
    cosine, sine = jnp.cos(angles), jnp.sin(angles) * jnp.where(lane % 64 < 32, -1.0, 1.0)
    places = places.astype(f32)
    return cosine, sine, places.reshape(1024, 1), places, starts.astype(f32)


def lanes(width):
    return lax.broadcasted_iota(jnp.int32, (1, width), 1)


def swap_halves(values):
    first = lanes(256) % 64 < 32
    return jnp.where(first, pltpu.roll(values, 224, 1), pltpu.roll(values, 32, 1))


def head_means(values):
    lane = lanes(256)
    found = jnp.zeros_like(values)
    for head in range(3):
        inside = (lane >= head * 64) & (lane < head * 64 + 64)
        mean = jnp.sum(jnp.where(inside, values, 0.0), axis=1, keepdims=True) * (1.0 / 64)
        found = jnp.where(inside, mean, found)
    return found


def twice(values):
    return jnp.concatenate([values, values], axis=1)


def attend_kernel(
    spot_ref,
    half_ref,
    far_ref,
    across_ref,
    gain_ref,
    cosine_ref,
    sine_ref,
    place_ref,
    place_row_ref,
    start_row_ref,
    weight_ref,
    normed_ref,
    qkv_ref,
    head_ref,
    scale_ref,
    mixed_ref,
    logs_ref,
    gains_ref,
    turned_ref,
):
    z_low, core = spot_ref[0], spot_ref[1]
    for at in range(4):
        for piece, parity in ((half_ref[at, :128, 1024:], z_low), (across_ref[at], 1 - z_low)):
            weight_ref[pl.ds(pl.multiple_of((at * 2 + parity) * 128, 128), 128), :] = piece
        for ref, slot in ((half_ref, at * 2 + core), (far_ref, at * 2 + 1 - core)):
            to = pl.ds(pl.multiple_of(slot * 128, 128), 128)
            gains_ref[:8, to] = ref[at, 128:, :128].astype(f32)[:8]
            gains_ref[8:, to] = ref[at, 128:, 128:256].astype(f32)[:8]
    gain = gain_ref[...]
    lane = lanes(256)
    for block in range(8):
        ref = half_ref if block < 4 else far_ref
        rows = slice(block * 128, block * 128 + 128)
        inputs = ref[block % 4, :128, :1024].astype(f32)
        scale = lax.rsqrt(jnp.mean(inputs * inputs, axis=1, keepdims=True) + norm_eps)
        normed = (inputs * scale * gains_ref[0:1, :]).astype(bf16)
        normed_ref[rows, :] = normed
        pre = matmul(normed, weight_ref[...])
        scales = lax.rsqrt(head_means(pre * pre) + norm_eps)
        heads = pre * scales
        head_ref[rows, :] = heads
        scale_ref[rows, :] = scales
        gained = heads * gain
        turned = gained * twice(cosine_ref[rows, :]) + swap_halves(gained) * twice(sine_ref[rows, :])
        qkv_ref[rows, :] = jnp.where(lane < 192, turned, pre).astype(bf16)
        turned_ref[:, rows] = jnp.where(lane < 192, turned, pre)[:, 128:].T.astype(bf16)

    keys = qkv_ref[:, 128:192]
    values = turned_ref[64:, :]
    place = place_ref[...]
    for part in range(4):
        rows = slice(part * 256, part * 256 + 256)
        allowed = (place <= place_row_ref[:, rows]) & (place >= start_row_ref[:, rows])
        for head in range(2):
            columns = slice(head * 64, head * 64 + 64)
            scores = matmul_nt(keys, qkv_ref[rows, columns]) * HD**-0.5
            scores = jnp.where(allowed, scores, -1e30)
            top = jnp.max(scores, axis=0, keepdims=True)
            exponent = jnp.exp(scores - top)
            total = jnp.sum(exponent, axis=0, keepdims=True)
            probs = (exponent * (1.0 / total)).astype(bf16)
            mixed_ref[rows, columns] = matmul(values, probs).T.astype(bf16)
            logs_ref[head : head + 1, rows] = top + jnp.log(total)


def attend(half, far, across, gain, tables, where):
    outs = [
        ((1024, 256), bf16),
        ((1024, 1024), bf16),
        ((1024, 256), bf16),
        ((1024, 256), f32),
        ((1024, 256), f32),
        ((1024, 128), bf16),
        ((8, 1024), f32),
        ((16, 1024), f32),
    ]
    arrays = (half, far, across, gain, *tables)
    scratch = [pltpu.VMEM((128, 1024), bf16)]
    scalars = spot([where[4], where[3]])
    return call(attend_kernel, scalars, arrays, outs, scratch, 58, 2 * 1024**3)


def attend_back_kernel(
    spot_ref,
    near_ref,
    far_ref,
    out_weight_ref,
    weight_ref,
    normed_ref,
    qkv_ref,
    head_ref,
    scale_ref,
    mixed_ref,
    logs_ref,
    gain_ref,
    cosine_ref,
    sine_ref,
    place_ref,
    place_row_ref,
    start_row_ref,
    gains_ref,
    second_ref,
    other_ref,
    own_ref,
    parts_ref,
    sums_ref,
    first_ref,
    out_grad_ref,
    pre_grad_ref,
    branch_ref,
    mixed_grad_ref,
    grad_ref,
    turned_ref,
):
    x = spot_ref[0]
    for step in range(4):
        to = pl.multiple_of(((x + step) % 4) * 128, 128)
        piece = slice(step * 128, step * 128 + 128)
        branch_ref[pl.ds(to, 128), :] = near_ref[piece, :]
        branch_ref[pl.ds(to + 512, 128), :] = far_ref[piece, :]
    mixed_grad_ref[...] = matmul_nt(branch_ref[...], out_weight_ref[...]).astype(bf16)
    keys, values = qkv_ref[:, 128:192], qkv_ref[:, 192:]
    turned_ref[...] = qkv_ref[:, 128:].astype(f32).T.astype(bf16)
    keys_turned = turned_ref[:64, :]
    place = place_ref[...]
    grad_ref[:, 128:] = jnp.zeros((1024, 128), f32)
    for part in range(4):
        rows = slice(part * 256, part * 256 + 256)
        allowed = (place <= place_row_ref[:, rows]) & (place >= start_row_ref[:, rows])
        for head in range(2):
            columns = slice(head * 64, head * 64 + 64)
            queries, upstream = qkv_ref[rows, columns], mixed_grad_ref[rows, columns]
            scores = matmul_nt(keys, queries) * HD**-0.5
            probs = jnp.where(allowed, jnp.exp(scores - logs_ref[head : head + 1, rows]), 0.0)
            prob_grad = matmul_nt(values, upstream)
            inner = jnp.sum(probs * prob_grad, axis=0, keepdims=True)
            score_grad = (probs * (prob_grad - inner)).astype(bf16)
            grad_ref[:, 128:192] += matmul(score_grad, queries) * HD**-0.5
            grad_ref[:, 192:] += matmul(probs.astype(bf16), upstream)
            grad_ref[rows, columns] = matmul(keys_turned, score_grad).T * HD**-0.5
    out_grad_ref[...] = matmul(mixed_ref[...].astype(f32).T.astype(bf16), branch_ref[...])
    gain = gain_ref[...]
    lane = lanes(256)
    sums_ref[...] = jnp.zeros((8, 256), f32)
    first_ref[...] = jnp.zeros((8, 1024), f32)
    for block in (4, 5, 6, 7, 0, 1, 2, 3):
        rows = slice(block * 128, block * 128 + 128)
        grads = grad_ref[rows, :]
        back = grads * twice(cosine_ref[rows, :]) - swap_halves(grads) * twice(sine_ref[rows, :])
        heads = head_ref[rows, :]
        sums_ref[0:1, :] += jnp.sum(back * heads, axis=0, keepdims=True)
        gained = back * gain
        entry = scale_ref[rows, :] * (gained - heads * head_means(gained * heads))
        pre_grad = jnp.where(lane < 192, entry, grads).astype(bf16)
        pre_grad_ref[rows, :] = pre_grad
        partial = matmul_nt(pre_grad, weight_ref[...])
        first_ref[0:1, :] += jnp.sum(partial * normed_ref[rows, :].astype(f32), axis=0, keepdims=True)
        to = pl.ds(pl.multiple_of(((block % 4 + 4 - x) % 4) * 128, 128), 128)
        if block < 4:
            own_ref[to, :] = partial.astype(bf16)
        else:
            other_ref[to, :] = partial.astype(bf16)

    turned_grad = matmul(pre_grad_ref[...].astype(f32).T.astype(bf16), normed_ref[...])
    column = lax.broadcasted_iota(jnp.int32, (256, 1024), 1)
    entry = lax.broadcasted_iota(jnp.int32, (256, 1024), 0)
    wanted = jnp.where(column % 128 < 8, column // 128 * 8 + column % 128, -1)
    row = lax.broadcasted_iota(jnp.int32, (128, 1024), 0)
    rows = []
    for inside in (entry < 128, (entry >= 128) & (entry < 192)):
        chosen = jnp.where(inside & (entry % 64 == wanted), 1.0, 0.0).astype(bf16)
        rows.append(matmul(sums_ref[...].astype(bf16), chosen)[0:1, :])
    rows = [first_ref[0:1, :] / gains_ref[0:1, :], second_ref[...]] + rows
    extra = jnp.zeros((128, 1024), f32)
    for at, some in enumerate(rows):
        extra = jnp.where(row == at, some, extra)
    for shard in range(8):
        span = slice(shard * 128, shard * 128 + 128)
        tiles = (turned_grad[:128, span].T, turned_grad[128:, span].T, extra[:, span].T)
        for j, tile in enumerate(tiles):
            for at in range(16):
                parts_ref[at // 4, at % 4, shard * 3 + j] = tile[at * 8 : at * 8 + 8]
    for y in range(4):
        for i in range(4):
            for z in range(4):
                for j in range(2):
                    low, left = y * 32 + i * 8, z * 256 + j * 128
                    parts_ref[y, z, 24 + i * 2 + j] = out_grad_ref[
                        low : low + 8, left : left + 128
                    ]


def attend_back(near, far, out_slot, kept, gain, tables, gains, second, where):
    outs = [((512, 1024), bf16), ((512, 1024), bf16), ((4, 4, 32, 8, 128), f32)]
    arrays = (near, far, out_slot, *kept, gain, *tables, gains, second)
    scratch = [
        pltpu.VMEM((8, 256), f32),
        pltpu.VMEM((8, 1024), f32),
        pltpu.VMEM((128, 1024), f32),
        pltpu.VMEM((1024, 256), bf16),
        pltpu.VMEM((1024, 1024), bf16),
        pltpu.VMEM((1024, 128), bf16),
        pltpu.VMEM((1024, 256), f32),
        pltpu.VMEM((128, 1024), bf16),
    ]
    return call(attend_back_kernel, spot([where[0]]), arrays, outs, scratch, 58, 4 * 1024**3)


def feed_kernel(
    spot_ref,
    half_ref,
    far_ref,
    upstream_ref,
    upstream_far_ref,
    came_ref,
    lower_ref,
    upper_ref,
    down_ref,
    other_ref,
    own_ref,
    hidden_ref,
    pre_grad_ref,
    normed_ref,
    turned_ref,
    weight_ref,
):
    z_low, core, x = spot_ref[0], spot_ref[1], spot_ref[2]
    for at in range(4):
        across = lower_ref if at < 2 else upper_ref
        for piece, parity in ((came_ref[at], z_low), (across[at % 2], 1 - z_low)):
            weight_ref[pl.ds(pl.multiple_of((at * 2 + parity) * 128, 128), 128), :] = piece
    normed_ref[:512] = half_ref[...]
    normed_ref[512:] = far_ref[...]

    def work(start, part, slot_core, from_ref):
        rows = pl.ds(pl.multiple_of(start, 256), 256)
        upstream = from_ref[pl.ds(pl.multiple_of(part * 256, 256), 256), :]
        slots = [
            pl.ds(pl.multiple_of((part * 4 + step * 2 + slot_core) * 128, 128), 128)
            for step in range(2)
        ]
        pre = matmul(normed_ref[rows, :], weight_ref[...])
        gate, up = pre[:, :576], pre[:, 576:]
        hidden_grad = matmul_nt(upstream, down_ref[...]).astype(bf16).astype(f32)
        sigmoid = 1.0 / (1.0 + jnp.exp(-gate))
        silu = gate * sigmoid
        hidden = (silu * up).astype(bf16)
        for step, slot in enumerate(slots):
            hidden_ref[slot, :] = hidden[step * 128 : step * 128 + 128]
            turned_ref[slot, :] = upstream[step * 128 : step * 128 + 128]
        gate_grad = hidden_grad * up * sigmoid * (1.0 + gate * (1.0 - sigmoid))
        pre_grad = jnp.concatenate([gate_grad, hidden_grad * silu], axis=1).astype(bf16)
        pre_grad_ref[rows, :] = pre_grad
        return matmul_nt(pre_grad, weight_ref[...])

    def keep(ref, part, partial):
        for step in range(2):
            to = pl.multiple_of(((part * 2 + step + 4 - x) % 4) * 128, 128)
            ref[pl.ds(to, 128), :] = partial[step * 128 : step * 128 + 128].astype(bf16)

    def other_half(part, carry):
        keep(other_ref, part, work(part * 256 + 512, part, 1 - core, upstream_far_ref))
        return carry

    def own_half(part, carry):
        keep(own_ref, part, work(part * 256, part, core, upstream_ref))
        return carry

    lax.fori_loop(0, 2, other_half, 0)
    lax.fori_loop(0, 2, own_half, 0)


def feed(half, far, upstream, upstream_far, weights, down_slot, where):
    arrays = (half, far, upstream, upstream_far, *weights, down_slot)
    outs = [
        ((512, 1024), bf16),
        ((512, 1024), bf16),
        ((1024, 576), bf16),
        ((1024, 1152), bf16),
        ((1024, 1024), bf16),
        ((1024, 1024), bf16),
    ]
    scratch = [pltpu.VMEM((1024, 1152), bf16)]
    scalars = spot([where[4], where[3], where[0]])
    return call(feed_kernel, scalars, arrays, outs, scratch, 58, 6 * 1024**3)


def feed_grads_kernel(spot_ref, mine_ref, other_ref, gate_ref, up_ref, down_ref):
    core = spot_ref[0]
    for at in range(16):
        mine = mine_ref[at].astype(f32)
        other = other_ref[at].astype(f32)
        first = jnp.where(core == 0, mine, other)
        second = jnp.where(core == 0, other, mine)
        block = jnp.concatenate([first[288:], second[288:]], axis=0)
        rows = slice(at * 8, at * 8 + 8)
        for x in range(4):
            wide = [
                jnp.concatenate(
                    [one[(x * 9 + i) * 8 : (x * 9 + i) * 8 + 8] for i in range(9)], axis=1
                )
                for one in (first, second)
            ]
            columns = slice(x * 1152, x * 1152 + 1152)
            gate_ref[rows, columns] = jnp.concatenate([one[:, :576] for one in wide], axis=1)
            up_ref[rows, columns] = jnp.concatenate([one[:, 576:] for one in wide], axis=1)
        for i in range(18):
            for j in range(2):
                piece = block[(i * 2 + j) * 8 : (i * 2 + j) * 8 + 8]
                low, left = at // 4 * 144 + i * 8, at % 4 * 256 + j * 128
                down_ref[low : low + 8, left : left + 128] = piece


def feed_grads(mine, other, where):
    outs = [((128, 4608), f32), ((128, 4608), f32), ((576, 1024), f32)]
    return call(feed_grads_kernel, spot(where[3:]), (mine, other), outs, (), 40)


def attention_grads_kernel(spot_ref, mine_ref, other_ref, q_ref, k_ref, v_ref, out_ref, extra_ref):
    core, z_low, x, y, z = (spot_ref[i] for i in range(5))
    home = core == z_low
    for y_step in range(4):
        for z_step in range(4):
            mine = mine_ref[y_step, z_step].astype(f32)
            other = other_ref[y_step, z_step].astype(f32)
            first = jnp.where(core == 0, mine[:96], other[:96])
            second = jnp.where(core == 0, other[:96], mine[:96])
            block = jnp.where(home, mine[96:], other[96:])
            y_at, z_at = (y + y_step) % 4, (z + z_step) % 4
            rows = pl.ds(pl.multiple_of((y_at * 4 + z_at) * 8, 8), 8)
            extra = jnp.zeros((8, 128), f32)
            for step in range(4):
                slot, low = (x + step) % 4, step * 24
                to = pl.multiple_of(slot * 256, 128)
                q_ref[rows, pl.ds(to, 128)] = first[low : low + 8]
                q_ref[rows, pl.ds(to + 128, 128)] = second[low : low + 8]
                one, two = first[low + 8 : low + 16], second[low + 8 : low + 16]
                columns = pl.ds(pl.multiple_of(slot * 128, 128), 128)
                k_ref[rows, columns] = jnp.concatenate([one[:, :64], two[:, :64]], axis=1)
                v_ref[rows, columns] = jnp.concatenate([one[:, 64:], two[:, 64:]], axis=1)
                extra = extra + first[low + 16 : low + 24] + second[low + 16 : low + 24]
            extra_ref[rows, :] = extra
            for i in range(4):
                for j in range(2):
                    to = pl.ds(pl.multiple_of(y_at * 32 + i * 8, 8), 8)
                    columns = pl.ds(pl.multiple_of(z_at * 256 + j * 128, 128), 128)
                    out_ref[to, columns] = block[(i * 2 + j) * 8 : (i * 2 + j) * 8 + 8]


def attention_grads(mine, other, where):
    outs = [
        ((128, 1024), f32),
        ((128, 512), f32),
        ((128, 512), f32),
        ((128, 1024), f32),
        ((128, 128), f32),
    ]
    x, y, z, core, z_low = where
    return call(
        attention_grads_kernel, spot([core, z_low, x, y, z]), (mine, other), outs, (), 24
    )


def on_device(
    tokens,
    seq_lengths,
    token_places,
    attention_gain,
    query_weight,
    key_weight,
    value_weight,
    query_gain,
    key_gain,
    out_weight,
    feedforward_gain,
    gate_weight,
    up_weight,
    down_weight,
    cotangent,
):
    shard, replica = lax.axis_index("shard"), lax.axis_index("replica")
    x, z_low = shard // 2, shard % 2
    y, z, core = replica // 4, (replica // 2) % 2 * 2 + z_low, replica % 2
    where = (x, y, z, core, z_low)

    facts = cat([token_places, jnp.broadcast_to(seq_lengths[:, :1], (1, 128))], 1)
    small = cat([query_gain, key_gain, jnp.zeros((112,), bf16)])
    packed = pack(tokens[0], attention_gain[None], feedforward_gain[None], small[None])
    packed = send(packed, regroup)
    facts = jnp.where(core == z_low, facts, send(facts, other_core))
    packed_out, for_feed = pick_columns(
        query_weight, key_weight, value_weight, gate_weight, up_weight, packed, core
    )
    packed_out, for_feed, facts, out_mine, cotangent = join(
        packed_out, for_feed, facts, out_weight, cotangent
    )
    half = exchange(packed_out, x_rings)
    tables = place_tables(facts, core)
    upstream_own = send(cotangent[0], regroup)
    out_slot = jnp.where(core == z_low, out_mine, send(out_mine, z_up_home))
    half, for_feed, upstream_own, out_slot, tables = join(
        half, for_feed, upstream_own, out_slot, tables
    )

    upstream = lax.all_gather(upstream_own, AXES, axis=0, axis_index_groups=x_rings, tiled=True)
    far = send(half, other_core)
    across = send(half[:, :128, 1024:], z_up)
    feed_came = exchange(for_feed, x_rings)
    far, across = join(far, across)
    inputs = packed[:128].astype(f32)
    notes = jnp.stack([half[:, 128, 256:272], far[:, 128, 256:272]], axis=1)
    notes = jnp.where(core == 0, notes, notes[:, ::-1]).astype(f32)
    gain_query, gain_key = notes[..., :8].reshape(64), notes[..., 8:].reshape(64)
    gain = cat([gain_query, gain_query, gain_key, jnp.ones((64,), f32)])[None]

    attention_slice, first_normed, qkv, heads, scales, mixed, logs, gains = attend(
        half, far, across, gain, tables, where
    )
    gain_first, gain_second = gains[0], gains[8]
    other_half = matmul(mixed[512:], out_slot).astype(bf16)
    other_half, mixed, feed_came = join(other_half, mixed, feed_came)
    got = send(other_half, other_core)
    own_half = matmul(mixed[:512], out_slot)
    lower, upper = send(feed_came[:2], z_up), send(feed_came[2:], z_down)
    parts = scatter_sums(own_half, got)
    parts, lower, upper, down_mine = join(parts, lower, upper, down_weight)

    middle = inputs + add_up(parts)
    second_scale = rms_scale(middle)
    half = gather_half((middle * second_scale * gain_second).astype(bf16)).reshape(512, 1024)
    down_got = send(down_mine, z_down_home)
    half, upstream, down_got = join(half, upstream, down_got)
    down_slot = jnp.where(core == z_low, down_mine, down_got)
    far = send(half, other_core)
    upstream_far = send(upstream, other_core)
    other_half, own_half, hidden, pre_grad, normed_all, upstream = feed(
        half, far, upstream, upstream_far, (feed_came, lower, upper), down_slot, where
    )
    first, rest = scatter_parts(own_half, send(other_half, other_core))
    first, rest, pre_grad, hidden, normed_all = join(first, rest, pre_grad, hidden, normed_all)

    parts = send_x(*rest)
    feed_weight_grad = matmul_tn(normed_all, pre_grad)
    down_weight_grad = matmul_tn(hidden, upstream)
    feed_parts = rows_for_planes(feed_weight_grad).reshape(16, 72, 8, 128)
    down_parts = block_for_planes(down_weight_grad).reshape(16, 36, 8, 128)
    first, parts, feed_parts, down_parts, hidden = join(
        first, parts, feed_parts, down_parts, hidden
    )
    down_parts = exchange(down_parts, planes)
    second_grad = first + add_up(jnp.stack(parts))
    middle_norm_grad, second_gain_terms = norm_back(middle, second_scale, gain_second, second_grad)
    middle_grad = upstream_own.astype(f32) + middle_norm_grad
    second_gain_grad = jnp.sum(second_gain_terms, axis=0)
    near = gather_x(middle_grad.astype(bf16))
    result_rows = matmul(hidden, down_slot).astype(bf16)
    near, result_rows, down_parts, feed_parts = join(near, result_rows, down_parts, feed_parts)
    feed_parts = exchange(feed_parts, planes)
    near = cat(near)
    far = send(near, other_core)
    result_sum = lax.psum_scatter(
        result_rows, AXES, scatter_dimension=0, axis_index_groups=x_groups, tiled=True
    )
    other_half, own_half, attention_parts = attend_back(
        near,
        far,
        out_slot,
        (attention_slice, first_normed, qkv, heads, scales, mixed, logs),
        gain,
        tables,
        gains,
        second_gain_grad[None],
        where,
    )
    first, rest = scatter_parts(own_half, send(other_half, other_core))
    first, rest, attention_parts = join(first, rest, attention_parts)

    parts = send_x(*rest)
    pieces = [pick(attention_parts, (y + step) % 4, 0) for step in range(4)]
    ring = send_ring(pieces, y_up, y_down, y_far)
    feed_got = exchange_rows(add_up(feed_parts).astype(bf16).reshape(8, 9, 8, 128))
    down_rows = halve_block(add_up(down_parts).astype(bf16), core)
    first, parts, ring, feed_got, down_rows = join(first, parts, ring, feed_got, down_rows)

    first_grad = first + add_up(jnp.stack(parts))
    input_norm_grad, _ = norm_back(inputs, rms_scale(inputs), gain_first, first_grad)
    input_grad = (middle_grad + input_norm_grad).astype(bf16)
    rows = pieces[0].astype(f32) + add_up(jnp.stack(ring))
    pieces = [pick(rows, (z + step) % 4, 0) for step in range(4)]
    ring = send_ring(pieces, z_up, z_down, z_far)
    feed_mine = return_planes(feed_got, down_rows)
    result = (middle + result_sum.astype(f32)).astype(bf16)
    ring, input_grad, result = join(ring, input_grad, result)

    rows = (pieces[0] + add_up(jnp.stack(ring))).astype(bf16)
    attention_got = exchange_x(rows[:24].reshape(8, 3, 8, 128), x)
    ends = send(jnp.stack([result, input_grad]), regroup)
    attention_got, ends = join(attention_got, ends)
    block, feed_mine = join(gather_z(attention_got, rows[24:], z_low), feed_mine)
    mine = gather_y(block)
    gate_sum, up_sum, down_sum = feed_grads(feed_mine, send(feed_mine, other_core), where)
    mine, gate_sum, up_sum, down_sum = join(mine, gate_sum, up_sum, down_sum)
    query_sum, key_sum, value_sum, out_sum, gain_sums = attention_grads(
        mine, send(mine, other_core), where
    )
    return (
        ends[:1],
        ends[1:].astype(f32),
        gain_sums[:, 0],
        query_sum,
        key_sum,
        value_sum,
        gain_sums[:8, 2],
        gain_sums[:8, 3],
        out_sum,
        gain_sums[:, 1],
        gate_sum,
        up_sum,
        down_sum,
    )


def solution(mesh):
    placed = (
        P("replica", "shard", None),
        P("replica", None),
        P("replica", None),
        P("shard"),
        P("shard", None),
        P("shard", None),
        P("shard", None),
        P("shard"),
        P("shard"),
        P("shard", None),
        P("shard"),
        P("shard", None),
        P("shard", None),
        P("shard", None),
        P("replica", "shard", None),
    )
    return jax.shard_map(
        on_device,
        mesh=mesh,
        in_specs=placed,
        out_specs=(
            P("replica", "shard", None),
            P("replica", "shard", None),
            P("shard"),
            P("shard", None),
            P("shard", None),
            P("shard", None),
            P("shard"),
            P("shard"),
            P("shard", None),
            P("shard"),
            P("shard", None),
            P("shard", None),
            P("shard", None),
        ),
        check_vma=False,
    )
```

```python
import jax
import jax.numpy as jnp
from jax import lax
from jax.experimental import pallas as pl
from jax.experimental.pallas import tpu as pltpu
from jax.sharding import PartitionSpec as P

HEADS = 16
KV_HEADS = 8
HD = 64
AXES = ("shard", "replica")

norm_eps = 1e-05
rope_base = 1000000.0
bf16 = jnp.bfloat16
f32 = jnp.float32


def place(x, y, z, core):
    return ((x % 4) * 2 + (z % 4) % 2) * 16 + ((y % 4) * 2 + (z % 4) // 2) * 2 + core % 2


def pairs(move, keep=lambda x, y, z, c: True):
    found = []
    for x in range(4):
        for y in range(4):
            for z in range(4):
                for c in range(2):
                    if keep(x, y, z, c):
                        found.append((place(x, y, z, c), place(*move(x, y, z, c))))
    return found


def home(x, y, z, c):
    return c == z % 2


x_up = pairs(lambda x, y, z, c: (x + 1, y, z, c))
x_down = pairs(lambda x, y, z, c: (x - 1, y, z, c))
x_far = pairs(lambda x, y, z, c: (x + 2, y, z, c))
y_up = pairs(lambda x, y, z, c: (x, y + 1, z, c))
y_down = pairs(lambda x, y, z, c: (x, y - 1, z, c))
y_far = pairs(lambda x, y, z, c: (x, y + 2, z, c))
z_up = pairs(lambda x, y, z, c: (x, y, z + 1, c))
z_down = pairs(lambda x, y, z, c: (x, y, z - 1, c))
z_far = pairs(lambda x, y, z, c: (x, y, z + 2, c))
z_up_home = pairs(lambda x, y, z, c: (x, y, z + 1, c), home)
z_down_home = pairs(lambda x, y, z, c: (x, y, z - 1, c), home)
other_core = pairs(lambda x, y, z, c: (x, y, z, 1 - c))
from_home = pairs(lambda x, y, z, c: (x, y, z, 1 - c), home)
regroup = pairs(lambda x, y, z, c: (x, y, (z // 2) * 2 + c, z % 2))


def send(values, moves):
    return lax.ppermute(values, AXES, moves)


def cat(pieces, axis=0):
    return jnp.concatenate(pieces, axis=axis)


def pick(values, index, axis):
    return lax.dynamic_index_in_dim(values, index, axis, keepdims=False)


def unroll(values, index, axis):
    doubled = cat([values, values], axis)
    return lax.dynamic_slice_in_dim(doubled, (4 - index) % 4, 4, axis)


x_rings = [
    [place(x, y, z, core) for x in range(4)] for core in range(2) for y in range(4) for z in range(4)
]
planes = [
    [place(x, y, z, core) for y in range(4) for z in range(4)] for x in range(4) for core in range(2)
]
x_groups = [
    [place(x, y, z, core) for x in range(4) for core in range(2)]
    for y in range(4)
    for z in range(4)
]


def join(*values):
    return lax.optimization_barrier(values)


def exchange(values, groups):
    return lax.all_to_all(values, AXES, 0, 0, axis_index_groups=groups)


def gather_half(block):
    return exchange(jnp.broadcast_to(block[None], (4, *block.shape)), x_rings)


def scatter_sums(own, got):
    summed = (own + got.astype(f32)).astype(bf16).reshape(4, 128, own.shape[1])
    return exchange(summed, x_rings)


def add_up(parts):
    return jnp.sum(parts.astype(f32), axis=0)


def units(values, rows, columns):
    height, width = values.shape
    return values.reshape(rows, height // rows // 8, 8, columns, width // columns // 128, 128)


def rows_for_planes(by_row):
    grid = by_row.astype(bf16).reshape(8, 4, 4, 8, by_row.shape[1] // 128, 128)
    return grid.transpose(1, 2, 0, 4, 3, 5)


def block_for_planes(by_block):
    return units(by_block.astype(bf16), 4, 4).transpose(0, 3, 1, 4, 2, 5)


def exchange_rows(by_row):
    return exchange(by_row.reshape(4, 2, *by_row.shape[1:]), x_rings)


def halve_block(by_block, core):
    halves = by_block.reshape(2, 18, 8, 128)
    mine, got = pick(halves, core, 0), send(pick(halves, 1 - core, 0), other_core)
    return [jnp.where(core == at, mine, got) for at in range(2)]


def return_planes(got, blocks):
    both = [
        cat([got[:, parity].reshape(-1, 128), blocks[parity].reshape(-1, 128)])
        for parity in range(2)
    ]
    both = jnp.stack(both)
    return exchange(
        jnp.broadcast_to(both[None], (8, *both.shape)).reshape(16, *both.shape[1:]), planes
    )


def exchange_x(by_row, x):
    own = by_row.reshape(4, 2, *by_row.shape[1:])
    near = [pick(own, (x + step) % 4, 0) for step in range(4)]
    return jnp.stack([near[0]] + send_x(*near[1:])[::-1])


def send_ring(pieces, up, down, far):
    low = [piece.astype(bf16) for piece in pieces[1:]]
    return [send(low[0], up), send(low[1], far), send(low[2], down)]


def gather_z(got, by_block, z_low):
    same = cat([pick(got, z_low, 1).reshape(-1, 128), by_block.reshape(-1, 128)])
    odd = cat([pick(got, 1 - z_low, 1).reshape(-1, 128), by_block.reshape(-1, 128)])
    return jnp.stack([same, send(odd, z_down), send(same, z_far), send(odd, z_up)])


def gather_y(block):
    return jnp.stack([block, send(block, y_down), send(block, y_far), send(block, y_up)])


def send_x(first, second, third):
    return [send(first, x_up), send(second, x_far), send(third, x_down)]


def gather_x(block):
    return [block, send(block, x_down), send(block, x_far), send(block, x_up)]


def quarter(values, step):
    return values[step * 128 : (step + 1) * 128]


def scatter_parts(own, got):
    sums = [quarter(own, step).astype(f32) + quarter(got, step).astype(f32) for step in range(4)]
    return sums[0], [part.astype(bf16) for part in sums[1:]]


def whole(shape):
    return pl.BlockSpec(shape, lambda i: (0,) * len(shape), pipeline_mode=pl.Buffered(1))


def spot(values):
    return jnp.stack(values).astype(jnp.int32)


def call(kernel, scalars, arrays, outs, scratch=(), limit=40, flops=0):
    size = sum(a.size * a.dtype.itemsize for a in arrays)
    return pl.pallas_call(
        kernel,
        out_shape=[jax.ShapeDtypeStruct(shape, kind) for shape, kind in outs],
        grid=(1,),
        in_specs=[pl.BlockSpec(memory_space=pltpu.SMEM)] + [whole(a.shape) for a in arrays],
        out_specs=[whole(shape) for shape, _ in outs],
        scratch_shapes=list(scratch),
        compiler_params=pltpu.CompilerParams(vmem_limit_bytes=limit * 2**20),
        cost_estimate=pl.CostEstimate(flops=flops, bytes_accessed=size, transcendentals=0),
    )(scalars, *arrays)


def rms_scale(values):
    return lax.rsqrt(jnp.mean(values * values, axis=-1, keepdims=True) + norm_eps)


def norm_back(inputs, scale_rows, gain_vector, upstream):
    normed = inputs * scale_rows
    scaled = upstream * gain_vector
    entry_grad = scale_rows * (scaled - normed * jnp.mean(scaled * normed, axis=-1, keepdims=True))
    return (entry_grad, upstream * normed)


def matmul(left_side, right_side):
    return jnp.dot(left_side, right_side, preferred_element_type=f32)


def matmul_tn(left_side, right_side):
    return lax.dot_general(
        left_side, right_side, (((0,), (0,)), ((), ())), preferred_element_type=f32
    )


def matmul_nt(left_side, right_side):
    return lax.dot_general(
        left_side, right_side, (((1,), (1,)), ((), ())), preferred_element_type=f32
    )


def columns_kernel(spot_ref, q_ref, k_ref, v_ref, gate_ref, up_ref, packed_ref, out_ref, feed_ref):
    core = spot_ref[0]
    for at in range(4):
        out_ref[at, :, :1024] = packed_ref[...]
        out_ref[at, 128:, 1024:] = jnp.zeros((16, 256), bf16)
        out_ref[at, :128, 1024:1152] = jnp.where(
            core == 0,
            q_ref[:, at * 256 : at * 256 + 128],
            q_ref[:, at * 256 + 128 : at * 256 + 256],
        )
        for ref, low in ((k_ref, 1152), (v_ref, 1216)):
            pair = ref[:, at * 128 : at * 128 + 128]
            out_ref[at, :128, low : low + 64] = jnp.where(core == 0, pair[:, :64], pair[:, 64:])
        for row, ref in enumerate((gate_ref, up_ref)):
            some = ref[:, at * 1152 : at * 1152 + 1152]
            feed_ref[at, :, row * 576 : row * 576 + 576] = jnp.where(
                core == 0, some[:, :576], some[:, 576:]
            )


def pick_columns(query_weight, key_weight, value_weight, gate_weight, up_weight, packed, core):
    outs = [((4, 144, 1280), bf16), ((4, 128, 1152), bf16)]
    arrays = (query_weight, key_weight, value_weight, gate_weight, up_weight, packed)
    return call(columns_kernel, spot([core]), arrays, outs, limit=58)


def pack_kernel(tokens_ref, first_ref, second_ref, query_ref, key_ref, out_ref):
    out_ref[:128, :] = tokens_ref[...]
    out_ref[128:, :] = jnp.zeros((16, 1024), bf16)
    low = 0
    for ref in (first_ref, second_ref, query_ref, key_ref):
        width = ref.shape[1]
        row = jnp.broadcast_to(ref[...].astype(f32), (16, width)).astype(bf16)
        out_ref[128:, low : low + width] = row
        low += width


def pack(*arrays):
    return pl.pallas_call(
        pack_kernel, out_shape=jax.ShapeDtypeStruct((144, 1024), bf16)
    )(*arrays)


def place_tables(facts, core):
    places = facts[0, :1024].reshape(4, 2, 128)
    places = jnp.stack([pick(places, core, 1), pick(places, 1 - core, 1)]).reshape(1, 1024)
    starts = jnp.where(places >= facts[:, 1024:1025], facts[:, 1024:1025], 0)
    lane = jnp.arange(128)
    frequency = rope_base ** (-2.0 * (lane % 32).astype(f32) / HD)
    angles = (places - starts).astype(f32).reshape(1024, 1) * frequency[None, :]
    cosine, sine = jnp.cos(angles), jnp.sin(angles) * jnp.where(lane % 64 < 32, -1.0, 1.0)
    places = places.astype(f32)
    return cosine, sine, places.reshape(1024, 1), places, starts.astype(f32)


def lanes(width):
    return lax.broadcasted_iota(jnp.int32, (1, width), 1)


def swap_halves(values):
    first = lanes(256) % 64 < 32
    return jnp.where(first, pltpu.roll(values, 224, 1), pltpu.roll(values, 32, 1))


def head_means(values):
    lane = lanes(256)
    found = jnp.zeros_like(values)
    for head in range(3):
        inside = (lane >= head * 64) & (lane < head * 64 + 64)
        mean = jnp.sum(jnp.where(inside, values, 0.0), axis=1, keepdims=True) * (1.0 / 64)
        found = jnp.where(inside, mean, found)
    return found


def twice(values):
    return jnp.concatenate([values, values], axis=1)


def attend_kernel(
    spot_ref,
    half_ref,
    far_ref,
    across_ref,
    gain_ref,
    cosine_ref,
    sine_ref,
    place_ref,
    place_row_ref,
    start_row_ref,
    weight_ref,
    normed_ref,
    qkv_ref,
    head_ref,
    scale_ref,
    mixed_ref,
    logs_ref,
    gains_ref,
    turned_ref,
):
    z_low, core = spot_ref[0], spot_ref[1]
    for at in range(4):
        for piece, parity in ((half_ref[at, :128, 1024:], z_low), (across_ref[at], 1 - z_low)):
            weight_ref[pl.ds(pl.multiple_of((at * 2 + parity) * 128, 128), 128), :] = piece
        for ref, slot in ((half_ref, at * 2 + core), (far_ref, at * 2 + 1 - core)):
            to = pl.ds(pl.multiple_of(slot * 128, 128), 128)
            gains_ref[:8, to] = ref[at, 128:, :128].astype(f32)[:8]
            gains_ref[8:, to] = ref[at, 128:, 128:256].astype(f32)[:8]
    gain = gain_ref[...]
    lane = lanes(256)
    for block in range(8):
        ref = half_ref if block < 4 else far_ref
        rows = slice(block * 128, block * 128 + 128)
        inputs = ref[block % 4, :128, :1024].astype(f32)
        scale = lax.rsqrt(jnp.mean(inputs * inputs, axis=1, keepdims=True) + norm_eps)
        normed = (inputs * scale * gains_ref[0:1, :]).astype(bf16)
        normed_ref[rows, :] = normed
        pre = matmul(normed, weight_ref[...])
        scales = lax.rsqrt(head_means(pre * pre) + norm_eps)
        heads = pre * scales
        head_ref[rows, :] = heads
        scale_ref[rows, :] = scales
        gained = heads * gain
        turned = gained * twice(cosine_ref[rows, :]) + swap_halves(gained) * twice(sine_ref[rows, :])
        qkv_ref[rows, :] = jnp.where(lane < 192, turned, pre).astype(bf16)
        turned_ref[:, rows] = jnp.where(lane < 192, turned, pre)[:, 128:].T.astype(bf16)

    keys = qkv_ref[:, 128:192]
    values = turned_ref[64:, :]
    place = place_ref[...]
    for part in range(4):
        rows = slice(part * 256, part * 256 + 256)
        allowed = (place <= place_row_ref[:, rows]) & (place >= start_row_ref[:, rows])
        for head in range(2):
            columns = slice(head * 64, head * 64 + 64)
            scores = matmul_nt(keys, qkv_ref[rows, columns]) * HD**-0.5
            scores = jnp.where(allowed, scores, -1e30)
            top = jnp.max(scores, axis=0, keepdims=True)
            exponent = jnp.exp(scores - top)
            total = jnp.sum(exponent, axis=0, keepdims=True)
            probs = (exponent * (1.0 / total)).astype(bf16)
            mixed_ref[rows, columns] = matmul(values, probs).T.astype(bf16)
            logs_ref[head : head + 1, rows] = top + jnp.log(total)


def attend(half, far, across, gain, tables, where):
    outs = [
        ((1024, 256), bf16),
        ((1024, 1024), bf16),
        ((1024, 256), bf16),
        ((1024, 256), f32),
        ((1024, 256), f32),
        ((1024, 128), bf16),
        ((8, 1024), f32),
        ((16, 1024), f32),
    ]
    arrays = (half, far, across, gain, *tables)
    scratch = [pltpu.VMEM((128, 1024), bf16)]
    scalars = spot([where[4], where[3]])
    return call(attend_kernel, scalars, arrays, outs, scratch, 58, 2 * 1024**3)


def attend_back_kernel(
    spot_ref,
    near_ref,
    far_ref,
    out_weight_ref,
    weight_ref,
    normed_ref,
    qkv_ref,
    head_ref,
    scale_ref,
    mixed_ref,
    logs_ref,
    gain_ref,
    cosine_ref,
    sine_ref,
    place_ref,
    place_row_ref,
    start_row_ref,
    gains_ref,
    second_ref,
    other_ref,
    own_ref,
    parts_ref,
    sums_ref,
    first_ref,
    out_grad_ref,
    pre_grad_ref,
    branch_ref,
    mixed_grad_ref,
    grad_ref,
    turned_ref,
):
    x = spot_ref[0]
    for step in range(4):
        to = pl.multiple_of(((x + step) % 4) * 128, 128)
        piece = slice(step * 128, step * 128 + 128)
        branch_ref[pl.ds(to, 128), :] = near_ref[piece, :]
        branch_ref[pl.ds(to + 512, 128), :] = far_ref[piece, :]
    mixed_grad_ref[...] = matmul_nt(branch_ref[...], out_weight_ref[...]).astype(bf16)
    keys, values = qkv_ref[:, 128:192], qkv_ref[:, 192:]
    turned_ref[...] = qkv_ref[:, 128:].astype(f32).T.astype(bf16)
    keys_turned = turned_ref[:64, :]
    place = place_ref[...]
    grad_ref[:, 128:] = jnp.zeros((1024, 128), f32)
    for part in range(4):
        rows = slice(part * 256, part * 256 + 256)
        allowed = (place <= place_row_ref[:, rows]) & (place >= start_row_ref[:, rows])
        for head in range(2):
            columns = slice(head * 64, head * 64 + 64)
            queries, upstream = qkv_ref[rows, columns], mixed_grad_ref[rows, columns]
            scores = matmul_nt(keys, queries) * HD**-0.5
            probs = jnp.where(allowed, jnp.exp(scores - logs_ref[head : head + 1, rows]), 0.0)
            prob_grad = matmul_nt(values, upstream)
            inner = jnp.sum(probs * prob_grad, axis=0, keepdims=True)
            score_grad = (probs * (prob_grad - inner)).astype(bf16)
            grad_ref[:, 128:192] += matmul(score_grad, queries) * HD**-0.5
            grad_ref[:, 192:] += matmul(probs.astype(bf16), upstream)
            grad_ref[rows, columns] = matmul(keys_turned, score_grad).T * HD**-0.5
    out_grad_ref[...] = matmul(mixed_ref[...].astype(f32).T.astype(bf16), branch_ref[...])
    gain = gain_ref[...]
    lane = lanes(256)
    sums_ref[...] = jnp.zeros((8, 256), f32)
    first_ref[...] = jnp.zeros((8, 1024), f32)
    for block in (4, 5, 6, 7, 0, 1, 2, 3):
        rows = slice(block * 128, block * 128 + 128)
        grads = grad_ref[rows, :]
        back = grads * twice(cosine_ref[rows, :]) - swap_halves(grads) * twice(sine_ref[rows, :])
        heads = head_ref[rows, :]
        sums_ref[0:1, :] += jnp.sum(back * heads, axis=0, keepdims=True)
        gained = back * gain
        entry = scale_ref[rows, :] * (gained - heads * head_means(gained * heads))
        pre_grad = jnp.where(lane < 192, entry, grads).astype(bf16)
        pre_grad_ref[rows, :] = pre_grad
        partial = matmul_nt(pre_grad, weight_ref[...])
        first_ref[0:1, :] += jnp.sum(partial * normed_ref[rows, :].astype(f32), axis=0, keepdims=True)
        to = pl.ds(pl.multiple_of(((block % 4 + 4 - x) % 4) * 128, 128), 128)
        if block < 4:
            own_ref[to, :] = partial.astype(bf16)
        else:
            other_ref[to, :] = partial.astype(bf16)

    turned_grad = matmul(pre_grad_ref[...].astype(f32).T.astype(bf16), normed_ref[...])
    column = lax.broadcasted_iota(jnp.int32, (256, 1024), 1)
    entry = lax.broadcasted_iota(jnp.int32, (256, 1024), 0)
    wanted = jnp.where(column % 128 < 8, column // 128 * 8 + column % 128, -1)
    row = lax.broadcasted_iota(jnp.int32, (128, 1024), 0)
    rows = []
    for inside in (entry < 128, (entry >= 128) & (entry < 192)):
        chosen = jnp.where(inside & (entry % 64 == wanted), 1.0, 0.0).astype(bf16)
        rows.append(matmul(sums_ref[...].astype(bf16), chosen)[0:1, :])
    rows = [first_ref[0:1, :] / gains_ref[0:1, :], second_ref[...]] + rows
    extra = jnp.zeros((128, 1024), f32)
    for at, some in enumerate(rows):
        extra = jnp.where(row == at, some, extra)
    for shard in range(8):
        span = slice(shard * 128, shard * 128 + 128)
        tiles = (turned_grad[:128, span].T, turned_grad[128:, span].T, extra[:, span].T)
        for j, tile in enumerate(tiles):
            for at in range(16):
                parts_ref[at // 4, at % 4, shard * 3 + j] = tile[at * 8 : at * 8 + 8]
    for y in range(4):
        for i in range(4):
            for z in range(4):
                for j in range(2):
                    low, left = y * 32 + i * 8, z * 256 + j * 128
                    parts_ref[y, z, 24 + i * 2 + j] = out_grad_ref[
                        low : low + 8, left : left + 128
                    ]


def attend_back(near, far, out_slot, kept, gain, tables, gains, second, where):
    outs = [((512, 1024), bf16), ((512, 1024), bf16), ((4, 4, 32, 8, 128), f32)]
    arrays = (near, far, out_slot, *kept, gain, *tables, gains, second)
    scratch = [
        pltpu.VMEM((8, 256), f32),
        pltpu.VMEM((8, 1024), f32),
        pltpu.VMEM((128, 1024), f32),
        pltpu.VMEM((1024, 256), bf16),
        pltpu.VMEM((1024, 1024), bf16),
        pltpu.VMEM((1024, 128), bf16),
        pltpu.VMEM((1024, 256), f32),
        pltpu.VMEM((128, 1024), bf16),
    ]
    return call(attend_back_kernel, spot([where[0]]), arrays, outs, scratch, 58, 4 * 1024**3)


def feed_kernel(
    spot_ref,
    half_ref,
    far_ref,
    upstream_ref,
    upstream_far_ref,
    came_ref,
    lower_ref,
    upper_ref,
    down_ref,
    other_ref,
    own_ref,
    hidden_ref,
    pre_grad_ref,
    normed_ref,
    turned_ref,
    weight_ref,
):
    z_low, core, x = spot_ref[0], spot_ref[1], spot_ref[2]
    for at in range(4):
        across = lower_ref if at < 2 else upper_ref
        for piece, parity in ((came_ref[at], z_low), (across[at % 2], 1 - z_low)):
            weight_ref[pl.ds(pl.multiple_of((at * 2 + parity) * 128, 128), 128), :] = piece
    normed_ref[:512] = half_ref[...]
    normed_ref[512:] = far_ref[...]

    def work(start, part, slot_core, from_ref):
        rows = pl.ds(pl.multiple_of(start, 256), 256)
        upstream = from_ref[pl.ds(pl.multiple_of(part * 256, 256), 256), :]
        slots = [
            pl.ds(pl.multiple_of((part * 4 + step * 2 + slot_core) * 128, 128), 128)
            for step in range(2)
        ]
        pre = matmul(normed_ref[rows, :], weight_ref[...])
        gate, up = pre[:, :576], pre[:, 576:]
        hidden_grad = matmul_nt(upstream, down_ref[...]).astype(bf16).astype(f32)
        sigmoid = 1.0 / (1.0 + jnp.exp(-gate))
        silu = gate * sigmoid
        hidden = (silu * up).astype(bf16)
        for step, slot in enumerate(slots):
            hidden_ref[slot, :] = hidden[step * 128 : step * 128 + 128]
            turned_ref[slot, :] = upstream[step * 128 : step * 128 + 128]
        gate_grad = hidden_grad * up * sigmoid * (1.0 + gate * (1.0 - sigmoid))
        pre_grad = jnp.concatenate([gate_grad, hidden_grad * silu], axis=1).astype(bf16)
        pre_grad_ref[rows, :] = pre_grad
        return matmul_nt(pre_grad, weight_ref[...])

    def keep(ref, part, partial):
        for step in range(2):
            to = pl.multiple_of(((part * 2 + step + 4 - x) % 4) * 128, 128)
            ref[pl.ds(to, 128), :] = partial[step * 128 : step * 128 + 128].astype(bf16)

    def other_half(part, carry):
        keep(other_ref, part, work(part * 256 + 512, part, 1 - core, upstream_far_ref))
        return carry

    def own_half(part, carry):
        keep(own_ref, part, work(part * 256, part, core, upstream_ref))
        return carry

    lax.fori_loop(0, 2, other_half, 0)
    lax.fori_loop(0, 2, own_half, 0)


def feed(half, far, upstream, upstream_far, weights, down_slot, where):
    arrays = (half, far, upstream, upstream_far, *weights, down_slot)
    outs = [
        ((512, 1024), bf16),
        ((512, 1024), bf16),
        ((1024, 576), bf16),
        ((1024, 1152), bf16),
        ((1024, 1024), bf16),
        ((1024, 1024), bf16),
    ]
    scratch = [pltpu.VMEM((1024, 1152), bf16)]
    scalars = spot([where[4], where[3], where[0]])
    return call(feed_kernel, scalars, arrays, outs, scratch, 58, 6 * 1024**3)


def feed_grads_kernel(spot_ref, mine_ref, other_ref, gate_ref, up_ref, down_ref):
    core = spot_ref[0]
    for at in range(16):
        mine = mine_ref[at].astype(f32)
        other = other_ref[at].astype(f32)
        first = jnp.where(core == 0, mine, other)
        second = jnp.where(core == 0, other, mine)
        block = jnp.concatenate([first[288:], second[288:]], axis=0)
        rows = slice(at * 8, at * 8 + 8)
        for x in range(4):
            wide = [
                jnp.concatenate(
                    [one[(x * 9 + i) * 8 : (x * 9 + i) * 8 + 8] for i in range(9)], axis=1
                )
                for one in (first, second)
            ]
            columns = slice(x * 1152, x * 1152 + 1152)
            gate_ref[rows, columns] = jnp.concatenate([one[:, :576] for one in wide], axis=1)
            up_ref[rows, columns] = jnp.concatenate([one[:, 576:] for one in wide], axis=1)
        for i in range(18):
            for j in range(2):
                piece = block[(i * 2 + j) * 8 : (i * 2 + j) * 8 + 8]
                low, left = at // 4 * 144 + i * 8, at % 4 * 256 + j * 128
                down_ref[low : low + 8, left : left + 128] = piece


def feed_grads(mine, other, where):
    outs = [((128, 4608), f32), ((128, 4608), f32), ((576, 1024), f32)]
    return call(feed_grads_kernel, spot(where[3:]), (mine, other), outs, (), 40, 5 * 1024**3)


def attention_grads_kernel(spot_ref, mine_ref, other_ref, q_ref, k_ref, v_ref, out_ref, extra_ref):
    core, z_low, x, y, z = (spot_ref[i] for i in range(5))
    home = core == z_low
    for y_step in range(4):
        for z_step in range(4):
            mine = mine_ref[y_step, z_step].astype(f32)
            other = other_ref[y_step, z_step].astype(f32)
            first = jnp.where(core == 0, mine[:96], other[:96])
            second = jnp.where(core == 0, other[:96], mine[:96])
            block = jnp.where(home, mine[96:], other[96:])
            y_at, z_at = (y + y_step) % 4, (z + z_step) % 4
            rows = pl.ds(pl.multiple_of((y_at * 4 + z_at) * 8, 8), 8)
            extra = jnp.zeros((8, 128), f32)
            for step in range(4):
                slot, low = (x + step) % 4, step * 24
                to = pl.multiple_of(slot * 256, 128)
                q_ref[rows, pl.ds(to, 128)] = first[low : low + 8]
                q_ref[rows, pl.ds(to + 128, 128)] = second[low : low + 8]
                one, two = first[low + 8 : low + 16], second[low + 8 : low + 16]
                columns = pl.ds(pl.multiple_of(slot * 128, 128), 128)
                k_ref[rows, columns] = jnp.concatenate([one[:, :64], two[:, :64]], axis=1)
                v_ref[rows, columns] = jnp.concatenate([one[:, 64:], two[:, 64:]], axis=1)
                extra = extra + first[low + 16 : low + 24] + second[low + 16 : low + 24]
            extra_ref[rows, :] = extra
            for i in range(4):
                for j in range(2):
                    to = pl.ds(pl.multiple_of(y_at * 32 + i * 8, 8), 8)
                    columns = pl.ds(pl.multiple_of(z_at * 256 + j * 128, 128), 128)
                    out_ref[to, columns] = block[(i * 2 + j) * 8 : (i * 2 + j) * 8 + 8]


def attention_grads(mine, other, where):
    outs = [
        ((128, 1024), f32),
        ((128, 512), f32),
        ((128, 512), f32),
        ((128, 1024), f32),
        ((128, 128), f32),
    ]
    x, y, z, core, z_low = where
    return call(
        attention_grads_kernel, spot([core, z_low, x, y, z]), (mine, other), outs, (), 24
    )


def on_device(
    tokens,
    seq_lengths,
    token_places,
    attention_gain,
    query_weight,
    key_weight,
    value_weight,
    query_gain,
    key_gain,
    out_weight,
    feedforward_gain,
    gate_weight,
    up_weight,
    down_weight,
    cotangent,
):
    shard, replica = lax.axis_index("shard"), lax.axis_index("replica")
    x, z_low = shard // 2, shard % 2
    y, z, core = replica // 4, (replica // 2) % 2 * 2 + z_low, replica % 2
    where = (x, y, z, core, z_low)

    packed = pack(
        tokens[0], attention_gain[None], feedforward_gain[None], query_gain[None], key_gain[None]
    )
    packed, token_places = join(packed, token_places)
    packed = send(packed, regroup)
    facts = cat([token_places, jnp.broadcast_to(seq_lengths[:, :1], (1, 128))], 1)
    facts = jnp.where(core == z_low, facts, send(facts, other_core))
    packed_out, for_feed = pick_columns(
        query_weight, key_weight, value_weight, gate_weight, up_weight, packed, core
    )
    packed_out, for_feed, facts, out_mine, cotangent = join(
        packed_out, for_feed, facts, out_weight, cotangent
    )
    half = exchange(packed_out, x_rings)
    tables = place_tables(facts, core)
    upstream_own = send(cotangent[0], regroup)
    out_slot = jnp.where(core == z_low, out_mine, send(out_mine, z_up_home))
    half, for_feed, upstream_own, out_slot, tables = join(
        half, for_feed, upstream_own, out_slot, tables
    )

    upstream = lax.all_gather(upstream_own, AXES, axis=0, axis_index_groups=x_rings, tiled=True)
    far = send(half, other_core)
    across = send(half[:, :128, 1024:], z_up)
    feed_came = exchange(for_feed, x_rings)
    far, across = join(far, across)
    inputs = packed[:128].astype(f32)
    notes = jnp.stack([half[:, 128, 256:272], far[:, 128, 256:272]], axis=1)
    notes = jnp.where(core == 0, notes, notes[:, ::-1]).astype(f32)
    gain_query, gain_key = notes[..., :8].reshape(64), notes[..., 8:].reshape(64)
    gain = cat([gain_query, gain_query, gain_key, jnp.ones((64,), f32)])[None]

    attention_slice, first_normed, qkv, heads, scales, mixed, logs, gains = attend(
        half, far, across, gain, tables, where
    )
    gain_first, gain_second = gains[0], gains[8]
    other_half = matmul(mixed[512:], out_slot).astype(bf16)
    other_half, mixed, feed_came = join(other_half, mixed, feed_came)
    got = send(other_half, other_core)
    own_half = matmul(mixed[:512], out_slot)
    lower, upper = send(feed_came[:2], z_up), send(feed_came[2:], z_down)
    parts = scatter_sums(own_half, got)
    parts, lower, upper, down_mine = join(parts, lower, upper, down_weight)

    middle = inputs + add_up(parts)
    second_scale = rms_scale(middle)
    half = gather_half((middle * second_scale * gain_second).astype(bf16)).reshape(512, 1024)
    down_got = send(down_mine, z_down_home)
    half, upstream, down_got = join(half, upstream, down_got)
    down_slot = jnp.where(core == z_low, down_mine, down_got)
    far = send(half, other_core)
    upstream_far = send(upstream, other_core)
    other_half, own_half, hidden, pre_grad, normed_all, upstream = feed(
        half, far, upstream, upstream_far, (feed_came, lower, upper), down_slot, where
    )
    first, rest = scatter_parts(own_half, send(other_half, other_core))
    first, rest, pre_grad, hidden, normed_all = join(first, rest, pre_grad, hidden, normed_all)

    parts = send_x(*rest)
    feed_weight_grad = matmul_tn(normed_all, pre_grad)
    down_weight_grad = matmul_tn(hidden, upstream)
    feed_parts = rows_for_planes(feed_weight_grad).reshape(16, 72, 8, 128)
    down_parts = block_for_planes(down_weight_grad).reshape(16, 36, 8, 128)
    first, parts, feed_parts, down_parts, hidden = join(
        first, parts, feed_parts, down_parts, hidden
    )
    down_parts = exchange(down_parts, planes)
    second_grad = first + add_up(jnp.stack(parts))
    middle_norm_grad, second_gain_terms = norm_back(middle, second_scale, gain_second, second_grad)
    middle_grad = upstream_own.astype(f32) + middle_norm_grad
    second_gain_grad = jnp.sum(second_gain_terms, axis=0)
    near = cat(gather_x(middle_grad.astype(bf16)))
    far = send(near, other_core)
    result_rows = matmul(hidden, down_slot).astype(bf16)
    near, far, result_rows, down_parts, feed_parts = join(
        near, far, result_rows, down_parts, feed_parts
    )
    feed_parts = exchange(feed_parts, planes)
    result_sum = lax.psum_scatter(
        result_rows, AXES, scatter_dimension=0, axis_index_groups=x_groups, tiled=True
    )
    other_half, own_half, attention_parts = attend_back(
        near,
        far,
        out_slot,
        (attention_slice, first_normed, qkv, heads, scales, mixed, logs),
        gain,
        tables,
        gains,
        second_gain_grad[None],
        where,
    )
    first, rest = scatter_parts(own_half, send(other_half, other_core))
    first, rest, attention_parts = join(first, rest, attention_parts)

    parts = send_x(*rest)
    pieces = [pick(attention_parts, (y + step) % 4, 0) for step in range(4)]
    ring = send_ring(pieces, y_up, y_down, y_far)
    feed_got = exchange_rows(add_up(feed_parts).astype(bf16).reshape(8, 9, 8, 128))
    down_rows = halve_block(add_up(down_parts).astype(bf16), core)
    first, parts, ring, feed_got, down_rows = join(first, parts, ring, feed_got, down_rows)

    first_grad = first + add_up(jnp.stack(parts))
    input_norm_grad, _ = norm_back(inputs, rms_scale(inputs), gain_first, first_grad)
    input_grad = (middle_grad + input_norm_grad).astype(bf16)
    rows = pieces[0].astype(f32) + add_up(jnp.stack(ring))
    pieces = [pick(rows, (z + step) % 4, 0) for step in range(4)]
    ring = send_ring(pieces, z_up, z_down, z_far)
    feed_mine = return_planes(feed_got, down_rows)
    result = (middle + result_sum.astype(f32)).astype(bf16)
    ring, input_grad, result = join(ring, input_grad, result)

    rows = (pieces[0] + add_up(jnp.stack(ring))).astype(bf16)
    attention_got = exchange_x(rows[:24].reshape(8, 3, 8, 128), x)
    ends = send(jnp.stack([result, input_grad]), regroup)
    attention_got, ends = join(attention_got, ends)
    block, feed_mine = join(gather_z(attention_got, rows[24:], z_low), feed_mine)
    mine = gather_y(block)
    gate_sum, up_sum, down_sum = feed_grads(feed_mine, send(feed_mine, other_core), where)
    mine, gate_sum, up_sum, down_sum = join(mine, gate_sum, up_sum, down_sum)
    query_sum, key_sum, value_sum, out_sum, gain_sums = attention_grads(
        mine, send(mine, other_core), where
    )
    return (
        ends[:1],
        ends[1:].astype(f32),
        gain_sums[:, 0],
        query_sum,
        key_sum,
        value_sum,
        gain_sums[:8, 2],
        gain_sums[:8, 3],
        out_sum,
        gain_sums[:, 1],
        gate_sum,
        up_sum,
        down_sum,
    )


def solution(mesh):
    placed = (
        P("replica", "shard", None),
        P("replica", None),
        P("replica", None),
        P("shard"),
        P("shard", None),
        P("shard", None),
        P("shard", None),
        P("shard"),
        P("shard"),
        P("shard", None),
        P("shard"),
        P("shard", None),
        P("shard", None),
        P("shard", None),
        P("replica", "shard", None),
    )
    return jax.shard_map(
        on_device,
        mesh=mesh,
        in_specs=placed,
        out_specs=(
            P("replica", "shard", None),
            P("replica", "shard", None),
            P("shard"),
            P("shard", None),
            P("shard", None),
            P("shard", None),
            P("shard"),
            P("shard"),
            P("shard", None),
            P("shard"),
            P("shard", None),
            P("shard", None),
            P("shard", None),
        ),
        check_vma=False,
    )
```
